32 devices in a mesh: groups: 2 (over y), tm: 4 (over z), head: 2 (over x), mp: 2 (over core).
Axes of the slice: x: 2, y: 2, z: 4, core: 2. Of those that a mesh axis runs over, the one named last changes fastest.
Arguments:
- queries: bfloat16 [2048, 2048], P(('groups', 'tm'), ('head', 'mp')), parts along dimension 0, may hold values from -6 to 6
- key_rows: bfloat16 [2048, 2048], P(('groups', 'tm'), ('head', 'mp')), parts along dimension 0, may hold values from -6 to 6
- value_rows: bfloat16 [2048, 2048], P(('groups', 'tm'), ('head', 'mp')), parts along dimension 0, may hold values from -12 to 12
- cotangent: bfloat16 [2048, 2048], P(('groups', 'tm'), ('head', 'mp')), parts along dimension 0, may hold values from -12 to 12
- block_active: int32 [16], P('groups'), parts along dimension 0, may hold values from 0 to 1
- send_counts: int32 [8, 2], P('groups'), parts along dimension 0, may hold values from 0 to 1, as said below
- block_mask: int32 [16, 8], P('groups'), parts along dimension 0, may hold values from 0 to 1, as said below
Outputs:
- attended: bfloat16 [4096, 2048], P(('groups', 'tm'), ('head', 'mp')), parts along dimension 0
- query_grad: bfloat16 [4096, 2048], P(('groups', 'tm'), ('head', 'mp')), parts along dimension 0
- key_grad: bfloat16 [2048, 2048], P(('groups', 'tm'), ('head', 'mp')), parts along dimension 0
- value_grad: bfloat16 [2048, 2048], P(('groups', 'tm'), ('head', 'mp')), parts along dimension 0
The draws below stay inside these ranges and needn't reach their ends.
There are 2 independent parts, one for each index of `groups`. The reference program is written for one: setup_inputs(seed, part) draws one part's arguments, and reference() takes and returns one part's arrays. A program takes and returns all parts, laid end to end along the dimension named above; each array names one. Nothing has to cross between parts.
Inputs may be any that keep to these rules, and one draw needn't show every extreme that they name: `send_counts`: column 0 of row i counts the first blocks of shard i that go to shard i-1, column 1 its last blocks that go to shard i+1 (shard 0 follows shard 4-1); the two sum to at most 2; every block that is handed on is active. `block_mask`: the diagonal is 1.
All inputs are finite; a program needn't handle non-finite values.
Results may differ from the reference program's by a relative error of at most 0.02.
Values may be sent and summed in bfloat16 or wider, within the bound.
A program may use at most 64 MiB of HBM per device.

```python
import math
import jax
import jax.numpy as jnp
from jax import lax

HEADS = 16
HD = 128
BLK = 128
NB = 2
CAP = 1
TB = 8
KEYS = 1024
SLOTS = 2048
WIDTH = 2048
N_TM = 4


def activity(base_key):
    mixed_key = jax.random.fold_in(base_key, 17)
    run_key, left_key, right_key = jax.random.split(mixed_key, 3)
    shards = TB // NB
    couples = jax.random.randint(run_key, ((TB + 1) // 2,), 0, 20)
    active = jnp.repeat((couples < 7).astype(jnp.int32), 2)[:TB]
    forced = (jnp.arange(TB, dtype=jnp.int32) < 2 * NB).astype(jnp.int32)
    active = jnp.maximum(active, forced)
    layout = active.reshape(shards, NB)
    leading = jnp.sum(jnp.cumprod(layout, axis=1), axis=1)
    trailing = jnp.sum(jnp.cumprod(layout[:, ::-1], axis=1), axis=1)
    to_left = jnp.minimum(jax.random.randint(left_key, (shards,), 0, CAP + 1), leading)
    to_right = jnp.minimum(jnp.minimum(jax.random.randint(right_key, (shards,), 0, CAP + 1), trailing), NB - to_left)
    shard_ids = jnp.arange(shards, dtype=jnp.int32)
    to_left = jnp.where(shard_ids == 0, CAP, jnp.where(shard_ids == 1, 0, to_left))
    to_right = jnp.where(shard_ids == 0, jnp.minimum(to_right, NB - CAP), jnp.where(shard_ids == 1, CAP, to_right))
    return (active.astype(jnp.int32), jnp.stack([to_left, to_right], axis=1).astype(jnp.int32))


def draw_block_active(key, part):
    return activity(key)[0]


def draw_send_counts(key, part):
    return activity(key)[1]


def draw_block_mask(key, part):
    picked = jax.random.randint(jax.random.fold_in(key, 29), (TB, TB), 0, 4) == 0
    diagonal = jnp.arange(TB, dtype=jnp.int32)[:, None] == jnp.arange(TB, dtype=jnp.int32)[None, :]
    return (picked | diagonal).astype(jnp.int32)


def query_key_pair(key):
    base_key = jax.random.fold_in(key, 23)
    query_key, keys_key = jax.random.split(base_key, 2)
    shape = (KEYS, HEADS * HD)
    query_part = jnp.clip(jax.random.normal(query_key, shape, jnp.float32), -6.0, 6.0)
    key_part = jnp.clip(jax.random.normal(keys_key, shape, jnp.float32), -6.0, 6.0)
    return (query_part, key_part)


def draw_queries(key, part):
    return query_key_pair(key)[0].astype(jnp.bfloat16)


def draw_key_rows(key, part):
    return query_key_pair(key)[1].astype(jnp.bfloat16)


def level_of(own_key, shape, cuts, least, high):
    loudness = 1.0
    for position, shards_of in cuts:
        steps = jax.random.uniform(jax.random.fold_in(jax.random.fold_in(own_key, 6), position), (shards_of,), jnp.float32, least / len(cuts), high / len(cuts))
        loudness = loudness * jnp.repeat(jnp.exp(steps), shape[position] // shards_of).reshape((-1,) + (1,) * (len(shape) - 1 - position))
    return loudness


def noise(rng, shape, deviation, reach, cuts=(), kind=jnp.bfloat16):
    array = deviation * jax.random.normal(rng, shape, jnp.float32)
    if cuts:
        array = array * level_of(rng, shape, cuts, -0.22, 0.18)
    return jnp.clip(array, -reach, reach).astype(kind)


def setup_inputs(seed: int = 0, part: int = 0) -> dict:
    arg_keys = jax.random.split(jax.random.key(seed), 8)
    part_keys = jax.random.split(jax.random.fold_in(arg_keys[7], part), 8)
    queries = draw_queries(jax.random.fold_in(jax.random.fold_in(arg_keys[7], part), 71), part)
    key_rows = draw_key_rows(jax.random.fold_in(jax.random.fold_in(arg_keys[7], part), 71), part)
    value_rows = noise(part_keys[2], (KEYS, WIDTH), 2.0, 12.0, ((0, 4), (1, 4)))
    cotangent = noise(part_keys[3], (KEYS, WIDTH), 2.0, 12.0, ((0, 4), (1, 4)))
    block_active = draw_block_active(jax.random.fold_in(jax.random.fold_in(arg_keys[7], part), 71), part)
    send_counts = draw_send_counts(jax.random.fold_in(jax.random.fold_in(arg_keys[7], part), 71), part)
    block_mask = draw_block_mask(jax.random.fold_in(jax.random.fold_in(arg_keys[7], part), 71), part)
    return {"queries": queries, "key_rows": key_rows, "value_rows": value_rows, "cotangent": cotangent, "block_active": block_active, "send_counts": send_counts, "block_mask": block_mask}


very_low = -1e+30

def pick(table, positions, extent):
    matches = positions[:, None] == jnp.arange(extent, dtype=jnp.int32)[None, :]
    return lax.optimization_barrier(jnp.sum(jnp.where(matches, table[None, :], 0), axis=1)).astype(jnp.int32)

def slot_layout(block_active, send_counts, block_mask, shards, own_blocks, capacity):
    slot_count = own_blocks + 2 * capacity
    all_blocks = shards * own_blocks
    places = jnp.arange(shards * slot_count, dtype=jnp.int32)
    device = places // slot_count
    slot_index = places % slot_count
    before = (device + shards - 1) % shards
    following = (device + 1) % shards
    to_left = send_counts[:, 0]
    to_right = send_counts[:, 1]
    from_before = slot_index < capacity
    from_after = slot_index >= capacity + own_blocks
    owner_shard = jnp.where(from_before, before, jnp.where(from_after, following, device))
    local_block = jnp.where(from_before, own_blocks - capacity + slot_index, jnp.where(from_after, slot_index - capacity - own_blocks, slot_index - capacity))
    middle_ok = (local_block >= pick(to_left, device, shards)) & (local_block < own_blocks - pick(to_right, device, shards))
    holds_record = jnp.where(from_before, slot_index >= capacity - pick(to_right, before, shards), jnp.where(from_after, local_block < pick(to_left, following, shards), middle_ok))
    anchor = (owner_shard * own_blocks + local_block).astype(jnp.int32)
    onehot = (anchor[:, None] == jnp.arange(all_blocks, dtype=jnp.int32)[None, :]).astype(jnp.float32)
    seeing = (block_mask * block_active[None, :]).astype(jnp.float32)
    block_rows = jnp.dot(onehot, seeing, precision=lax.Precision.HIGHEST)
    active = jnp.dot(onehot, block_active.astype(jnp.float32), precision=lax.Precision.HIGHEST)
    present = jnp.where(holds_record, active, 0.0).astype(jnp.float32)
    return (anchor, block_rows * present[:, None], present)

def reference(queries, key_rows, value_rows, cotangent, block_active, send_counts, block_mask):
    model_width = HEADS * HD
    scaling = 1.0 / math.sqrt(HD)
    anchor, table, present = slot_layout(block_active, send_counts, block_mask, N_TM, NB, CAP)
    slot_queries = queries.reshape(TB, BLK, model_width)[anchor].reshape(SLOTS, model_width)
    slot_cotan = cotangent.reshape(TB, BLK, model_width)[anchor].reshape(SLOTS, model_width)
    key_hot = ((jnp.arange(KEYS, dtype=jnp.int32) // BLK)[:, None] == jnp.arange(TB, dtype=jnp.int32)[None, :]).astype(jnp.float32)
    token_table = jnp.repeat(table, BLK, axis=0)
    allowed = jnp.dot(token_table, key_hot.T, precision=lax.Precision.HIGHEST) > 0.5
    live = jnp.repeat(present, BLK) > 0.5

    def one_head(head_index):
        offset = head_index * HD
        query_head = lax.dynamic_slice_in_dim(slot_queries, offset, HD, 1)
        cotan_head = lax.dynamic_slice_in_dim(slot_cotan, offset, HD, 1)
        key_head = lax.dynamic_slice_in_dim(key_rows, offset, HD, 1)
        value_head = lax.dynamic_slice_in_dim(value_rows, offset, HD, 1)
        scores = jnp.dot(query_head, key_head.T, preferred_element_type=jnp.float32) * scaling
        peak = lax.optimization_barrier(jnp.max(jnp.where(allowed, scores, very_low), axis=1))
        expo = jnp.where(allowed, jnp.exp(jnp.where(allowed, scores - peak[:, None], 0.0)), 0.0)
        denominator = jnp.where(live, lax.optimization_barrier(jnp.sum(expo, axis=1)), 1.0)
        attended = (jnp.dot(expo.astype(jnp.bfloat16), value_head, preferred_element_type=jnp.float32) / denominator[:, None]).astype(jnp.bfloat16)
        log_norm = peak + jnp.log(denominator)
        deltas = lax.optimization_barrier(jnp.sum(cotan_head.astype(jnp.float32) * attended.astype(jnp.float32), axis=1))
        probs = jnp.where(allowed, jnp.exp(jnp.where(allowed, scores - log_norm[:, None], 0.0)), 0.0)
        weight_grad = jnp.dot(cotan_head, value_head.T, preferred_element_type=jnp.float32)
        score_grad = (probs * (weight_grad - deltas[:, None])).astype(jnp.bfloat16)
        query_grad = (jnp.dot(score_grad, key_head, preferred_element_type=jnp.float32) * scaling).astype(jnp.bfloat16)
        key_grad = (jnp.dot(score_grad.T, query_head, preferred_element_type=jnp.float32) * scaling).astype(jnp.bfloat16)
        value_grad = jnp.dot(probs.astype(jnp.bfloat16).T, cotan_head, preferred_element_type=jnp.float32).astype(jnp.bfloat16)
        return (attended, query_grad, key_grad, value_grad)
    results = lax.map(one_head, jnp.arange(HEADS, dtype=jnp.int32))

    def merge_heads(stacked):
        return jnp.transpose(stacked, (1, 0, 2)).reshape(stacked.shape[1], model_width)
    return (merge_heads(results[0]), merge_heads(results[1]), merge_heads(results[2]), merge_heads(results[3]))
```

```python
import functools
import math

import jax
import jax.numpy as jnp
from jax import lax
from jax.experimental import pallas as pl
from jax.experimental.pallas import tpu as pltpu
from jax.sharding import PartitionSpec as P

HD = 128
BLK = 128
CAP = 1


very_low = -1e30


def extended_2(shard, sides, width):
    for axis, dim in sides:
        peers, length = (lax.axis_size(axis), shard.shape[dim])
        up = [(i, (i + 1) % peers) for i in range(peers)]
        down = [(j, i) for i, j in up]
        last = lax.slice_in_dim(shard, length - width, length, axis=dim)
        first = lax.slice_in_dim(shard, 0, width, axis=dim)
        before = lax.ppermute(last, axis, up)
        after = lax.ppermute(first, axis, down)
        shard = jnp.concatenate([before, shard, after], axis=dim)
    return shard


def pick(table, positions, extent):
    matches = positions[:, None] == jnp.arange(extent, dtype=jnp.int32)[None, :]
    return jnp.sum(jnp.where(matches, table[None, :], 0), axis=1)


def slot_layout(block_active, send_counts, block_mask, shards, own_blocks, capacity):
    slot_count = own_blocks + 2 * capacity
    all_blocks = shards * own_blocks
    places = jnp.arange(shards * slot_count, dtype=jnp.int32)
    device = places // slot_count
    slot_index = places % slot_count
    before = (device + shards - 1) % shards
    following = (device + 1) % shards
    to_left = send_counts[:, 0]
    to_right = send_counts[:, 1]
    from_before = slot_index < capacity
    from_after = slot_index >= capacity + own_blocks
    owner_shard = jnp.where(from_before, before, jnp.where(from_after, following, device))
    local_block = jnp.where(
        from_before,
        own_blocks - capacity + slot_index,
        jnp.where(from_after, slot_index - capacity - own_blocks, slot_index - capacity),
    )
    middle_ok = (local_block >= pick(to_left, device, shards)) & (
        local_block < own_blocks - pick(to_right, device, shards)
    )
    holds_record = jnp.where(
        from_before,
        slot_index >= capacity - pick(to_right, before, shards),
        jnp.where(from_after, local_block < pick(to_left, following, shards), middle_ok),
    )
    anchor = owner_shard * own_blocks + local_block
    onehot = (anchor[:, None] == jnp.arange(all_blocks, dtype=jnp.int32)[None, :]).astype(
        jnp.float32
    )
    seeing = (block_mask * block_active[None, :]).astype(jnp.float32)
    block_rows = jnp.dot(onehot, seeing, precision=lax.Precision.HIGHEST)
    active = jnp.dot(onehot, block_active.astype(jnp.float32), precision=lax.Precision.HIGHEST)
    present = jnp.where(holds_record, active, 0.0)
    return (anchor, block_rows * present[:, None], present)


def block_hot(offset, length, extent):
    blocks = (offset + jnp.arange(length, dtype=jnp.int32)) // BLK
    return (blocks[:, None] == jnp.arange(extent, dtype=jnp.int32)[None, :]).astype(jnp.bfloat16)


def sweep(update, running, pieces, offset):
    row_count = pieces[0].shape[0]
    step_rows = math.gcd(row_count, 1024)
    if step_rows == row_count:
        return update(running, pieces, offset)

    def one_turn(turn_index, carried):
        part_pieces = tuple(
            (
                lax.dynamic_slice_in_dim(member, turn_index * step_rows, step_rows, 0)
                for member in pieces
            )
        )
        return update(carried, part_pieces, offset + turn_index * step_rows)

    return lax.fori_loop(0, row_count // step_rows, one_turn, running)


def body(queries, key_rows, value_rows, cotangent, block_active, send_counts, block_mask):
    shards = lax.axis_size("tm")
    shard_index = lax.axis_index("tm")
    model_width = queries.shape[1]
    head_count = model_width // HD
    own_rows = queries.shape[0]
    own_blocks = own_rows // BLK
    all_blocks = block_active.shape[0]
    slot_count = own_blocks + 2 * CAP
    slot_rows = slot_count * BLK
    scaling = 1.0 / math.sqrt(HD)
    anchor, table, present = slot_layout(
        block_active, send_counts, block_mask, shards, own_blocks, CAP
    )
    records = jnp.concatenate([queries, cotangent], axis=1)
    extended = extended_2(records, (("tm", 0),), CAP * BLK)
    query_slots = extended[:, :model_width].reshape(slot_rows, head_count, HD)
    cotan_slots = extended[:, model_width:].reshape(slot_rows, head_count, HD)
    my_table = lax.dynamic_slice_in_dim(table, shard_index * slot_count, slot_count, 0)
    query_table = jnp.repeat(my_table, BLK, axis=0).astype(jnp.bfloat16)
    live = (
        jnp.repeat(lax.dynamic_slice_in_dim(present, shard_index * slot_count, slot_count, 0), BLK)
        > 0.5
    )
    keys_all, values_all = (
        lax.all_gather(key_rows, "tm", axis=0, tiled=True),
        lax.all_gather(value_rows, "tm", axis=0, tiled=True),
    )

    def own_scores(key_piece, offset):
        allowed = (
            lax.dot_general(
                query_table,
                block_hot(offset, key_piece.shape[0], all_blocks),
                (((1,), (1,)), ((), ())),
                preferred_element_type=jnp.float32,
            )[:, None, :]
            > 0.5
        )
        scores = (
            jnp.einsum("qhd,khd->qhk", query_slots, key_piece, preferred_element_type=jnp.float32)
            * scaling
        )
        return (allowed, scores)

    def forward(running, pieces, offset):
        peak, masses, accum = running
        key_piece = pieces[0].reshape(-1, head_count, HD)
        value_piece = pieces[1].reshape(-1, head_count, HD)
        allowed, scores = own_scores(key_piece, offset)
        new_peak = jnp.maximum(peak, jnp.max(jnp.where(allowed, scores, very_low), axis=2))
        weights = jnp.where(
            allowed, jnp.exp(jnp.where(allowed, scores - new_peak[:, :, None], 0.0)), 0.0
        )
        shrink = jnp.exp(peak - new_peak)
        masses = masses * shrink + jnp.sum(weights, axis=2)
        accum = accum * shrink[:, :, None] + jnp.einsum(
            "qhk,khd->qhd",
            weights.astype(jnp.bfloat16),
            value_piece,
            preferred_element_type=jnp.float32,
        )
        return (new_peak, masses, accum)

    initial = (
        jnp.full((slot_rows, head_count), very_low, jnp.float32),
        jnp.zeros((slot_rows, head_count), jnp.float32),
        jnp.zeros((slot_rows, head_count, HD), jnp.float32),
    )
    peak, masses, accum = sweep(forward, initial, (keys_all, values_all), 0)
    denominator = jnp.where(live[:, None], masses, 1.0)
    attended = (accum / denominator[:, :, None]).astype(jnp.bfloat16)
    log_norm = peak + jnp.log(denominator)
    deltas = jnp.sum(cotan_slots.astype(jnp.float32) * attended.astype(jnp.float32), axis=2)

    def own_gradients(key_piece, value_piece, offset):
        allowed, scores = own_scores(key_piece, offset)
        probs = jnp.where(
            allowed, jnp.exp(jnp.where(allowed, scores - log_norm[:, :, None], 0.0)), 0.0
        )
        weight_grad = jnp.einsum(
            "qhd,khd->qhk", cotan_slots, value_piece, preferred_element_type=jnp.float32
        )
        return (probs, (probs * (weight_grad - deltas[:, :, None])).astype(jnp.bfloat16))

    zero_query = jnp.zeros((slot_rows, head_count, HD), jnp.float32)

    def query_pass(query_sum, pieces, offset):
        key_piece = pieces[0].reshape(-1, head_count, HD)
        value_piece = pieces[1].reshape(-1, head_count, HD)
        probs, score_grad = own_gradients(key_piece, value_piece, offset)
        return query_sum + jnp.einsum(
            "qhk,khd->qhd", score_grad, key_piece, preferred_element_type=jnp.float32
        )

    query_sum = sweep(query_pass, zero_query, (keys_all, values_all), 0)
    own_keys = key_rows.reshape(own_rows, head_count, HD)
    own_values = value_rows.reshape(own_rows, head_count, HD)
    own_hot = block_hot(shard_index * own_rows, own_rows, all_blocks)
    slot_table = table.astype(jnp.bfloat16)
    logsum_all, delta_all = (
        lax.all_gather(log_norm, "tm", axis=0, tiled=True),
        lax.all_gather(deltas, "tm", axis=0, tiled=True),
    )

    def owner_work(running, pieces, offset):
        key_sum, value_sum = running
        query_piece, cotan_piece = pieces
        row_count = query_piece.shape[0]
        logsum_piece = lax.dynamic_slice_in_dim(logsum_all, offset, row_count, 0)
        delta_piece = lax.dynamic_slice_in_dim(delta_all, offset, row_count, 0)
        piece_table = jnp.dot(
            block_hot(offset, row_count, shards * slot_count),
            slot_table,
            preferred_element_type=jnp.float32,
        ).astype(jnp.bfloat16)
        allowed = (
            lax.dot_general(
                piece_table, own_hot, (((1,), (1,)), ((), ())), preferred_element_type=jnp.float32
            )[:, None, :]
            > 0.5
        )
        query_three = query_piece.reshape(row_count, head_count, HD)
        cotan_three = cotan_piece.reshape(row_count, head_count, HD)
        scores = (
            jnp.einsum("qhd,khd->qhk", query_three, own_keys, preferred_element_type=jnp.float32)
            * scaling
        )
        probs = jnp.where(
            allowed, jnp.exp(jnp.where(allowed, scores - logsum_piece[:, :, None], 0.0)), 0.0
        )
        weight_grad = jnp.einsum(
            "qhd,khd->qhk", cotan_three, own_values, preferred_element_type=jnp.float32
        )
        score_grad = (probs * (weight_grad - delta_piece[:, :, None])).astype(jnp.bfloat16)
        key_sum = key_sum + jnp.einsum(
            "qhk,qhd->khd", score_grad, query_three, preferred_element_type=jnp.float32
        )
        value_sum = value_sum + jnp.einsum(
            "qhk,qhd->khd",
            probs.astype(jnp.bfloat16),
            cotan_three,
            preferred_element_type=jnp.float32,
        )
        return (key_sum, value_sum)

    key_zero = jnp.zeros((own_rows, head_count, HD), jnp.float32)
    key_sum, value_sum = sweep(
        owner_work,
        (key_zero, key_zero),
        (
            lax.all_gather(query_slots.reshape(slot_rows, model_width), "tm", axis=0, tiled=True),
            lax.all_gather(cotan_slots.reshape(slot_rows, model_width), "tm", axis=0, tiled=True),
        ),
        jnp.int32(0),
    )
    key_grad = (key_sum * scaling).astype(jnp.bfloat16).reshape(own_rows, model_width)
    value_grad = value_sum.astype(jnp.bfloat16).reshape(own_rows, model_width)
    query_grad = (query_sum * scaling).astype(jnp.bfloat16).reshape(slot_rows, model_width)
    return (attended.reshape(slot_rows, model_width), query_grad, key_grad, value_grad)


def head_kernel(
    shards,
    rows,
    act_ref,
    cnt_ref,
    mask_ref,
    q_hbm,
    k_hbm,
    v_hbm,
    g_hbm,
    att_hbm,
    dq_hbm,
    dk_hbm,
    dv_hbm,
    held,
    scores,
    weights,
    grads,
    key_sum,
    value_sum,
    stage,
    stage_kv,
    in_send,
    in_recv,
    out_send,
    out_recv,
    kv_send,
    kv_recv,
    in_local,
    out_local,
    kv_local,
):
    me = lax.axis_index("tm")
    total = shards * rows
    blocks = total // BLK
    scaling = 1.0 / math.sqrt(HD)
    sources = (k_hbm, v_hbm, q_hbm, g_hbm)
    outs = (att_hbm, dq_hbm)
    kv_outs = (dk_hbm, dv_hbm)

    def columns(index):
        return pl.ds(pl.multiple_of(index * HD, HD), HD)

    def shard_rows(index):
        return pl.ds(pl.multiple_of(index * rows, rows), rows)

    def incoming(array, source, target):
        return pltpu.make_async_remote_copy(
            src_ref=sources[array].at[:, columns(target)],
            dst_ref=held.at[array, shard_rows(source), :],
            send_sem=in_send.at[array, target],
            recv_sem=in_recv.at[array, source],
            device_id={"tm": target},
            device_id_type=pl.DeviceIdType.MESH,
        )

    def own_incoming(array):
        return pltpu.make_async_copy(
            sources[array].at[:, columns(me)],
            held.at[array, shard_rows(me), :],
            in_local.at[array],
        )

    pieces = (
        (shards - 1, 0, (rows // BLK + 1) * BLK, BLK),
        (0, BLK, BLK, rows),
        (1, BLK + rows, 0, BLK),
    )

    def outgoing(array, piece, chunk, target, source):
        _, low, slot_low, size = pieces[piece]
        return pltpu.make_async_remote_copy(
            src_ref=stage.at[array, chunk, pl.ds(low, size), :],
            dst_ref=outs[array].at[pl.ds(slot_low, size), columns(source)],
            send_sem=out_send.at[array, piece, chunk],
            recv_sem=out_recv.at[array, piece, source],
            device_id={"tm": target},
            device_id_type=pl.DeviceIdType.MESH,
        )

    def own_outgoing(array, piece, chunk):
        _, low, slot_low, size = pieces[piece]
        return pltpu.make_async_copy(
            stage.at[array, chunk, pl.ds(low, size), :],
            outs[array].at[pl.ds(slot_low, size), columns(me)],
            out_local.at[array, piece],
        )

    def send_pieces(array, chunk):
        for piece in range(3):
            target = lax.rem(chunk + pieces[piece][0], shards)

            @pl.when(target == me)
            def _():
                own_outgoing(array, piece, chunk).start()

            @pl.when(target != me)
            def _():
                outgoing(array, piece, chunk, target, me).start()

    def kv_outgoing(array, source, target):
        return pltpu.make_async_remote_copy(
            src_ref=stage_kv.at[array, shard_rows(target), :],
            dst_ref=kv_outs[array].at[:, columns(source)],
            send_sem=kv_send.at[array, target],
            recv_sem=kv_recv.at[array, source],
            device_id={"tm": target},
            device_id_type=pl.DeviceIdType.MESH,
        )

    def kv_own(array):
        return pltpu.make_async_copy(
            stage_kv.at[array, shard_rows(me), :],
            kv_outs[array].at[:, columns(me)],
            kv_local.at[array],
        )

    barrier = pltpu.get_barrier_semaphore()
    for step in range(1, shards):
        pl.semaphore_signal(
            barrier,
            inc=1,
            device_id={"tm": lax.rem(me + step, shards)},
            device_id_type=pl.DeviceIdType.MESH,
        )
    for array in range(4):
        own_incoming(array).start()
    pl.semaphore_wait(barrier, shards - 1)
    for array in range(4):
        for step in range(1, shards):
            incoming(array, me, lax.rem(me + step, shards)).start()

    key_sum[...] = jnp.zeros_like(key_sum)
    value_sum[...] = jnp.zeros_like(value_sum)
    for array in range(4):
        own_incoming(array).wait()
    for array in range(2):
        for step in range(1, shards):
            source = lax.rem(me + step, shards)
            incoming(array, source, me).wait_recv()

    lane_block = lax.broadcasted_iota(jnp.int32, (1, rows), 1) // BLK

    def one_chunk(turn, carry):
        chunk = lax.rem(me + turn, shards)

        @pl.when(turn > 0)
        def _():
            incoming(2, chunk, me).wait_recv()
            incoming(3, chunk, me).wait_recv()

        own = shard_rows(chunk)
        query = held[2, own, :]
        cotan = held[3, own, :]
        peak = jnp.full((1, rows), very_low, jnp.float32)
        for b in range(blocks):
            part = pl.ds(b * BLK, BLK)
            bias = jnp.full((1, rows), very_low, jnp.float32)
            for j in range(rows // BLK):
                a = chunk * (rows // BLK) + j
                seen = act_ref[b] * act_ref[a] * mask_ref[a, b]
                level = jnp.where(seen > 0, 0.0, very_low)
                bias = jnp.where(lane_block == j, level, bias)
            tile = lax.dot_general(
                held[0, part, :], query, (((1,), (1,)), ((), ())), preferred_element_type=jnp.float32
            )
            tile = tile * scaling + bias
            scores[part, :] = tile
            peak = jnp.maximum(peak, jnp.max(tile, axis=0, keepdims=True))
        peak = jnp.maximum(peak, -1e20)
        mass = jnp.zeros((1, rows), jnp.float32)
        for b in range(blocks):
            part = pl.ds(b * BLK, BLK)
            tile = jnp.exp(scores[part, :] - peak)
            scores[part, :] = tile
            weights[part, :] = tile.astype(jnp.bfloat16)
            mass = mass + jnp.sum(tile, axis=0, keepdims=True)
        inverse = 1.0 / jnp.where(mass > 0.0, mass, 1.0)
        att_t = lax.dot_general(
            held[1], weights[...], (((0,), (0,)), ((), ())), preferred_element_type=jnp.float32
        )
        att_t = (att_t * inverse).astype(jnp.bfloat16).astype(jnp.float32)
        delta = jnp.sum(jnp.transpose(cotan.astype(jnp.float32)) * att_t, axis=0, keepdims=True)
        last = rows // BLK - 1
        to_left = cnt_ref[chunk, 0] > 0
        to_right = cnt_ref[chunk, 1] > 0

        def stage_slots(array, result):
            result = result.astype(jnp.bfloat16)
            first, final = result[:BLK], result[last * BLK :]
            zero = jnp.zeros_like(first)
            stage[array, chunk, pl.ds(0, BLK), :] = jnp.where(to_left, first, zero)
            stage[array, chunk, pl.ds(BLK, BLK), :] = jnp.where(to_left, zero, first)
            stage[array, chunk, pl.ds(rows, BLK), :] = jnp.where(to_right, zero, final)
            stage[array, chunk, pl.ds(rows + BLK, BLK), :] = jnp.where(to_right, final, zero)

        stage_slots(0, jnp.transpose(att_t))
        send_pieces(0, chunk)
        for b in range(blocks):
            part = pl.ds(b * BLK, BLK)
            tile = lax.dot_general(
                held[1, part, :], cotan, (((1,), (1,)), ((), ())), preferred_element_type=jnp.float32
            )
            probs = scores[part, :] * inverse
            grad = (probs * (tile - delta)).astype(jnp.bfloat16)
            grads[part, :] = grad
            key_sum[part, :] += jnp.dot(grad, query, preferred_element_type=jnp.float32)
            value_sum[part, :] += jnp.dot(
                probs.astype(jnp.bfloat16), cotan, preferred_element_type=jnp.float32
            )
        dq_t = lax.dot_general(
            held[0], grads[...], (((0,), (0,)), ((), ())), preferred_element_type=jnp.float32
        )
        stage_slots(1, jnp.transpose(dq_t * scaling))
        send_pieces(1, chunk)
        return carry

    lax.fori_loop(0, shards, one_chunk, 0)
    stage_kv[0] = (key_sum[...] * scaling).astype(jnp.bfloat16)
    stage_kv[1] = value_sum[...].astype(jnp.bfloat16)
    for array in range(2):
        for step in range(1, shards):
            kv_outgoing(array, me, lax.rem(me + step, shards)).start()
        kv_own(array).start()

    for step in range(1, shards):
        peer = lax.rem(me + step, shards)
        for array in range(4):
            incoming(array, me, peer).wait_send()
        for array in range(2):
            kv_outgoing(array, me, peer).wait_send()
            kv_outgoing(array, peer, me).wait_recv()
            for piece in range(3):
                outgoing(array, piece, 0, me, peer).wait_recv()
                target_chunk = lax.rem(peer + shards - pieces[piece][0], shards)
                outgoing(array, piece, target_chunk, peer, me).wait_send()
    for array in range(2):
        kv_own(array).wait()
        for piece in range(3):
            own_outgoing(array, piece, 0).wait()


def exchanged_heads(queries, key_rows, value_rows, cotangent, block_active, send_counts, block_mask):
    shards = lax.axis_size("tm")
    rows, width = queries.shape
    total = shards * rows
    slot_rows = rows + 2 * CAP * BLK
    anywhere = pl.BlockSpec(memory_space=pl.ANY)
    scalars = pl.BlockSpec(memory_space=pltpu.SMEM)
    return pl.pallas_call(
        functools.partial(head_kernel, shards, rows),
        out_shape=(
            jax.ShapeDtypeStruct((slot_rows, width), jnp.bfloat16),
            jax.ShapeDtypeStruct((slot_rows, width), jnp.bfloat16),
            jax.ShapeDtypeStruct((rows, width), jnp.bfloat16),
            jax.ShapeDtypeStruct((rows, width), jnp.bfloat16),
        ),
        in_specs=[scalars] * 3 + [anywhere] * 4,
        out_specs=(anywhere,) * 4,
        scratch_shapes=[
            pltpu.VMEM((4, total, HD), jnp.bfloat16),
            pltpu.VMEM((total, rows), jnp.float32),
            pltpu.VMEM((total, rows), jnp.bfloat16),
            pltpu.VMEM((total, rows), jnp.bfloat16),
            pltpu.VMEM((total, HD), jnp.float32),
            pltpu.VMEM((total, HD), jnp.float32),
            pltpu.VMEM((2, shards, slot_rows, HD), jnp.bfloat16),
            pltpu.VMEM((2, total, HD), jnp.bfloat16),
            pltpu.SemaphoreType.DMA((4, shards)),
            pltpu.SemaphoreType.DMA((4, shards)),
            pltpu.SemaphoreType.DMA((2, 3, shards)),
            pltpu.SemaphoreType.DMA((2, 3, shards)),
            pltpu.SemaphoreType.DMA((2, shards)),
            pltpu.SemaphoreType.DMA((2, shards)),
            pltpu.SemaphoreType.DMA((4,)),
            pltpu.SemaphoreType.DMA((2, 3)),
            pltpu.SemaphoreType.DMA((2,)),
        ],
        compiler_params=pltpu.CompilerParams(
            collective_id=0, has_side_effects=True, vmem_limit_bytes=40 * 1024 * 1024
        ),
    )(block_active, send_counts, block_mask, queries, key_rows, value_rows, cotangent)


def routed(queries, key_rows, value_rows, cotangent, block_active, send_counts, block_mask):
    shards = lax.axis_size("tm")
    rows, width = queries.shape
    args = (queries, key_rows, value_rows, cotangent, block_active, send_counts, block_mask)
    if shards > 1 and width == shards * HD and rows == 2 * BLK:
        return exchanged_heads(*args)
    return body(*args)


def solution(mesh):
    in_specs = (
        P(("groups", "tm"), ("head", "mp")),
        P(("groups", "tm"), ("head", "mp")),
        P(("groups", "tm"), ("head", "mp")),
        P(("groups", "tm"), ("head", "mp")),
        P("groups"),
        P("groups", None),
        P("groups", None),
    )
    out_specs = (
        P(("groups", "tm"), ("head", "mp")),
        P(("groups", "tm"), ("head", "mp")),
        P(("groups", "tm"), ("head", "mp")),
        P(("groups", "tm"), ("head", "mp")),
    )
    return jax.shard_map(
        routed, mesh=mesh, in_specs=in_specs, out_specs=out_specs, check_vma=False)
```

```python
import functools
import math

import jax
import jax.numpy as jnp
from jax import lax
from jax.experimental import pallas as pl
from jax.experimental.pallas import tpu as pltpu
from jax.sharding import PartitionSpec as P

HD = 128
BLK = 128
CAP = 1


very_low = -1e30


def extended_2(shard, sides, width):
    for axis, dim in sides:
        peers, length = (lax.axis_size(axis), shard.shape[dim])
        up = [(i, (i + 1) % peers) for i in range(peers)]
        down = [(j, i) for i, j in up]
        last = lax.slice_in_dim(shard, length - width, length, axis=dim)
        first = lax.slice_in_dim(shard, 0, width, axis=dim)
        before = lax.ppermute(last, axis, up)
        after = lax.ppermute(first, axis, down)
        shard = jnp.concatenate([before, shard, after], axis=dim)
    return shard


def pick(table, positions, extent):
    matches = positions[:, None] == jnp.arange(extent, dtype=jnp.int32)[None, :]
    return jnp.sum(jnp.where(matches, table[None, :], 0), axis=1)


def slot_layout(block_active, send_counts, block_mask, shards, own_blocks, capacity):
    slot_count = own_blocks + 2 * capacity
    all_blocks = shards * own_blocks
    places = jnp.arange(shards * slot_count, dtype=jnp.int32)
    device = places // slot_count
    slot_index = places % slot_count
    before = (device + shards - 1) % shards
    following = (device + 1) % shards
    to_left = send_counts[:, 0]
    to_right = send_counts[:, 1]
    from_before = slot_index < capacity
    from_after = slot_index >= capacity + own_blocks
    owner_shard = jnp.where(from_before, before, jnp.where(from_after, following, device))
    local_block = jnp.where(
        from_before,
        own_blocks - capacity + slot_index,
        jnp.where(from_after, slot_index - capacity - own_blocks, slot_index - capacity),
    )
    middle_ok = (local_block >= pick(to_left, device, shards)) & (
        local_block < own_blocks - pick(to_right, device, shards)
    )
    holds_record = jnp.where(
        from_before,
        slot_index >= capacity - pick(to_right, before, shards),
        jnp.where(from_after, local_block < pick(to_left, following, shards), middle_ok),
    )
    anchor = owner_shard * own_blocks + local_block
    onehot = (anchor[:, None] == jnp.arange(all_blocks, dtype=jnp.int32)[None, :]).astype(
        jnp.float32
    )
    seeing = (block_mask * block_active[None, :]).astype(jnp.float32)
    block_rows = jnp.dot(onehot, seeing, precision=lax.Precision.HIGHEST)
    active = jnp.dot(onehot, block_active.astype(jnp.float32), precision=lax.Precision.HIGHEST)
    present = jnp.where(holds_record, active, 0.0)
    return (anchor, block_rows * present[:, None], present)


def block_hot(offset, length, extent):
    blocks = (offset + jnp.arange(length, dtype=jnp.int32)) // BLK
    return (blocks[:, None] == jnp.arange(extent, dtype=jnp.int32)[None, :]).astype(jnp.bfloat16)


def sweep(update, running, pieces, offset):
    row_count = pieces[0].shape[0]
    step_rows = math.gcd(row_count, 1024)
    if step_rows == row_count:
        return update(running, pieces, offset)

    def one_turn(turn_index, carried):
        part_pieces = tuple(
            (
                lax.dynamic_slice_in_dim(member, turn_index * step_rows, step_rows, 0)
                for member in pieces
            )
        )
        return update(carried, part_pieces, offset + turn_index * step_rows)

    return lax.fori_loop(0, row_count // step_rows, one_turn, running)


def body(queries, key_rows, value_rows, cotangent, block_active, send_counts, block_mask):
    shards = lax.axis_size("tm")
    shard_index = lax.axis_index("tm")
    model_width = queries.shape[1]
    head_count = model_width // HD
    own_rows = queries.shape[0]
    own_blocks = own_rows // BLK
    all_blocks = block_active.shape[0]
    slot_count = own_blocks + 2 * CAP
    slot_rows = slot_count * BLK
    scaling = 1.0 / math.sqrt(HD)
    anchor, table, present = slot_layout(
        block_active, send_counts, block_mask, shards, own_blocks, CAP
    )
    records = jnp.concatenate([queries, cotangent], axis=1)
    extended = extended_2(records, (("tm", 0),), CAP * BLK)
    query_slots = extended[:, :model_width].reshape(slot_rows, head_count, HD)
    cotan_slots = extended[:, model_width:].reshape(slot_rows, head_count, HD)
    my_table = lax.dynamic_slice_in_dim(table, shard_index * slot_count, slot_count, 0)
    query_table = jnp.repeat(my_table, BLK, axis=0).astype(jnp.bfloat16)
    live = (
        jnp.repeat(lax.dynamic_slice_in_dim(present, shard_index * slot_count, slot_count, 0), BLK)
        > 0.5
    )
    keys_all, values_all = (
        lax.all_gather(key_rows, "tm", axis=0, tiled=True),
        lax.all_gather(value_rows, "tm", axis=0, tiled=True),
    )

    def own_scores(key_piece, offset):
        allowed = (
            lax.dot_general(
                query_table,
                block_hot(offset, key_piece.shape[0], all_blocks),
                (((1,), (1,)), ((), ())),
                preferred_element_type=jnp.float32,
            )[:, None, :]
            > 0.5
        )
        scores = (
            jnp.einsum("qhd,khd->qhk", query_slots, key_piece, preferred_element_type=jnp.float32)
            * scaling
        )
        return (allowed, scores)

    def forward(running, pieces, offset):
        peak, masses, accum = running
        key_piece = pieces[0].reshape(-1, head_count, HD)
        value_piece = pieces[1].reshape(-1, head_count, HD)
        allowed, scores = own_scores(key_piece, offset)
        new_peak = jnp.maximum(peak, jnp.max(jnp.where(allowed, scores, very_low), axis=2))
        weights = jnp.where(
            allowed, jnp.exp(jnp.where(allowed, scores - new_peak[:, :, None], 0.0)), 0.0
        )
        shrink = jnp.exp(peak - new_peak)
        masses = masses * shrink + jnp.sum(weights, axis=2)
        accum = accum * shrink[:, :, None] + jnp.einsum(
            "qhk,khd->qhd",
            weights.astype(jnp.bfloat16),
            value_piece,
            preferred_element_type=jnp.float32,
        )
        return (new_peak, masses, accum)

    initial = (
        jnp.full((slot_rows, head_count), very_low, jnp.float32),
        jnp.zeros((slot_rows, head_count), jnp.float32),
        jnp.zeros((slot_rows, head_count, HD), jnp.float32),
    )
    peak, masses, accum = sweep(forward, initial, (keys_all, values_all), 0)
    denominator = jnp.where(live[:, None], masses, 1.0)
    attended = (accum / denominator[:, :, None]).astype(jnp.bfloat16)
    log_norm = peak + jnp.log(denominator)
    deltas = jnp.sum(cotan_slots.astype(jnp.float32) * attended.astype(jnp.float32), axis=2)

    def own_gradients(key_piece, value_piece, offset):
        allowed, scores = own_scores(key_piece, offset)
        probs = jnp.where(
            allowed, jnp.exp(jnp.where(allowed, scores - log_norm[:, :, None], 0.0)), 0.0
        )
        weight_grad = jnp.einsum(
            "qhd,khd->qhk", cotan_slots, value_piece, preferred_element_type=jnp.float32
        )
        return (probs, (probs * (weight_grad - deltas[:, :, None])).astype(jnp.bfloat16))

    zero_query = jnp.zeros((slot_rows, head_count, HD), jnp.float32)

    def query_pass(query_sum, pieces, offset):
        key_piece = pieces[0].reshape(-1, head_count, HD)
        value_piece = pieces[1].reshape(-1, head_count, HD)
        probs, score_grad = own_gradients(key_piece, value_piece, offset)
        return query_sum + jnp.einsum(
            "qhk,khd->qhd", score_grad, key_piece, preferred_element_type=jnp.float32
        )

    query_sum = sweep(query_pass, zero_query, (keys_all, values_all), 0)
    own_keys = key_rows.reshape(own_rows, head_count, HD)
    own_values = value_rows.reshape(own_rows, head_count, HD)
    own_hot = block_hot(shard_index * own_rows, own_rows, all_blocks)
    slot_table = table.astype(jnp.bfloat16)
    logsum_all, delta_all = (
        lax.all_gather(log_norm, "tm", axis=0, tiled=True),
        lax.all_gather(deltas, "tm", axis=0, tiled=True),
    )

    def owner_work(running, pieces, offset):
        key_sum, value_sum = running
        query_piece, cotan_piece = pieces
        row_count = query_piece.shape[0]
        logsum_piece = lax.dynamic_slice_in_dim(logsum_all, offset, row_count, 0)
        delta_piece = lax.dynamic_slice_in_dim(delta_all, offset, row_count, 0)
        piece_table = jnp.dot(
            block_hot(offset, row_count, shards * slot_count),
            slot_table,
            preferred_element_type=jnp.float32,
        ).astype(jnp.bfloat16)
        allowed = (
            lax.dot_general(
                piece_table, own_hot, (((1,), (1,)), ((), ())), preferred_element_type=jnp.float32
            )[:, None, :]
            > 0.5
        )
        query_three = query_piece.reshape(row_count, head_count, HD)
        cotan_three = cotan_piece.reshape(row_count, head_count, HD)
        scores = (
            jnp.einsum("qhd,khd->qhk", query_three, own_keys, preferred_element_type=jnp.float32)
            * scaling
        )
        probs = jnp.where(
            allowed, jnp.exp(jnp.where(allowed, scores - logsum_piece[:, :, None], 0.0)), 0.0
        )
        weight_grad = jnp.einsum(
            "qhd,khd->qhk", cotan_three, own_values, preferred_element_type=jnp.float32
        )
        score_grad = (probs * (weight_grad - delta_piece[:, :, None])).astype(jnp.bfloat16)
        key_sum = key_sum + jnp.einsum(
            "qhk,qhd->khd", score_grad, query_three, preferred_element_type=jnp.float32
        )
        value_sum = value_sum + jnp.einsum(
            "qhk,qhd->khd",
            probs.astype(jnp.bfloat16),
            cotan_three,
            preferred_element_type=jnp.float32,
        )
        return (key_sum, value_sum)

    key_zero = jnp.zeros((own_rows, head_count, HD), jnp.float32)
    key_sum, value_sum = sweep(
        owner_work,
        (key_zero, key_zero),
        (
            lax.all_gather(query_slots.reshape(slot_rows, model_width), "tm", axis=0, tiled=True),
            lax.all_gather(cotan_slots.reshape(slot_rows, model_width), "tm", axis=0, tiled=True),
        ),
        jnp.int32(0),
    )
    key_grad = (key_sum * scaling).astype(jnp.bfloat16).reshape(own_rows, model_width)
    value_grad = value_sum.astype(jnp.bfloat16).reshape(own_rows, model_width)
    query_grad = (query_sum * scaling).astype(jnp.bfloat16).reshape(slot_rows, model_width)
    return (attended.reshape(slot_rows, model_width), query_grad, key_grad, value_grad)


def head_kernel(
    shards,
    rows,
    act_ref,
    cnt_ref,
    mask_ref,
    q_hbm,
    k_hbm,
    v_hbm,
    g_hbm,
    att_hbm,
    dq_hbm,
    dk_hbm,
    dv_hbm,
    held,
    scores,
    weights,
    grads,
    key_sum,
    value_sum,
    stage,
    stage_kv,
    in_send,
    in_recv,
    out_send,
    out_recv,
    kv_send,
    kv_recv,
    in_local,
    out_local,
    kv_local,
):
    me = lax.axis_index("tm")
    total = shards * rows
    blocks = total // BLK
    scaling = 1.0 / math.sqrt(HD)
    sources = (k_hbm, v_hbm, q_hbm, g_hbm)
    outs = (att_hbm, dq_hbm)
    kv_outs = (dk_hbm, dv_hbm)

    def columns(index):
        return pl.ds(pl.multiple_of(index * HD, HD), HD)

    def shard_rows(index):
        return pl.ds(pl.multiple_of(index * rows, rows), rows)

    def incoming(array, source, target):
        return pltpu.make_async_remote_copy(
            src_ref=sources[array].at[:, columns(target)],
            dst_ref=held.at[array, shard_rows(source), :],
            send_sem=in_send.at[array, target],
            recv_sem=in_recv.at[array, source],
            device_id={"tm": target},
            device_id_type=pl.DeviceIdType.MESH,
        )

    def own_incoming(array):
        return pltpu.make_async_copy(
            sources[array].at[:, columns(me)],
            held.at[array, shard_rows(me), :],
            in_local.at[array],
        )

    pieces = (
        (shards - 1, 0, (rows // BLK + 1) * BLK, BLK),
        (0, BLK, BLK, rows),
        (1, BLK + rows, 0, BLK),
    )

    def outgoing(array, piece, chunk, target, source):
        _, low, slot_low, size = pieces[piece]
        return pltpu.make_async_remote_copy(
            src_ref=stage.at[array, chunk, pl.ds(low, size), :],
            dst_ref=outs[array].at[pl.ds(slot_low, size), columns(source)],
            send_sem=out_send.at[array, piece, chunk],
            recv_sem=out_recv.at[array, piece, source],
            device_id={"tm": target},
            device_id_type=pl.DeviceIdType.MESH,
        )

    def own_outgoing(array, piece, chunk):
        _, low, slot_low, size = pieces[piece]
        return pltpu.make_async_copy(
            stage.at[array, chunk, pl.ds(low, size), :],
            outs[array].at[pl.ds(slot_low, size), columns(me)],
            out_local.at[array, piece],
        )

    def send_pieces(array, chunk):
        for piece in range(3):
            target = lax.rem(chunk + pieces[piece][0], shards)

            @pl.when(target == me)
            def _():
                own_outgoing(array, piece, chunk).start()

            @pl.when(target != me)
            def _():
                outgoing(array, piece, chunk, target, me).start()

    def kv_outgoing(array, source, target):
        return pltpu.make_async_remote_copy(
            src_ref=stage_kv.at[array, shard_rows(target), :],
            dst_ref=kv_outs[array].at[:, columns(source)],
            send_sem=kv_send.at[array, target],
            recv_sem=kv_recv.at[array, source],
            device_id={"tm": target},
            device_id_type=pl.DeviceIdType.MESH,
        )

    def kv_own(array):
        return pltpu.make_async_copy(
            stage_kv.at[array, shard_rows(me), :],
            kv_outs[array].at[:, columns(me)],
            kv_local.at[array],
        )

    barrier = pltpu.get_barrier_semaphore()
    for step in range(1, shards):
        pl.semaphore_signal(
            barrier,
            inc=1,
            device_id={"tm": lax.rem(me + step, shards)},
            device_id_type=pl.DeviceIdType.MESH,
        )
    for array in range(4):
        own_incoming(array).start()
    pl.semaphore_wait(barrier, shards - 1)
    for array in range(4):
        for step in range(1, shards):
            incoming(array, me, lax.rem(me + step, shards)).start()

    key_sum[...] = jnp.zeros_like(key_sum)
    value_sum[...] = jnp.zeros_like(value_sum)
    for array in range(4):
        own_incoming(array).wait()
    for array in range(2):
        for step in range(1, shards):
            source = lax.rem(me + step, shards)
            incoming(array, source, me).wait_recv()

    lane_block = lax.broadcasted_iota(jnp.int32, (1, rows), 1) // BLK

    def one_chunk(turn, carry):
        pair = turn // 2
        side = (turn - 2 * pair) * (1 - 2 * lax.rem(me, 2))
        chunk = lax.rem(me + side + shards // 2 + 2 * pair + shards, shards)

        @pl.when(chunk != me)
        def _():
            incoming(2, chunk, me).wait_recv()
            incoming(3, chunk, me).wait_recv()

        own = shard_rows(chunk)
        query = held[2, own, :]
        cotan = held[3, own, :]
        peak = jnp.full((1, rows), very_low, jnp.float32)
        for b in range(blocks):
            part = pl.ds(b * BLK, BLK)
            bias = jnp.full((1, rows), very_low, jnp.float32)
            for j in range(rows // BLK):
                a = chunk * (rows // BLK) + j
                seen = act_ref[b] * act_ref[a] * mask_ref[a, b]
                level = jnp.where(seen > 0, 0.0, very_low)
                bias = jnp.where(lane_block == j, level, bias)
            tile = lax.dot_general(
                held[0, part, :], query, (((1,), (1,)), ((), ())), preferred_element_type=jnp.float32
            )
            tile = tile * scaling + bias
            scores[part, :] = tile
            peak = jnp.maximum(peak, jnp.max(tile, axis=0, keepdims=True))
        peak = jnp.maximum(peak, -1e20)
        mass = jnp.zeros((1, rows), jnp.float32)
        for b in range(blocks):
            part = pl.ds(b * BLK, BLK)
            tile = jnp.exp(scores[part, :] - peak)
            scores[part, :] = tile
            weights[part, :] = tile.astype(jnp.bfloat16)
            mass = mass + jnp.sum(tile, axis=0, keepdims=True)
        inverse = 1.0 / jnp.where(mass > 0.0, mass, 1.0)
        att_t = lax.dot_general(
            held[1], weights[...], (((0,), (0,)), ((), ())), preferred_element_type=jnp.float32
        )
        att_t = (att_t * inverse).astype(jnp.bfloat16).astype(jnp.float32)
        delta = jnp.sum(jnp.transpose(cotan.astype(jnp.float32)) * att_t, axis=0, keepdims=True)
        last = rows // BLK - 1
        to_left = cnt_ref[chunk, 0] > 0
        to_right = cnt_ref[chunk, 1] > 0

        def stage_slots(array, result):
            result = result.astype(jnp.bfloat16)
            first, final = result[:BLK], result[last * BLK :]
            zero = jnp.zeros_like(first)
            stage[array, chunk, pl.ds(0, BLK), :] = jnp.where(to_left, first, zero)
            stage[array, chunk, pl.ds(BLK, BLK), :] = jnp.where(to_left, zero, first)
            stage[array, chunk, pl.ds(rows, BLK), :] = jnp.where(to_right, zero, final)
            stage[array, chunk, pl.ds(rows + BLK, BLK), :] = jnp.where(to_right, final, zero)

        stage_slots(0, jnp.transpose(att_t))
        send_pieces(0, chunk)
        for b in range(blocks):
            part = pl.ds(b * BLK, BLK)
            tile = lax.dot_general(
                held[1, part, :], cotan, (((1,), (1,)), ((), ())), preferred_element_type=jnp.float32
            )
            probs = scores[part, :] * inverse
            grad = (probs * (tile - delta)).astype(jnp.bfloat16)
            grads[part, :] = grad
            key_sum[part, :] += jnp.dot(grad, query, preferred_element_type=jnp.float32)
            value_sum[part, :] += jnp.dot(
                probs.astype(jnp.bfloat16), cotan, preferred_element_type=jnp.float32
            )
        dq_t = lax.dot_general(
            held[0], grads[...], (((0,), (0,)), ((), ())), preferred_element_type=jnp.float32
        )
        stage_slots(1, jnp.transpose(dq_t * scaling))
        send_pieces(1, chunk)
        return carry

    lax.fori_loop(0, shards, one_chunk, 0)
    stage_kv[0] = (key_sum[...] * scaling).astype(jnp.bfloat16)
    stage_kv[1] = value_sum[...].astype(jnp.bfloat16)
    for array in range(2):
        for step in range(1, shards):
            kv_outgoing(array, me, lax.rem(me + step, shards)).start()
        kv_own(array).start()

    for step in range(1, shards):
        peer = lax.rem(me + step, shards)
        for array in range(4):
            incoming(array, me, peer).wait_send()
        for array in range(2):
            kv_outgoing(array, me, peer).wait_send()
            kv_outgoing(array, peer, me).wait_recv()
            for piece in range(3):
                outgoing(array, piece, 0, me, peer).wait_recv()
                target_chunk = lax.rem(peer + shards - pieces[piece][0], shards)
                outgoing(array, piece, target_chunk, peer, me).wait_send()
    for array in range(2):
        kv_own(array).wait()
        for piece in range(3):
            own_outgoing(array, piece, 0).wait()


def exchanged_heads(queries, key_rows, value_rows, cotangent, block_active, send_counts, block_mask):
    shards = lax.axis_size("tm")
    rows, width = queries.shape
    total = shards * rows
    slot_rows = rows + 2 * CAP * BLK
    anywhere = pl.BlockSpec(memory_space=pl.ANY)
    scalars = pl.BlockSpec(memory_space=pltpu.SMEM)
    return pl.pallas_call(
        functools.partial(head_kernel, shards, rows),
        out_shape=(
            jax.ShapeDtypeStruct((slot_rows, width), jnp.bfloat16),
            jax.ShapeDtypeStruct((slot_rows, width), jnp.bfloat16),
            jax.ShapeDtypeStruct((rows, width), jnp.bfloat16),
            jax.ShapeDtypeStruct((rows, width), jnp.bfloat16),
        ),
        in_specs=[scalars] * 3 + [pl.BlockSpec(memory_space=pltpu.HBM)] * 4,
        out_specs=(anywhere,) * 4,
        scratch_shapes=[
            pltpu.VMEM((4, total, HD), jnp.bfloat16),
            pltpu.VMEM((total, rows), jnp.float32),
            pltpu.VMEM((total, rows), jnp.bfloat16),
            pltpu.VMEM((total, rows), jnp.bfloat16),
            pltpu.VMEM((total, HD), jnp.float32),
            pltpu.VMEM((total, HD), jnp.float32),
            pltpu.VMEM((2, shards, slot_rows, HD), jnp.bfloat16),
            pltpu.VMEM((2, total, HD), jnp.bfloat16),
            pltpu.SemaphoreType.DMA((4, shards)),
            pltpu.SemaphoreType.DMA((4, shards)),
            pltpu.SemaphoreType.DMA((2, 3, shards)),
            pltpu.SemaphoreType.DMA((2, 3, shards)),
            pltpu.SemaphoreType.DMA((2, shards)),
            pltpu.SemaphoreType.DMA((2, shards)),
            pltpu.SemaphoreType.DMA((4,)),
            pltpu.SemaphoreType.DMA((2, 3)),
            pltpu.SemaphoreType.DMA((2,)),
        ],
        compiler_params=pltpu.CompilerParams(
            collective_id=0, has_side_effects=True, vmem_limit_bytes=40 * 1024 * 1024
        ),
    )(block_active, send_counts, block_mask, queries, key_rows, value_rows, cotangent)


def routed(queries, key_rows, value_rows, cotangent, block_active, send_counts, block_mask):
    shards = lax.axis_size("tm")
    rows, width = queries.shape
    args = (queries, key_rows, value_rows, cotangent, block_active, send_counts, block_mask)
    if shards % 2 == 0 and width == shards * HD and rows == 2 * BLK:
        return exchanged_heads(*args)
    return body(*args)


def solution(mesh):
    in_specs = (
        P(("groups", "tm"), ("head", "mp")),
        P(("groups", "tm"), ("head", "mp")),
        P(("groups", "tm"), ("head", "mp")),
        P(("groups", "tm"), ("head", "mp")),
        P("groups"),
        P("groups", None),
        P("groups", None),
    )
    out_specs = (
        P(("groups", "tm"), ("head", "mp")),
        P(("groups", "tm"), ("head", "mp")),
        P(("groups", "tm"), ("head", "mp")),
        P(("groups", "tm"), ("head", "mp")),
    )
    return jax.shard_map(
        routed, mesh=mesh, in_specs=in_specs, out_specs=out_specs, check_vma=False)
```

```python
import functools
import math

import jax
import jax.numpy as jnp
from jax import lax
from jax.experimental import pallas as pl
from jax.experimental.pallas import tpu as pltpu
from jax.sharding import PartitionSpec as P

HD = 128
BLK = 128
CAP = 1


very_low = -1e30


def extended_2(shard, sides, width):
    for axis, dim in sides:
        peers, length = (lax.axis_size(axis), shard.shape[dim])
        up = [(i, (i + 1) % peers) for i in range(peers)]
        down = [(j, i) for i, j in up]
        last = lax.slice_in_dim(shard, length - width, length, axis=dim)
        first = lax.slice_in_dim(shard, 0, width, axis=dim)
        before = lax.ppermute(last, axis, up)
        after = lax.ppermute(first, axis, down)
        shard = jnp.concatenate([before, shard, after], axis=dim)
    return shard


def pick(table, positions, extent):
    matches = positions[:, None] == jnp.arange(extent, dtype=jnp.int32)[None, :]
    return jnp.sum(jnp.where(matches, table[None, :], 0), axis=1)


def slot_layout(block_active, send_counts, block_mask, shards, own_blocks, capacity):
    slot_count = own_blocks + 2 * capacity
    all_blocks = shards * own_blocks
    places = jnp.arange(shards * slot_count, dtype=jnp.int32)
    device = places // slot_count
    slot_index = places % slot_count
    before = (device + shards - 1) % shards
    following = (device + 1) % shards
    to_left = send_counts[:, 0]
    to_right = send_counts[:, 1]
    from_before = slot_index < capacity
    from_after = slot_index >= capacity + own_blocks
    owner_shard = jnp.where(from_before, before, jnp.where(from_after, following, device))
    local_block = jnp.where(
        from_before,
        own_blocks - capacity + slot_index,
        jnp.where(from_after, slot_index - capacity - own_blocks, slot_index - capacity),
    )
    middle_ok = (local_block >= pick(to_left, device, shards)) & (
        local_block < own_blocks - pick(to_right, device, shards)
    )
    holds_record = jnp.where(
        from_before,
        slot_index >= capacity - pick(to_right, before, shards),
        jnp.where(from_after, local_block < pick(to_left, following, shards), middle_ok),
    )
    anchor = owner_shard * own_blocks + local_block
    onehot = (anchor[:, None] == jnp.arange(all_blocks, dtype=jnp.int32)[None, :]).astype(
        jnp.float32
    )
    seeing = (block_mask * block_active[None, :]).astype(jnp.float32)
    block_rows = jnp.dot(onehot, seeing, precision=lax.Precision.HIGHEST)
    active = jnp.dot(onehot, block_active.astype(jnp.float32), precision=lax.Precision.HIGHEST)
    present = jnp.where(holds_record, active, 0.0)
    return (anchor, block_rows * present[:, None], present)


def block_hot(offset, length, extent):
    blocks = (offset + jnp.arange(length, dtype=jnp.int32)) // BLK
    return (blocks[:, None] == jnp.arange(extent, dtype=jnp.int32)[None, :]).astype(jnp.bfloat16)


def sweep(update, running, pieces, offset):
    row_count = pieces[0].shape[0]
    step_rows = math.gcd(row_count, 1024)
    if step_rows == row_count:
        return update(running, pieces, offset)

    def one_turn(turn_index, carried):
        part_pieces = tuple(
            (
                lax.dynamic_slice_in_dim(member, turn_index * step_rows, step_rows, 0)
                for member in pieces
            )
        )
        return update(carried, part_pieces, offset + turn_index * step_rows)

    return lax.fori_loop(0, row_count // step_rows, one_turn, running)


def body(queries, key_rows, value_rows, cotangent, block_active, send_counts, block_mask):
    shards = lax.axis_size("tm")
    shard_index = lax.axis_index("tm")
    model_width = queries.shape[1]
    head_count = model_width // HD
    own_rows = queries.shape[0]
    own_blocks = own_rows // BLK
    all_blocks = block_active.shape[0]
    slot_count = own_blocks + 2 * CAP
    slot_rows = slot_count * BLK
    scaling = 1.0 / math.sqrt(HD)
    anchor, table, present = slot_layout(
        block_active, send_counts, block_mask, shards, own_blocks, CAP
    )
    records = jnp.concatenate([queries, cotangent], axis=1)
    extended = extended_2(records, (("tm", 0),), CAP * BLK)
    query_slots = extended[:, :model_width].reshape(slot_rows, head_count, HD)
    cotan_slots = extended[:, model_width:].reshape(slot_rows, head_count, HD)
    my_table = lax.dynamic_slice_in_dim(table, shard_index * slot_count, slot_count, 0)
    query_table = jnp.repeat(my_table, BLK, axis=0).astype(jnp.bfloat16)
    live = (
        jnp.repeat(lax.dynamic_slice_in_dim(present, shard_index * slot_count, slot_count, 0), BLK)
        > 0.5
    )
    keys_all, values_all = (
        lax.all_gather(key_rows, "tm", axis=0, tiled=True),
        lax.all_gather(value_rows, "tm", axis=0, tiled=True),
    )

    def own_scores(key_piece, offset):
        allowed = (
            lax.dot_general(
                query_table,
                block_hot(offset, key_piece.shape[0], all_blocks),
                (((1,), (1,)), ((), ())),
                preferred_element_type=jnp.float32,
            )[:, None, :]
            > 0.5
        )
        scores = (
            jnp.einsum("qhd,khd->qhk", query_slots, key_piece, preferred_element_type=jnp.float32)
            * scaling
        )
        return (allowed, scores)

    def forward(running, pieces, offset):
        peak, masses, accum = running
        key_piece = pieces[0].reshape(-1, head_count, HD)
        value_piece = pieces[1].reshape(-1, head_count, HD)
        allowed, scores = own_scores(key_piece, offset)
        new_peak = jnp.maximum(peak, jnp.max(jnp.where(allowed, scores, very_low), axis=2))
        weights = jnp.where(
            allowed, jnp.exp(jnp.where(allowed, scores - new_peak[:, :, None], 0.0)), 0.0
        )
        shrink = jnp.exp(peak - new_peak)
        masses = masses * shrink + jnp.sum(weights, axis=2)
        accum = accum * shrink[:, :, None] + jnp.einsum(
            "qhk,khd->qhd",
            weights.astype(jnp.bfloat16),
            value_piece,
            preferred_element_type=jnp.float32,
        )
        return (new_peak, masses, accum)

    initial = (
        jnp.full((slot_rows, head_count), very_low, jnp.float32),
        jnp.zeros((slot_rows, head_count), jnp.float32),
        jnp.zeros((slot_rows, head_count, HD), jnp.float32),
    )
    peak, masses, accum = sweep(forward, initial, (keys_all, values_all), 0)
    denominator = jnp.where(live[:, None], masses, 1.0)
    attended = (accum / denominator[:, :, None]).astype(jnp.bfloat16)
    log_norm = peak + jnp.log(denominator)
    deltas = jnp.sum(cotan_slots.astype(jnp.float32) * attended.astype(jnp.float32), axis=2)

    def own_gradients(key_piece, value_piece, offset):
        allowed, scores = own_scores(key_piece, offset)
        probs = jnp.where(
            allowed, jnp.exp(jnp.where(allowed, scores - log_norm[:, :, None], 0.0)), 0.0
        )
        weight_grad = jnp.einsum(
            "qhd,khd->qhk", cotan_slots, value_piece, preferred_element_type=jnp.float32
        )
        return (probs, (probs * (weight_grad - deltas[:, :, None])).astype(jnp.bfloat16))

    zero_query = jnp.zeros((slot_rows, head_count, HD), jnp.float32)

    def query_pass(query_sum, pieces, offset):
        key_piece = pieces[0].reshape(-1, head_count, HD)
        value_piece = pieces[1].reshape(-1, head_count, HD)
        probs, score_grad = own_gradients(key_piece, value_piece, offset)
        return query_sum + jnp.einsum(
            "qhk,khd->qhd", score_grad, key_piece, preferred_element_type=jnp.float32
        )

    query_sum = sweep(query_pass, zero_query, (keys_all, values_all), 0)
    own_keys = key_rows.reshape(own_rows, head_count, HD)
    own_values = value_rows.reshape(own_rows, head_count, HD)
    own_hot = block_hot(shard_index * own_rows, own_rows, all_blocks)
    slot_table = table.astype(jnp.bfloat16)
    logsum_all, delta_all = (
        lax.all_gather(log_norm, "tm", axis=0, tiled=True),
        lax.all_gather(deltas, "tm", axis=0, tiled=True),
    )

    def owner_work(running, pieces, offset):
        key_sum, value_sum = running
        query_piece, cotan_piece = pieces
        row_count = query_piece.shape[0]
        logsum_piece = lax.dynamic_slice_in_dim(logsum_all, offset, row_count, 0)
        delta_piece = lax.dynamic_slice_in_dim(delta_all, offset, row_count, 0)
        piece_table = jnp.dot(
            block_hot(offset, row_count, shards * slot_count),
            slot_table,
            preferred_element_type=jnp.float32,
        ).astype(jnp.bfloat16)
        allowed = (
            lax.dot_general(
                piece_table, own_hot, (((1,), (1,)), ((), ())), preferred_element_type=jnp.float32
            )[:, None, :]
            > 0.5
        )
        query_three = query_piece.reshape(row_count, head_count, HD)
        cotan_three = cotan_piece.reshape(row_count, head_count, HD)
        scores = (
            jnp.einsum("qhd,khd->qhk", query_three, own_keys, preferred_element_type=jnp.float32)
            * scaling
        )
        probs = jnp.where(
            allowed, jnp.exp(jnp.where(allowed, scores - logsum_piece[:, :, None], 0.0)), 0.0
        )
        weight_grad = jnp.einsum(
            "qhd,khd->qhk", cotan_three, own_values, preferred_element_type=jnp.float32
        )
        score_grad = (probs * (weight_grad - delta_piece[:, :, None])).astype(jnp.bfloat16)
        key_sum = key_sum + jnp.einsum(
            "qhk,qhd->khd", score_grad, query_three, preferred_element_type=jnp.float32
        )
        value_sum = value_sum + jnp.einsum(
            "qhk,qhd->khd",
            probs.astype(jnp.bfloat16),
            cotan_three,
            preferred_element_type=jnp.float32,
        )
        return (key_sum, value_sum)

    key_zero = jnp.zeros((own_rows, head_count, HD), jnp.float32)
    key_sum, value_sum = sweep(
        owner_work,
        (key_zero, key_zero),
        (
            lax.all_gather(query_slots.reshape(slot_rows, model_width), "tm", axis=0, tiled=True),
            lax.all_gather(cotan_slots.reshape(slot_rows, model_width), "tm", axis=0, tiled=True),
        ),
        jnp.int32(0),
    )
    key_grad = (key_sum * scaling).astype(jnp.bfloat16).reshape(own_rows, model_width)
    value_grad = value_sum.astype(jnp.bfloat16).reshape(own_rows, model_width)
    query_grad = (query_sum * scaling).astype(jnp.bfloat16).reshape(slot_rows, model_width)
    return (attended.reshape(slot_rows, model_width), query_grad, key_grad, value_grad)


def head_kernel(
    shards,
    rows,
    act_ref,
    cnt_ref,
    mask_ref,
    q_hbm,
    k_hbm,
    v_hbm,
    g_hbm,
    att_hbm,
    dq_hbm,
    dk_hbm,
    dv_hbm,
    held,
    scores,
    weights,
    grads,
    key_sum,
    value_sum,
    stage,
    stage_kv,
    in_send,
    in_recv,
    out_send,
    out_recv,
    kv_send,
    kv_recv,
    in_local,
    out_local,
    kv_local,
    relay_in,
    relay_own,
    relay_on,
    relay_recv,
    on_send,
    on_recv,
    relay_local,
):
    me = lax.axis_index("tm")
    half = me // 2
    up = lax.rem(me, 2)
    near = 2 - half
    neighbour = me + 1 - 2 * up
    is_near = me == 1 + half
    total = shards * rows
    blocks = total // BLK
    scaling = 1.0 / math.sqrt(HD)
    sources = (k_hbm, v_hbm, q_hbm, g_hbm)
    outs = (att_hbm, dq_hbm)
    kv_outs = (dk_hbm, dv_hbm)

    def columns(index):
        return pl.ds(pl.multiple_of(index * HD, HD), HD)

    def shard_rows(index):
        return pl.ds(pl.multiple_of(index * rows, rows), rows)

    def incoming(array, source, target):
        return pltpu.make_async_remote_copy(
            src_ref=sources[array].at[:, columns(target)],
            dst_ref=held.at[array, shard_rows(source), :],
            send_sem=in_send.at[array, target],
            recv_sem=in_recv.at[array, source],
            device_id={"tm": target},
            device_id_type=pl.DeviceIdType.MESH,
        )

    def own_incoming(array):
        return pltpu.make_async_copy(
            sources[array].at[:, columns(me)],
            held.at[array, shard_rows(me), :],
            in_local.at[array],
        )

    pieces = (
        (shards - 1, 0, (rows // BLK + 1) * BLK, BLK),
        (0, BLK, BLK, rows),
        (1, BLK + rows, 0, BLK),
    )

    def outgoing(array, piece, chunk, target, source):
        _, low, slot_low, size = pieces[piece]
        return pltpu.make_async_remote_copy(
            src_ref=stage.at[array, chunk, pl.ds(low, size), :],
            dst_ref=outs[array].at[pl.ds(slot_low, size), columns(source)],
            send_sem=out_send.at[array, piece, chunk],
            recv_sem=out_recv.at[array, piece, source],
            device_id={"tm": target},
            device_id_type=pl.DeviceIdType.MESH,
        )

    def own_outgoing(array, piece, chunk):
        _, low, slot_low, size = pieces[piece]
        return pltpu.make_async_copy(
            stage.at[array, chunk, pl.ds(low, size), :],
            outs[array].at[pl.ds(slot_low, size), columns(me)],
            out_local.at[array, piece],
        )

    def middle_half(array, chunk, source):
        low = pl.multiple_of(BLK + lax.rem(chunk, 2) * BLK, BLK)
        return pltpu.make_async_remote_copy(
            src_ref=stage.at[array, chunk, pl.ds(low, BLK), :],
            dst_ref=outs[array].at[pl.ds(low, BLK), columns(source)],
            send_sem=out_send.at[array, 1, chunk],
            recv_sem=out_recv.at[array, 1, source],
            device_id={"tm": chunk},
            device_id_type=pl.DeviceIdType.MESH,
        )

    def to_relay(array, odd, chunk, source_place):
        low = 0 if odd else BLK + rows
        return pltpu.make_async_remote_copy(
            src_ref=stage.at[array, chunk, pl.ds(low, BLK), :],
            dst_ref=relay_in.at[array, source_place, pl.ds(odd * BLK, BLK), :],
            send_sem=out_send.at[array, 0 if odd else 2, chunk],
            recv_sem=relay_recv.at[array, odd, source_place],
            device_id={"tm": near},
            device_id_type=pl.DeviceIdType.MESH,
        )

    def handed_on(array, place, slot_low):
        source = 2 * (1 - half) + place
        return pltpu.make_async_remote_copy(
            src_ref=relay_on.at[array, place],
            dst_ref=outs[array].at[
                pl.ds(pl.multiple_of(slot_low, 2 * BLK), 2 * BLK), columns(source)
            ],
            send_sem=on_send.at[array, place],
            recv_sem=on_recv.at[array, place],
            device_id={"tm": neighbour},
            device_id_type=pl.DeviceIdType.MESH,
        )

    def relay_kept(array, place):
        source = 2 * (1 - half) + place
        return pltpu.make_async_copy(
            relay_own.at[array, place],
            outs[array].at[
                pl.ds(pl.multiple_of((1 - up) * 2 * BLK, 2 * BLK), 2 * BLK), columns(source)
            ],
            relay_local.at[array, place],
        )

    def send_pieces(array, chunk):
        far = chunk // 2 != half
        odd = lax.rem(chunk, 2) == 1

        @pl.when(jnp.logical_not(far))
        def _():
            send_some(array, chunk, (0, 1, 2))

        @pl.when(far & jnp.logical_not(odd))
        def _():
            send_some(array, chunk, (0,))
            middle_half(array, chunk, me).start()
            to_relay(array, 0, chunk, up).start()

        @pl.when(far & odd)
        def _():
            send_some(array, chunk, (2,))
            middle_half(array, chunk, me).start()
            to_relay(array, 1, chunk, up).start()

    def send_some(array, chunk, which):
        for piece in which:
            target = lax.rem(chunk + pieces[piece][0], shards)

            @pl.when(target == me)
            def _():
                own_outgoing(array, piece, chunk).start()

            @pl.when(target != me)
            def _():
                outgoing(array, piece, chunk, target, me).start()

    def kv_outgoing(array, source, target):
        return pltpu.make_async_remote_copy(
            src_ref=stage_kv.at[array, shard_rows(target), :],
            dst_ref=kv_outs[array].at[:, columns(source)],
            send_sem=kv_send.at[array, target],
            recv_sem=kv_recv.at[array, source],
            device_id={"tm": target},
            device_id_type=pl.DeviceIdType.MESH,
        )

    def kv_own(array):
        return pltpu.make_async_copy(
            stage_kv.at[array, shard_rows(me), :],
            kv_outs[array].at[:, columns(me)],
            kv_local.at[array],
        )

    barrier = pltpu.get_barrier_semaphore()
    for step in range(1, shards):
        pl.semaphore_signal(
            barrier,
            inc=1,
            device_id={"tm": lax.rem(me + step, shards)},
            device_id_type=pl.DeviceIdType.MESH,
        )
    for array in range(4):
        own_incoming(array).start()
    pl.semaphore_wait(barrier, shards - 1)
    for array in range(4):
        for step in range(1, shards):
            incoming(array, me, lax.rem(me + step, shards)).start()

    key_sum[...] = jnp.zeros_like(key_sum)
    value_sum[...] = jnp.zeros_like(value_sum)
    for array in range(4):
        own_incoming(array).wait()
    for array in range(2):
        for step in range(1, shards):
            source = lax.rem(me + step, shards)
            incoming(array, source, me).wait_recv()

    lane_block = lax.broadcasted_iota(jnp.int32, (1, rows), 1) // BLK

    def one_chunk(turn, carry):
        pair = turn // 2
        side = (turn - 2 * pair) * (1 - 2 * lax.rem(me, 2))
        chunk = lax.rem(me + side + shards // 2 + 2 * pair + shards, shards)

        @pl.when(chunk != me)
        def _():
            incoming(2, chunk, me).wait_recv()
            incoming(3, chunk, me).wait_recv()

        own = shard_rows(chunk)
        query = held[2, own, :]
        cotan = held[3, own, :]
        peak = jnp.full((1, rows), very_low, jnp.float32)
        for b in range(blocks):
            part = pl.ds(b * BLK, BLK)
            bias = jnp.full((1, rows), very_low, jnp.float32)
            for j in range(rows // BLK):
                a = chunk * (rows // BLK) + j
                seen = act_ref[b] * act_ref[a] * mask_ref[a, b]
                level = jnp.where(seen > 0, 0.0, very_low)
                bias = jnp.where(lane_block == j, level, bias)
            tile = lax.dot_general(
                held[0, part, :], query, (((1,), (1,)), ((), ())), preferred_element_type=jnp.float32
            )
            tile = tile * scaling + bias
            scores[part, :] = tile
            peak = jnp.maximum(peak, jnp.max(tile, axis=0, keepdims=True))
        peak = jnp.maximum(peak, -1e20)
        mass = jnp.zeros((1, rows), jnp.float32)
        for b in range(blocks):
            part = pl.ds(b * BLK, BLK)
            tile = jnp.exp(scores[part, :] - peak)
            scores[part, :] = tile
            weights[part, :] = tile.astype(jnp.bfloat16)
            mass = mass + jnp.sum(tile, axis=0, keepdims=True)
        inverse = 1.0 / jnp.where(mass > 0.0, mass, 1.0)
        att_t = lax.dot_general(
            held[1], weights[...], (((0,), (0,)), ((), ())), preferred_element_type=jnp.float32
        )
        att_t = (att_t * inverse).astype(jnp.bfloat16).astype(jnp.float32)
        delta = jnp.sum(jnp.transpose(cotan.astype(jnp.float32)) * att_t, axis=0, keepdims=True)
        last = rows // BLK - 1
        to_left = cnt_ref[chunk, 0] > 0
        to_right = cnt_ref[chunk, 1] > 0

        far = chunk // 2 != half
        raw_first = to_left | (far & (lax.rem(chunk, 2) == 1))
        raw_final = to_right | (far & (lax.rem(chunk, 2) == 0))

        def stage_slots(array, result):
            result = result.astype(jnp.bfloat16)
            first, final = result[:BLK], result[last * BLK :]
            zero = jnp.zeros_like(first)
            stage[array, chunk, pl.ds(0, BLK), :] = jnp.where(raw_first, first, zero)
            stage[array, chunk, pl.ds(BLK, BLK), :] = jnp.where(to_left, zero, first)
            stage[array, chunk, pl.ds(rows, BLK), :] = jnp.where(to_right, zero, final)
            stage[array, chunk, pl.ds(rows + BLK, BLK), :] = jnp.where(raw_final, final, zero)

        stage_slots(0, jnp.transpose(att_t))
        send_pieces(0, chunk)
        for b in range(blocks):
            part = pl.ds(b * BLK, BLK)
            tile = lax.dot_general(
                held[1, part, :], cotan, (((1,), (1,)), ((), ())), preferred_element_type=jnp.float32
            )
            probs = scores[part, :] * inverse
            grad = (probs * (tile - delta)).astype(jnp.bfloat16)
            grads[part, :] = grad
            key_sum[part, :] += jnp.dot(grad, query, preferred_element_type=jnp.float32)
            value_sum[part, :] += jnp.dot(
                probs.astype(jnp.bfloat16), cotan, preferred_element_type=jnp.float32
            )
        dq_t = lax.dot_general(
            held[0], grads[...], (((0,), (0,)), ((), ())), preferred_element_type=jnp.float32
        )
        stage_slots(1, jnp.transpose(dq_t * scaling))
        send_pieces(1, chunk)
        return carry

    lax.fori_loop(0, shards, one_chunk, 0)
    stage_kv[0] = (key_sum[...] * scaling).astype(jnp.bfloat16)
    stage_kv[1] = value_sum[...].astype(jnp.bfloat16)
    for array in range(2):
        for step in range(1, shards):
            kv_outgoing(array, me, lax.rem(me + step, shards)).start()
        kv_own(array).start()

    @pl.when(is_near)
    def _():
        lower = me - up
        right = cnt_ref[lower, 1]
        left = cnt_ref[lower + 1, 0]
        for array in range(2):
            for place in range(2):
                to_relay(array, 0, lower, place).wait_recv()
                to_relay(array, 1, lower + 1, place).wait_recv()
                for b, keep in ((0, right == up), (1, left == 1 - up)):
                    part = pl.ds(b * BLK, BLK)
                    block = relay_in[array, place, part, :]
                    zero = jnp.zeros_like(block)
                    relay_own[array, place, part, :] = jnp.where(keep, block, zero)
                    relay_on[array, place, part, :] = jnp.where(keep, zero, block)
                handed_on(array, place, up * 2 * BLK).start()
                relay_kept(array, place).start()
        for array in range(2):
            for place in range(2):
                handed_on(array, place, up * 2 * BLK).wait_send()
                relay_kept(array, place).wait()

    @pl.when(jnp.logical_not(is_near))
    def _():
        for array in range(2):
            for place in range(2):
                handed_on(array, place, (1 - up) * 2 * BLK).wait_recv()

    for step in range(1, shards):
        peer = lax.rem(me + step, shards)
        for array in range(4):
            incoming(array, me, peer).wait_send()
        for array in range(2):
            kv_outgoing(array, me, peer).wait_send()
            kv_outgoing(array, peer, me).wait_recv()

        @pl.when(peer // 2 == half)
        def _():
            for array in range(2):
                for piece in range(3):
                    outgoing(array, piece, 0, me, peer).wait_recv()
                outgoing(array, 1, peer, peer, me).wait_send()

        @pl.when(peer // 2 != half)
        def _():
            for array in range(2):
                middle_half(array, me, peer).wait_recv()
                middle_half(array, peer, me).wait_send()

            @pl.when(up == 0)
            def _():
                for array in range(2):
                    outgoing(array, 2, 0, me, peer).wait_recv()

            @pl.when(up == 1)
            def _():
                for array in range(2):
                    outgoing(array, 0, 0, me, peer).wait_recv()

    for step in range(shards):
        chunk = lax.rem(me + step, shards)
        for piece in (0, 2):
            if (step + pieces[piece][0]) % shards != 0:
                for array in range(2):
                    outgoing(array, piece, chunk, near, me).wait_send()
    for array in range(2):
        kv_own(array).wait()
        for piece in range(3):
            own_outgoing(array, piece, 0).wait()


def exchanged_heads(queries, key_rows, value_rows, cotangent, block_active, send_counts, block_mask):
    shards = lax.axis_size("tm")
    rows, width = queries.shape
    total = shards * rows
    slot_rows = rows + 2 * CAP * BLK
    anywhere = pl.BlockSpec(memory_space=pl.ANY)
    scalars = pl.BlockSpec(memory_space=pltpu.SMEM)
    return pl.pallas_call(
        functools.partial(head_kernel, shards, rows),
        out_shape=(
            jax.ShapeDtypeStruct((slot_rows, width), jnp.bfloat16),
            jax.ShapeDtypeStruct((slot_rows, width), jnp.bfloat16),
            jax.ShapeDtypeStruct((rows, width), jnp.bfloat16),
            jax.ShapeDtypeStruct((rows, width), jnp.bfloat16),
        ),
        in_specs=[scalars] * 3 + [pl.BlockSpec(memory_space=pltpu.HBM)] * 4,
        out_specs=(anywhere,) * 4,
        scratch_shapes=[
            pltpu.VMEM((4, total, HD), jnp.bfloat16),
            pltpu.VMEM((total, rows), jnp.float32),
            pltpu.VMEM((total, rows), jnp.bfloat16),
            pltpu.VMEM((total, rows), jnp.bfloat16),
            pltpu.VMEM((total, HD), jnp.float32),
            pltpu.VMEM((total, HD), jnp.float32),
            pltpu.VMEM((2, shards, slot_rows, HD), jnp.bfloat16),
            pltpu.VMEM((2, total, HD), jnp.bfloat16),
            pltpu.SemaphoreType.DMA((4, shards)),
            pltpu.SemaphoreType.DMA((4, shards)),
            pltpu.SemaphoreType.DMA((2, 3, shards)),
            pltpu.SemaphoreType.DMA((2, 3, shards)),
            pltpu.SemaphoreType.DMA((2, shards)),
            pltpu.SemaphoreType.DMA((2, shards)),
            pltpu.SemaphoreType.DMA((4,)),
            pltpu.SemaphoreType.DMA((2, 3)),
            pltpu.SemaphoreType.DMA((2,)),
            pltpu.VMEM((2, 2, 2 * BLK, HD), jnp.bfloat16),
            pltpu.VMEM((2, 2, 2 * BLK, HD), jnp.bfloat16),
            pltpu.VMEM((2, 2, 2 * BLK, HD), jnp.bfloat16),
            pltpu.SemaphoreType.DMA((2, 2, 2)),
            pltpu.SemaphoreType.DMA((2, 2)),
            pltpu.SemaphoreType.DMA((2, 2)),
            pltpu.SemaphoreType.DMA((2, 2)),
        ],
        compiler_params=pltpu.CompilerParams(
            collective_id=0, has_side_effects=True, vmem_limit_bytes=63 * 1024 * 1024
        ),
    )(block_active, send_counts, block_mask, queries, key_rows, value_rows, cotangent)


def routed(queries, key_rows, value_rows, cotangent, block_active, send_counts, block_mask):
    shards = lax.axis_size("tm")
    rows, width = queries.shape
    args = (queries, key_rows, value_rows, cotangent, block_active, send_counts, block_mask)
    if shards == 4 and width == shards * HD and rows == 2 * BLK:
        return exchanged_heads(*args)
    return body(*args)


def solution(mesh):
    in_specs = (
        P(("groups", "tm"), ("head", "mp")),
        P(("groups", "tm"), ("head", "mp")),
        P(("groups", "tm"), ("head", "mp")),
        P(("groups", "tm"), ("head", "mp")),
        P("groups"),
        P("groups", None),
        P("groups", None),
    )
    out_specs = (
        P(("groups", "tm"), ("head", "mp")),
        P(("groups", "tm"), ("head", "mp")),
        P(("groups", "tm"), ("head", "mp")),
        P(("groups", "tm"), ("head", "mp")),
    )
    return jax.shard_map(
        routed, mesh=mesh, in_specs=in_specs, out_specs=out_specs, check_vma=False)
```

```python
import functools
import math

import jax
import jax.numpy as jnp
from jax import lax
from jax.experimental import pallas as pl
from jax.experimental.pallas import tpu as pltpu
from jax.sharding import PartitionSpec as P

HD = 128
BLK = 128
CAP = 1


very_low = -1e30


def extended_2(shard, sides, width):
    for axis, dim in sides:
        peers, length = (lax.axis_size(axis), shard.shape[dim])
        up = [(i, (i + 1) % peers) for i in range(peers)]
        down = [(j, i) for i, j in up]
        last = lax.slice_in_dim(shard, length - width, length, axis=dim)
        first = lax.slice_in_dim(shard, 0, width, axis=dim)
        before = lax.ppermute(last, axis, up)
        after = lax.ppermute(first, axis, down)
        shard = jnp.concatenate([before, shard, after], axis=dim)
    return shard


def pick(table, positions, extent):
    matches = positions[:, None] == jnp.arange(extent, dtype=jnp.int32)[None, :]
    return jnp.sum(jnp.where(matches, table[None, :], 0), axis=1)


def slot_layout(block_active, send_counts, block_mask, shards, own_blocks, capacity):
    slot_count = own_blocks + 2 * capacity
    all_blocks = shards * own_blocks
    places = jnp.arange(shards * slot_count, dtype=jnp.int32)
    device = places // slot_count
    slot_index = places % slot_count
    before = (device + shards - 1) % shards
    following = (device + 1) % shards
    to_left = send_counts[:, 0]
    to_right = send_counts[:, 1]
    from_before = slot_index < capacity
    from_after = slot_index >= capacity + own_blocks
    owner_shard = jnp.where(from_before, before, jnp.where(from_after, following, device))
    local_block = jnp.where(
        from_before,
        own_blocks - capacity + slot_index,
        jnp.where(from_after, slot_index - capacity - own_blocks, slot_index - capacity),
    )
    middle_ok = (local_block >= pick(to_left, device, shards)) & (
        local_block < own_blocks - pick(to_right, device, shards)
    )
    holds_record = jnp.where(
        from_before,
        slot_index >= capacity - pick(to_right, before, shards),
        jnp.where(from_after, local_block < pick(to_left, following, shards), middle_ok),
    )
    anchor = owner_shard * own_blocks + local_block
    onehot = (anchor[:, None] == jnp.arange(all_blocks, dtype=jnp.int32)[None, :]).astype(
        jnp.float32
    )
    seeing = (block_mask * block_active[None, :]).astype(jnp.float32)
    block_rows = jnp.dot(onehot, seeing, precision=lax.Precision.HIGHEST)
    active = jnp.dot(onehot, block_active.astype(jnp.float32), precision=lax.Precision.HIGHEST)
    present = jnp.where(holds_record, active, 0.0)
    return (anchor, block_rows * present[:, None], present)


def block_hot(offset, length, extent):
    blocks = (offset + jnp.arange(length, dtype=jnp.int32)) // BLK
    return (blocks[:, None] == jnp.arange(extent, dtype=jnp.int32)[None, :]).astype(jnp.bfloat16)


def sweep(update, running, pieces, offset):
    row_count = pieces[0].shape[0]
    step_rows = math.gcd(row_count, 1024)
    if step_rows == row_count:
        return update(running, pieces, offset)

    def one_turn(turn_index, carried):
        part_pieces = tuple(
            (
                lax.dynamic_slice_in_dim(member, turn_index * step_rows, step_rows, 0)
                for member in pieces
            )
        )
        return update(carried, part_pieces, offset + turn_index * step_rows)

    return lax.fori_loop(0, row_count // step_rows, one_turn, running)


def body(queries, key_rows, value_rows, cotangent, block_active, send_counts, block_mask):
    shards = lax.axis_size("tm")
    shard_index = lax.axis_index("tm")
    model_width = queries.shape[1]
    head_count = model_width // HD
    own_rows = queries.shape[0]
    own_blocks = own_rows // BLK
    all_blocks = block_active.shape[0]
    slot_count = own_blocks + 2 * CAP
    slot_rows = slot_count * BLK
    scaling = 1.0 / math.sqrt(HD)
    anchor, table, present = slot_layout(
        block_active, send_counts, block_mask, shards, own_blocks, CAP
    )
    records = jnp.concatenate([queries, cotangent], axis=1)
    extended = extended_2(records, (("tm", 0),), CAP * BLK)
    query_slots = extended[:, :model_width].reshape(slot_rows, head_count, HD)
    cotan_slots = extended[:, model_width:].reshape(slot_rows, head_count, HD)
    my_table = lax.dynamic_slice_in_dim(table, shard_index * slot_count, slot_count, 0)
    query_table = jnp.repeat(my_table, BLK, axis=0).astype(jnp.bfloat16)
    live = (
        jnp.repeat(lax.dynamic_slice_in_dim(present, shard_index * slot_count, slot_count, 0), BLK)
        > 0.5
    )
    keys_all, values_all = (
        lax.all_gather(key_rows, "tm", axis=0, tiled=True),
        lax.all_gather(value_rows, "tm", axis=0, tiled=True),
    )

    def own_scores(key_piece, offset):
        allowed = (
            lax.dot_general(
                query_table,
                block_hot(offset, key_piece.shape[0], all_blocks),
                (((1,), (1,)), ((), ())),
                preferred_element_type=jnp.float32,
            )[:, None, :]
            > 0.5
        )
        scores = (
            jnp.einsum("qhd,khd->qhk", query_slots, key_piece, preferred_element_type=jnp.float32)
            * scaling
        )
        return (allowed, scores)

    def forward(running, pieces, offset):
        peak, masses, accum = running
        key_piece = pieces[0].reshape(-1, head_count, HD)
        value_piece = pieces[1].reshape(-1, head_count, HD)
        allowed, scores = own_scores(key_piece, offset)
        new_peak = jnp.maximum(peak, jnp.max(jnp.where(allowed, scores, very_low), axis=2))
        weights = jnp.where(
            allowed, jnp.exp(jnp.where(allowed, scores - new_peak[:, :, None], 0.0)), 0.0
        )
        shrink = jnp.exp(peak - new_peak)
        masses = masses * shrink + jnp.sum(weights, axis=2)
        accum = accum * shrink[:, :, None] + jnp.einsum(
            "qhk,khd->qhd",
            weights.astype(jnp.bfloat16),
            value_piece,
            preferred_element_type=jnp.float32,
        )
        return (new_peak, masses, accum)

    initial = (
        jnp.full((slot_rows, head_count), very_low, jnp.float32),
        jnp.zeros((slot_rows, head_count), jnp.float32),
        jnp.zeros((slot_rows, head_count, HD), jnp.float32),
    )
    peak, masses, accum = sweep(forward, initial, (keys_all, values_all), 0)
    denominator = jnp.where(live[:, None], masses, 1.0)
    attended = (accum / denominator[:, :, None]).astype(jnp.bfloat16)
    log_norm = peak + jnp.log(denominator)
    deltas = jnp.sum(cotan_slots.astype(jnp.float32) * attended.astype(jnp.float32), axis=2)

    def own_gradients(key_piece, value_piece, offset):
        allowed, scores = own_scores(key_piece, offset)
        probs = jnp.where(
            allowed, jnp.exp(jnp.where(allowed, scores - log_norm[:, :, None], 0.0)), 0.0
        )
        weight_grad = jnp.einsum(
            "qhd,khd->qhk", cotan_slots, value_piece, preferred_element_type=jnp.float32
        )
        return (probs, (probs * (weight_grad - deltas[:, :, None])).astype(jnp.bfloat16))

    zero_query = jnp.zeros((slot_rows, head_count, HD), jnp.float32)

    def query_pass(query_sum, pieces, offset):
        key_piece = pieces[0].reshape(-1, head_count, HD)
        value_piece = pieces[1].reshape(-1, head_count, HD)
        probs, score_grad = own_gradients(key_piece, value_piece, offset)
        return query_sum + jnp.einsum(
            "qhk,khd->qhd", score_grad, key_piece, preferred_element_type=jnp.float32
        )

    query_sum = sweep(query_pass, zero_query, (keys_all, values_all), 0)
    own_keys = key_rows.reshape(own_rows, head_count, HD)
    own_values = value_rows.reshape(own_rows, head_count, HD)
    own_hot = block_hot(shard_index * own_rows, own_rows, all_blocks)
    slot_table = table.astype(jnp.bfloat16)
    logsum_all, delta_all = (
        lax.all_gather(log_norm, "tm", axis=0, tiled=True),
        lax.all_gather(deltas, "tm", axis=0, tiled=True),
    )

    def owner_work(running, pieces, offset):
        key_sum, value_sum = running
        query_piece, cotan_piece = pieces
        row_count = query_piece.shape[0]
        logsum_piece = lax.dynamic_slice_in_dim(logsum_all, offset, row_count, 0)
        delta_piece = lax.dynamic_slice_in_dim(delta_all, offset, row_count, 0)
        piece_table = jnp.dot(
            block_hot(offset, row_count, shards * slot_count),
            slot_table,
            preferred_element_type=jnp.float32,
        ).astype(jnp.bfloat16)
        allowed = (
            lax.dot_general(
                piece_table, own_hot, (((1,), (1,)), ((), ())), preferred_element_type=jnp.float32
            )[:, None, :]
            > 0.5
        )
        query_three = query_piece.reshape(row_count, head_count, HD)
        cotan_three = cotan_piece.reshape(row_count, head_count, HD)
        scores = (
            jnp.einsum("qhd,khd->qhk", query_three, own_keys, preferred_element_type=jnp.float32)
            * scaling
        )
        probs = jnp.where(
            allowed, jnp.exp(jnp.where(allowed, scores - logsum_piece[:, :, None], 0.0)), 0.0
        )
        weight_grad = jnp.einsum(
            "qhd,khd->qhk", cotan_three, own_values, preferred_element_type=jnp.float32
        )
        score_grad = (probs * (weight_grad - delta_piece[:, :, None])).astype(jnp.bfloat16)
        key_sum = key_sum + jnp.einsum(
            "qhk,qhd->khd", score_grad, query_three, preferred_element_type=jnp.float32
        )
        value_sum = value_sum + jnp.einsum(
            "qhk,qhd->khd",
            probs.astype(jnp.bfloat16),
            cotan_three,
            preferred_element_type=jnp.float32,
        )
        return (key_sum, value_sum)

    key_zero = jnp.zeros((own_rows, head_count, HD), jnp.float32)
    key_sum, value_sum = sweep(
        owner_work,
        (key_zero, key_zero),
        (
            lax.all_gather(query_slots.reshape(slot_rows, model_width), "tm", axis=0, tiled=True),
            lax.all_gather(cotan_slots.reshape(slot_rows, model_width), "tm", axis=0, tiled=True),
        ),
        jnp.int32(0),
    )
    key_grad = (key_sum * scaling).astype(jnp.bfloat16).reshape(own_rows, model_width)
    value_grad = value_sum.astype(jnp.bfloat16).reshape(own_rows, model_width)
    query_grad = (query_sum * scaling).astype(jnp.bfloat16).reshape(slot_rows, model_width)
    return (attended.reshape(slot_rows, model_width), query_grad, key_grad, value_grad)


def head_kernel(
    shards,
    rows,
    act_ref,
    cnt_ref,
    mask_ref,
    q_hbm,
    k_hbm,
    v_hbm,
    g_hbm,
    att_hbm,
    dq_hbm,
    dk_hbm,
    dv_hbm,
    held,
    scores,
    weights,
    grads,
    key_sum,
    value_sum,
    stage,
    stage_kv,
    in_send,
    in_recv,
    out_send,
    out_recv,
    kv_send,
    kv_recv,
    in_local,
    out_local,
    kv_local,
    relay_in,
    relay_own,
    relay_on,
    relay_recv,
    on_send,
    on_recv,
    relay_local,
):
    me = lax.axis_index("tm")
    half = me // 2
    up = lax.rem(me, 2)
    near = 2 - half
    neighbour = me + 1 - 2 * up
    is_near = me == 1 + half
    total = shards * rows
    blocks = total // BLK
    scaling = 1.0 / math.sqrt(HD)
    sources = (k_hbm, v_hbm, q_hbm, g_hbm)
    outs = (att_hbm, dq_hbm)
    kv_outs = (dk_hbm, dv_hbm)

    def columns(index):
        return pl.ds(pl.multiple_of(index * HD, HD), HD)

    def shard_rows(index):
        return pl.ds(pl.multiple_of(index * rows, rows), rows)

    def incoming(array, source, target):
        return pltpu.make_async_remote_copy(
            src_ref=sources[array].at[:, columns(target)],
            dst_ref=held.at[array, shard_rows(source), :],
            send_sem=in_send.at[array, target],
            recv_sem=in_recv.at[array, source],
            device_id={"tm": target},
            device_id_type=pl.DeviceIdType.MESH,
        )

    def own_incoming(array):
        return pltpu.make_async_copy(
            sources[array].at[:, columns(me)],
            held.at[array, shard_rows(me), :],
            in_local.at[array],
        )

    pieces = (
        (shards - 1, 0, (rows // BLK + 1) * BLK, BLK),
        (0, BLK, BLK, rows),
        (1, BLK + rows, 0, BLK),
    )

    def outgoing(array, piece, chunk, target, source):
        _, low, slot_low, size = pieces[piece]
        return pltpu.make_async_remote_copy(
            src_ref=stage.at[array, chunk, pl.ds(low, size), :],
            dst_ref=outs[array].at[pl.ds(slot_low, size), columns(source)],
            send_sem=out_send.at[array, piece, chunk],
            recv_sem=out_recv.at[array, piece, source],
            device_id={"tm": target},
            device_id_type=pl.DeviceIdType.MESH,
        )

    def own_outgoing(array, piece, chunk):
        _, low, slot_low, size = pieces[piece]
        return pltpu.make_async_copy(
            stage.at[array, chunk, pl.ds(low, size), :],
            outs[array].at[pl.ds(slot_low, size), columns(me)],
            out_local.at[array, piece],
        )

    def middle_half(array, chunk, source):
        low = pl.multiple_of(BLK + lax.rem(chunk, 2) * BLK, BLK)
        return pltpu.make_async_remote_copy(
            src_ref=stage.at[array, chunk, pl.ds(low, BLK), :],
            dst_ref=outs[array].at[pl.ds(low, BLK), columns(source)],
            send_sem=out_send.at[array, 1, chunk],
            recv_sem=out_recv.at[array, 1, source],
            device_id={"tm": chunk},
            device_id_type=pl.DeviceIdType.MESH,
        )

    def to_relay(array, odd, chunk, source_place):
        low = 0 if odd else BLK + rows
        return pltpu.make_async_remote_copy(
            src_ref=stage.at[array, chunk, pl.ds(low, BLK), :],
            dst_ref=relay_in.at[array, source_place, pl.ds(odd * BLK, BLK), :],
            send_sem=out_send.at[array, 0 if odd else 2, chunk],
            recv_sem=relay_recv.at[array, odd, source_place],
            device_id={"tm": near},
            device_id_type=pl.DeviceIdType.MESH,
        )

    def handed_on(array, place, slot_low):
        source = 2 * (1 - half) + place
        return pltpu.make_async_remote_copy(
            src_ref=relay_on.at[array, place],
            dst_ref=outs[array].at[
                pl.ds(pl.multiple_of(slot_low, 2 * BLK), 2 * BLK), columns(source)
            ],
            send_sem=on_send.at[array, place],
            recv_sem=on_recv.at[array, place],
            device_id={"tm": neighbour},
            device_id_type=pl.DeviceIdType.MESH,
        )

    def relay_kept(array, place):
        source = 2 * (1 - half) + place
        return pltpu.make_async_copy(
            relay_own.at[array, place],
            outs[array].at[
                pl.ds(pl.multiple_of((1 - up) * 2 * BLK, 2 * BLK), 2 * BLK), columns(source)
            ],
            relay_local.at[array, place],
        )

    def send_pieces(array, chunk):
        far = chunk // 2 != half
        odd = lax.rem(chunk, 2) == 1

        @pl.when(jnp.logical_not(far))
        def _():
            send_some(array, chunk, (0, 1, 2))

        @pl.when(far & jnp.logical_not(odd))
        def _():
            send_some(array, chunk, (0,))
            middle_half(array, chunk, me).start()
            to_relay(array, 0, chunk, up).start()

        @pl.when(far & odd)
        def _():
            send_some(array, chunk, (2,))
            middle_half(array, chunk, me).start()
            to_relay(array, 1, chunk, up).start()

    def send_some(array, chunk, which):
        for piece in which:
            target = lax.rem(chunk + pieces[piece][0], shards)

            @pl.when(target == me)
            def _():
                own_outgoing(array, piece, chunk).start()

            @pl.when(target != me)
            def _():
                outgoing(array, piece, chunk, target, me).start()

    def kv_outgoing(array, source, target):
        return pltpu.make_async_remote_copy(
            src_ref=stage_kv.at[array, shard_rows(target), :],
            dst_ref=kv_outs[array].at[:, columns(source)],
            send_sem=kv_send.at[array, target],
            recv_sem=kv_recv.at[array, source],
            device_id={"tm": target},
            device_id_type=pl.DeviceIdType.MESH,
        )

    def kv_own(array):
        return pltpu.make_async_copy(
            stage_kv.at[array, shard_rows(me), :],
            kv_outs[array].at[:, columns(me)],
            kv_local.at[array],
        )

    barrier = pltpu.get_barrier_semaphore()
    for step in range(1, shards):
        pl.semaphore_signal(
            barrier,
            inc=1,
            device_id={"tm": lax.rem(me + step, shards)},
            device_id_type=pl.DeviceIdType.MESH,
        )
    for array in range(4):
        own_incoming(array).start()
    pl.semaphore_wait(barrier, shards - 1)
    for array in range(4):
        for step in range(1, shards):
            incoming(array, me, lax.rem(me + step, shards)).start()

    key_sum[...] = jnp.zeros_like(key_sum)
    value_sum[...] = jnp.zeros_like(value_sum)
    for array in range(4):
        own_incoming(array).wait()
    for array in range(2):
        for step in range(1, shards):
            source = lax.rem(me + step, shards)
            incoming(array, source, me).wait_recv()

    lane_block = lax.broadcasted_iota(jnp.int32, (1, rows), 1) // BLK

    def one_chunk(turn, carry):
        pair = turn // 2
        side = (turn - 2 * pair) * (1 - 2 * lax.rem(me, 2))
        chunk = lax.rem(me + side + shards // 2 + 2 * pair + shards, shards)

        @pl.when(chunk != me)
        def _():
            incoming(2, chunk, me).wait_recv()
            incoming(3, chunk, me).wait_recv()

        own = shard_rows(chunk)
        query = held[2, own, :]
        cotan = held[3, own, :]
        peak = jnp.full((1, rows), very_low, jnp.float32)
        for b in range(blocks):
            part = pl.ds(b * BLK, BLK)
            bias = jnp.full((1, rows), very_low, jnp.float32)
            for j in range(rows // BLK):
                a = chunk * (rows // BLK) + j
                seen = act_ref[b] * act_ref[a] * mask_ref[a, b]
                level = jnp.where(seen > 0, 0.0, very_low)
                bias = jnp.where(lane_block == j, level, bias)
            tile = lax.dot_general(
                held[0, part, :], query, (((1,), (1,)), ((), ())), preferred_element_type=jnp.float32
            )
            tile = tile * scaling + bias
            scores[part, :] = tile
            peak = jnp.maximum(peak, jnp.max(tile, axis=0, keepdims=True))
        peak = jnp.maximum(peak, -1e20)
        mass = jnp.zeros((1, rows), jnp.float32)
        for b in range(blocks):
            part = pl.ds(b * BLK, BLK)
            tile = jnp.exp(scores[part, :] - peak)
            scores[part, :] = tile
            weights[part, :] = tile.astype(jnp.bfloat16)
            mass = mass + jnp.sum(tile, axis=0, keepdims=True)
        inverse = 1.0 / jnp.where(mass > 0.0, mass, 1.0)
        att_t = lax.dot_general(
            held[1], weights[...], (((0,), (0,)), ((), ())), preferred_element_type=jnp.float32
        )
        att_t = (att_t * inverse).astype(jnp.bfloat16).astype(jnp.float32)
        delta = jnp.sum(jnp.transpose(cotan.astype(jnp.float32)) * att_t, axis=0, keepdims=True)
        last = rows // BLK - 1
        to_left = cnt_ref[0, chunk] > 0
        to_right = cnt_ref[1, chunk] > 0

        far = chunk // 2 != half
        raw_first = to_left | (far & (lax.rem(chunk, 2) == 1))
        raw_final = to_right | (far & (lax.rem(chunk, 2) == 0))

        def stage_slots(array, result):
            result = result.astype(jnp.bfloat16)
            first, final = result[:BLK], result[last * BLK :]
            zero = jnp.zeros_like(first)
            stage[array, chunk, pl.ds(0, BLK), :] = jnp.where(raw_first, first, zero)
            stage[array, chunk, pl.ds(BLK, BLK), :] = jnp.where(to_left, zero, first)
            stage[array, chunk, pl.ds(rows, BLK), :] = jnp.where(to_right, zero, final)
            stage[array, chunk, pl.ds(rows + BLK, BLK), :] = jnp.where(raw_final, final, zero)

        stage_slots(0, jnp.transpose(att_t))
        send_pieces(0, chunk)
        for b in range(blocks):
            part = pl.ds(b * BLK, BLK)
            tile = lax.dot_general(
                held[1, part, :], cotan, (((1,), (1,)), ((), ())), preferred_element_type=jnp.float32
            )
            probs = scores[part, :] * inverse
            grad = (probs * (tile - delta)).astype(jnp.bfloat16)
            grads[part, :] = grad
            key_sum[part, :] += jnp.dot(grad, query, preferred_element_type=jnp.float32)
            value_sum[part, :] += jnp.dot(
                probs.astype(jnp.bfloat16), cotan, preferred_element_type=jnp.float32
            )
        dq_t = lax.dot_general(
            held[0], grads[...], (((0,), (0,)), ((), ())), preferred_element_type=jnp.float32
        )
        stage_slots(1, jnp.transpose(dq_t * scaling))
        send_pieces(1, chunk)
        return carry

    lax.fori_loop(0, shards, one_chunk, 0)
    stage_kv[0] = (key_sum[...] * scaling).astype(jnp.bfloat16)
    stage_kv[1] = value_sum[...].astype(jnp.bfloat16)
    for array in range(2):
        for step in range(1, shards):
            kv_outgoing(array, me, lax.rem(me + step, shards)).start()
        kv_own(array).start()

    @pl.when(is_near)
    def _():
        lower = me - up
        right = cnt_ref[1, lower]
        left = cnt_ref[0, lower + 1]
        for array in range(2):
            for place in range(2):
                to_relay(array, 0, lower, place).wait_recv()
                to_relay(array, 1, lower + 1, place).wait_recv()
                for b, keep in ((0, right == up), (1, left == 1 - up)):
                    part = pl.ds(b * BLK, BLK)
                    block = relay_in[array, place, part, :]
                    zero = jnp.zeros_like(block)
                    relay_own[array, place, part, :] = jnp.where(keep, block, zero)
                    relay_on[array, place, part, :] = jnp.where(keep, zero, block)
                handed_on(array, place, up * 2 * BLK).start()
                relay_kept(array, place).start()
        for array in range(2):
            for place in range(2):
                handed_on(array, place, up * 2 * BLK).wait_send()
                relay_kept(array, place).wait()

    @pl.when(jnp.logical_not(is_near))
    def _():
        for array in range(2):
            for place in range(2):
                handed_on(array, place, (1 - up) * 2 * BLK).wait_recv()

    for step in range(1, shards):
        peer = lax.rem(me + step, shards)
        for array in range(4):
            incoming(array, me, peer).wait_send()
        for array in range(2):
            kv_outgoing(array, me, peer).wait_send()
            kv_outgoing(array, peer, me).wait_recv()

        @pl.when(peer // 2 == half)
        def _():
            for array in range(2):
                for piece in range(3):
                    outgoing(array, piece, 0, me, peer).wait_recv()
                outgoing(array, 1, peer, peer, me).wait_send()

        @pl.when(peer // 2 != half)
        def _():
            for array in range(2):
                middle_half(array, me, peer).wait_recv()
                middle_half(array, peer, me).wait_send()

            @pl.when(up == 0)
            def _():
                for array in range(2):
                    outgoing(array, 2, 0, me, peer).wait_recv()

            @pl.when(up == 1)
            def _():
                for array in range(2):
                    outgoing(array, 0, 0, me, peer).wait_recv()

    for step in range(shards):
        chunk = lax.rem(me + step, shards)
        for piece in (0, 2):
            if (step + pieces[piece][0]) % shards != 0:
                for array in range(2):
                    outgoing(array, piece, chunk, near, me).wait_send()
    for array in range(2):
        kv_own(array).wait()
        for piece in range(3):
            own_outgoing(array, piece, 0).wait()


def exchanged_heads(queries, key_rows, value_rows, cotangent, block_active, send_counts, block_mask):
    shards = lax.axis_size("tm")
    rows, width = queries.shape
    total = shards * rows
    slot_rows = rows + 2 * CAP * BLK
    anywhere = pl.BlockSpec(memory_space=pl.ANY)
    scalars = pl.BlockSpec(memory_space=pltpu.SMEM)
    return pl.pallas_call(
        functools.partial(head_kernel, shards, rows),
        out_shape=(
            jax.ShapeDtypeStruct((slot_rows, width), jnp.bfloat16),
            jax.ShapeDtypeStruct((slot_rows, width), jnp.bfloat16),
            jax.ShapeDtypeStruct((rows, width), jnp.bfloat16),
            jax.ShapeDtypeStruct((rows, width), jnp.bfloat16),
        ),
        in_specs=[scalars] * 3 + [pl.BlockSpec(memory_space=pltpu.HBM)] * 4,
        out_specs=(anywhere,) * 4,
        scratch_shapes=[
            pltpu.VMEM((4, total, HD), jnp.bfloat16),
            pltpu.VMEM((total, rows), jnp.float32),
            pltpu.VMEM((total, rows), jnp.bfloat16),
            pltpu.VMEM((total, rows), jnp.bfloat16),
            pltpu.VMEM((total, HD), jnp.float32),
            pltpu.VMEM((total, HD), jnp.float32),
            pltpu.VMEM((2, shards, slot_rows, HD), jnp.bfloat16),
            pltpu.VMEM((2, total, HD), jnp.bfloat16),
            pltpu.SemaphoreType.DMA((4, shards)),
            pltpu.SemaphoreType.DMA((4, shards)),
            pltpu.SemaphoreType.DMA((2, 3, shards)),
            pltpu.SemaphoreType.DMA((2, 3, shards)),
            pltpu.SemaphoreType.DMA((2, shards)),
            pltpu.SemaphoreType.DMA((2, shards)),
            pltpu.SemaphoreType.DMA((4,)),
            pltpu.SemaphoreType.DMA((2, 3)),
            pltpu.SemaphoreType.DMA((2,)),
            pltpu.VMEM((2, 2, 2 * BLK, HD), jnp.bfloat16),
            pltpu.VMEM((2, 2, 2 * BLK, HD), jnp.bfloat16),
            pltpu.VMEM((2, 2, 2 * BLK, HD), jnp.bfloat16),
            pltpu.SemaphoreType.DMA((2, 2, 2)),
            pltpu.SemaphoreType.DMA((2, 2)),
            pltpu.SemaphoreType.DMA((2, 2)),
            pltpu.SemaphoreType.DMA((2, 2)),
        ],
        compiler_params=pltpu.CompilerParams(
            collective_id=0, has_side_effects=True, vmem_limit_bytes=63 * 1024 * 1024
        ),
    )(block_active, send_counts.T, block_mask, queries, key_rows, value_rows, cotangent)


def routed(queries, key_rows, value_rows, cotangent, block_active, send_counts, block_mask):
    shards = lax.axis_size("tm")
    rows, width = queries.shape
    args = (queries, key_rows, value_rows, cotangent, block_active, send_counts, block_mask)
    if shards == 4 and width == shards * HD and rows == 2 * BLK:
        return exchanged_heads(*args)
    return body(*args)


def solution(mesh):
    in_specs = (
        P(("groups", "tm"), ("head", "mp")),
        P(("groups", "tm"), ("head", "mp")),
        P(("groups", "tm"), ("head", "mp")),
        P(("groups", "tm"), ("head", "mp")),
        P("groups"),
        P("groups", None),
        P("groups", None),
    )
    out_specs = (
        P(("groups", "tm"), ("head", "mp")),
        P(("groups", "tm"), ("head", "mp")),
        P(("groups", "tm"), ("head", "mp")),
        P(("groups", "tm"), ("head", "mp")),
    )
    return jax.shard_map(
        routed, mesh=mesh, in_specs=in_specs, out_specs=out_specs, check_vma=False)
```

```python
import functools
import math

import jax
import jax.numpy as jnp
from jax import lax
from jax.experimental import pallas as pl
from jax.experimental.pallas import tpu as pltpu
from jax.sharding import PartitionSpec as P

HD = 128
BLK = 128
CAP = 1


very_low = -1e30


def extended_2(shard, sides, width):
    for axis, dim in sides:
        peers, length = (lax.axis_size(axis), shard.shape[dim])
        up = [(i, (i + 1) % peers) for i in range(peers)]
        down = [(j, i) for i, j in up]
        last = lax.slice_in_dim(shard, length - width, length, axis=dim)
        first = lax.slice_in_dim(shard, 0, width, axis=dim)
        before = lax.ppermute(last, axis, up)
        after = lax.ppermute(first, axis, down)
        shard = jnp.concatenate([before, shard, after], axis=dim)
    return shard


def pick(table, positions, extent):
    matches = positions[:, None] == jnp.arange(extent, dtype=jnp.int32)[None, :]
    return jnp.sum(jnp.where(matches, table[None, :], 0), axis=1)


def slot_layout(block_active, send_counts, block_mask, shards, own_blocks, capacity):
    slot_count = own_blocks + 2 * capacity
    all_blocks = shards * own_blocks
    places = jnp.arange(shards * slot_count, dtype=jnp.int32)
    device = places // slot_count
    slot_index = places % slot_count
    before = (device + shards - 1) % shards
    following = (device + 1) % shards
    to_left = send_counts[:, 0]
    to_right = send_counts[:, 1]
    from_before = slot_index < capacity
    from_after = slot_index >= capacity + own_blocks
    owner_shard = jnp.where(from_before, before, jnp.where(from_after, following, device))
    local_block = jnp.where(
        from_before,
        own_blocks - capacity + slot_index,
        jnp.where(from_after, slot_index - capacity - own_blocks, slot_index - capacity),
    )
    middle_ok = (local_block >= pick(to_left, device, shards)) & (
        local_block < own_blocks - pick(to_right, device, shards)
    )
    holds_record = jnp.where(
        from_before,
        slot_index >= capacity - pick(to_right, before, shards),
        jnp.where(from_after, local_block < pick(to_left, following, shards), middle_ok),
    )
    anchor = owner_shard * own_blocks + local_block
    onehot = (anchor[:, None] == jnp.arange(all_blocks, dtype=jnp.int32)[None, :]).astype(
        jnp.float32
    )
    seeing = (block_mask * block_active[None, :]).astype(jnp.float32)
    block_rows = jnp.dot(onehot, seeing, precision=lax.Precision.HIGHEST)
    active = jnp.dot(onehot, block_active.astype(jnp.float32), precision=lax.Precision.HIGHEST)
    present = jnp.where(holds_record, active, 0.0)
    return (anchor, block_rows * present[:, None], present)


def block_hot(offset, length, extent):
    blocks = (offset + jnp.arange(length, dtype=jnp.int32)) // BLK
    return (blocks[:, None] == jnp.arange(extent, dtype=jnp.int32)[None, :]).astype(jnp.bfloat16)


def sweep(update, running, pieces, offset):
    row_count = pieces[0].shape[0]
    step_rows = math.gcd(row_count, 1024)
    if step_rows == row_count:
        return update(running, pieces, offset)

    def one_turn(turn_index, carried):
        part_pieces = tuple(
            (
                lax.dynamic_slice_in_dim(member, turn_index * step_rows, step_rows, 0)
                for member in pieces
            )
        )
        return update(carried, part_pieces, offset + turn_index * step_rows)

    return lax.fori_loop(0, row_count // step_rows, one_turn, running)


def body(queries, key_rows, value_rows, cotangent, block_active, send_counts, block_mask):
    shards = lax.axis_size("tm")
    shard_index = lax.axis_index("tm")
    model_width = queries.shape[1]
    head_count = model_width // HD
    own_rows = queries.shape[0]
    own_blocks = own_rows // BLK
    all_blocks = block_active.shape[0]
    slot_count = own_blocks + 2 * CAP
    slot_rows = slot_count * BLK
    scaling = 1.0 / math.sqrt(HD)
    anchor, table, present = slot_layout(
        block_active, send_counts, block_mask, shards, own_blocks, CAP
    )
    records = jnp.concatenate([queries, cotangent], axis=1)
    extended = extended_2(records, (("tm", 0),), CAP * BLK)
    query_slots = extended[:, :model_width].reshape(slot_rows, head_count, HD)
    cotan_slots = extended[:, model_width:].reshape(slot_rows, head_count, HD)
    my_table = lax.dynamic_slice_in_dim(table, shard_index * slot_count, slot_count, 0)
    query_table = jnp.repeat(my_table, BLK, axis=0).astype(jnp.bfloat16)
    live = (
        jnp.repeat(lax.dynamic_slice_in_dim(present, shard_index * slot_count, slot_count, 0), BLK)
        > 0.5
    )
    keys_all, values_all = (
        lax.all_gather(key_rows, "tm", axis=0, tiled=True),
        lax.all_gather(value_rows, "tm", axis=0, tiled=True),
    )

    def own_scores(key_piece, offset):
        allowed = (
            lax.dot_general(
                query_table,
                block_hot(offset, key_piece.shape[0], all_blocks),
                (((1,), (1,)), ((), ())),
                preferred_element_type=jnp.float32,
            )[:, None, :]
            > 0.5
        )
        scores = (
            jnp.einsum("qhd,khd->qhk", query_slots, key_piece, preferred_element_type=jnp.float32)
            * scaling
        )
        return (allowed, scores)

    def forward(running, pieces, offset):
        peak, masses, accum = running
        key_piece = pieces[0].reshape(-1, head_count, HD)
        value_piece = pieces[1].reshape(-1, head_count, HD)
        allowed, scores = own_scores(key_piece, offset)
        new_peak = jnp.maximum(peak, jnp.max(jnp.where(allowed, scores, very_low), axis=2))
        weights = jnp.where(
            allowed, jnp.exp(jnp.where(allowed, scores - new_peak[:, :, None], 0.0)), 0.0
        )
        shrink = jnp.exp(peak - new_peak)
        masses = masses * shrink + jnp.sum(weights, axis=2)
        accum = accum * shrink[:, :, None] + jnp.einsum(
            "qhk,khd->qhd",
            weights.astype(jnp.bfloat16),
            value_piece,
            preferred_element_type=jnp.float32,
        )
        return (new_peak, masses, accum)

    initial = (
        jnp.full((slot_rows, head_count), very_low, jnp.float32),
        jnp.zeros((slot_rows, head_count), jnp.float32),
        jnp.zeros((slot_rows, head_count, HD), jnp.float32),
    )
    peak, masses, accum = sweep(forward, initial, (keys_all, values_all), 0)
    denominator = jnp.where(live[:, None], masses, 1.0)
    attended = (accum / denominator[:, :, None]).astype(jnp.bfloat16)
    log_norm = peak + jnp.log(denominator)
    deltas = jnp.sum(cotan_slots.astype(jnp.float32) * attended.astype(jnp.float32), axis=2)

    def own_gradients(key_piece, value_piece, offset):
        allowed, scores = own_scores(key_piece, offset)
        probs = jnp.where(
            allowed, jnp.exp(jnp.where(allowed, scores - log_norm[:, :, None], 0.0)), 0.0
        )
        weight_grad = jnp.einsum(
            "qhd,khd->qhk", cotan_slots, value_piece, preferred_element_type=jnp.float32
        )
        return (probs, (probs * (weight_grad - deltas[:, :, None])).astype(jnp.bfloat16))

    zero_query = jnp.zeros((slot_rows, head_count, HD), jnp.float32)

    def query_pass(query_sum, pieces, offset):
        key_piece = pieces[0].reshape(-1, head_count, HD)
        value_piece = pieces[1].reshape(-1, head_count, HD)
        probs, score_grad = own_gradients(key_piece, value_piece, offset)
        return query_sum + jnp.einsum(
            "qhk,khd->qhd", score_grad, key_piece, preferred_element_type=jnp.float32
        )

    query_sum = sweep(query_pass, zero_query, (keys_all, values_all), 0)
    own_keys = key_rows.reshape(own_rows, head_count, HD)
    own_values = value_rows.reshape(own_rows, head_count, HD)
    own_hot = block_hot(shard_index * own_rows, own_rows, all_blocks)
    slot_table = table.astype(jnp.bfloat16)
    logsum_all, delta_all = (
        lax.all_gather(log_norm, "tm", axis=0, tiled=True),
        lax.all_gather(deltas, "tm", axis=0, tiled=True),
    )

    def owner_work(running, pieces, offset):
        key_sum, value_sum = running
        query_piece, cotan_piece = pieces
        row_count = query_piece.shape[0]
        logsum_piece = lax.dynamic_slice_in_dim(logsum_all, offset, row_count, 0)
        delta_piece = lax.dynamic_slice_in_dim(delta_all, offset, row_count, 0)
        piece_table = jnp.dot(
            block_hot(offset, row_count, shards * slot_count),
            slot_table,
            preferred_element_type=jnp.float32,
        ).astype(jnp.bfloat16)
        allowed = (
            lax.dot_general(
                piece_table, own_hot, (((1,), (1,)), ((), ())), preferred_element_type=jnp.float32
            )[:, None, :]
            > 0.5
        )
        query_three = query_piece.reshape(row_count, head_count, HD)
        cotan_three = cotan_piece.reshape(row_count, head_count, HD)
        scores = (
            jnp.einsum("qhd,khd->qhk", query_three, own_keys, preferred_element_type=jnp.float32)
            * scaling
        )
        probs = jnp.where(
            allowed, jnp.exp(jnp.where(allowed, scores - logsum_piece[:, :, None], 0.0)), 0.0
        )
        weight_grad = jnp.einsum(
            "qhd,khd->qhk", cotan_three, own_values, preferred_element_type=jnp.float32
        )
        score_grad = (probs * (weight_grad - delta_piece[:, :, None])).astype(jnp.bfloat16)
        key_sum = key_sum + jnp.einsum(
            "qhk,qhd->khd", score_grad, query_three, preferred_element_type=jnp.float32
        )
        value_sum = value_sum + jnp.einsum(
            "qhk,qhd->khd",
            probs.astype(jnp.bfloat16),
            cotan_three,
            preferred_element_type=jnp.float32,
        )
        return (key_sum, value_sum)

    key_zero = jnp.zeros((own_rows, head_count, HD), jnp.float32)
    key_sum, value_sum = sweep(
        owner_work,
        (key_zero, key_zero),
        (
            lax.all_gather(query_slots.reshape(slot_rows, model_width), "tm", axis=0, tiled=True),
            lax.all_gather(cotan_slots.reshape(slot_rows, model_width), "tm", axis=0, tiled=True),
        ),
        jnp.int32(0),
    )
    key_grad = (key_sum * scaling).astype(jnp.bfloat16).reshape(own_rows, model_width)
    value_grad = value_sum.astype(jnp.bfloat16).reshape(own_rows, model_width)
    query_grad = (query_sum * scaling).astype(jnp.bfloat16).reshape(slot_rows, model_width)
    return (attended.reshape(slot_rows, model_width), query_grad, key_grad, value_grad)


def head_kernel(
    shards,
    rows,
    act_ref,
    cnt_ref,
    mask_ref,
    q_hbm,
    k_hbm,
    v_hbm,
    g_hbm,
    att_hbm,
    dq_hbm,
    dk_hbm,
    dv_hbm,
    held,
    scores,
    weights,
    grads,
    key_sum,
    value_sum,
    stage,
    stage_kv,
    in_send,
    in_recv,
    out_send,
    out_recv,
    kv_send,
    kv_recv,
    in_local,
    out_local,
    kv_local,
    relay_in,
    relay_own,
    relay_on,
    relay_recv,
    on_send,
    on_recv,
    relay_local,
):
    me = lax.axis_index("tm")
    half = me // 2
    up = lax.rem(me, 2)
    near = 2 - half
    neighbour = me + 1 - 2 * up
    is_near = me == 1 + half
    total = shards * rows
    blocks = total // BLK
    scaling = 1.0 / math.sqrt(HD)
    sources = (k_hbm, v_hbm, q_hbm, g_hbm)
    outs = (att_hbm, dq_hbm)
    kv_outs = (dk_hbm, dv_hbm)

    def columns(index):
        return pl.ds(pl.multiple_of(index * HD, HD), HD)

    def shard_rows(index):
        return pl.ds(pl.multiple_of(index * rows, rows), rows)

    def incoming(array, source, target):
        return pltpu.make_async_remote_copy(
            src_ref=sources[array].at[:, columns(target)],
            dst_ref=held.at[array, shard_rows(source), :],
            send_sem=in_send.at[array, target],
            recv_sem=in_recv.at[array, source],
            device_id={"tm": target},
            device_id_type=pl.DeviceIdType.MESH,
        )

    def own_incoming(array):
        return pltpu.make_async_copy(
            sources[array].at[:, columns(me)],
            held.at[array, shard_rows(me), :],
            in_local.at[array],
        )

    pieces = (
        (shards - 1, 0, (rows // BLK + 1) * BLK, BLK),
        (0, BLK, BLK, rows),
        (1, BLK + rows, 0, BLK),
    )

    def outgoing(array, piece, chunk, target, source):
        _, low, slot_low, size = pieces[piece]
        return pltpu.make_async_remote_copy(
            src_ref=stage.at[array, chunk, pl.ds(low, size), :],
            dst_ref=outs[array].at[pl.ds(slot_low, size), columns(source)],
            send_sem=out_send.at[array, piece, chunk],
            recv_sem=out_recv.at[array, piece, source],
            device_id={"tm": target},
            device_id_type=pl.DeviceIdType.MESH,
        )

    def own_outgoing(array, piece, chunk):
        _, low, slot_low, size = pieces[piece]
        return pltpu.make_async_copy(
            stage.at[array, chunk, pl.ds(low, size), :],
            outs[array].at[pl.ds(slot_low, size), columns(me)],
            out_local.at[array, piece],
        )

    def middle_half(array, chunk, source):
        low = pl.multiple_of(BLK + lax.rem(chunk, 2) * BLK, BLK)
        return pltpu.make_async_remote_copy(
            src_ref=stage.at[array, chunk, pl.ds(low, BLK), :],
            dst_ref=outs[array].at[pl.ds(low, BLK), columns(source)],
            send_sem=out_send.at[array, 1, chunk],
            recv_sem=out_recv.at[array, 1, source],
            device_id={"tm": chunk},
            device_id_type=pl.DeviceIdType.MESH,
        )

    def to_relay(array, odd, chunk, source_place):
        low = 0 if odd else BLK + rows
        return pltpu.make_async_remote_copy(
            src_ref=stage.at[array, chunk, pl.ds(low, BLK), :],
            dst_ref=relay_in.at[array, source_place, pl.ds(odd * BLK, BLK), :],
            send_sem=out_send.at[array, 0 if odd else 2, chunk],
            recv_sem=relay_recv.at[array, odd, source_place],
            device_id={"tm": near},
            device_id_type=pl.DeviceIdType.MESH,
        )

    def handed_on(array, place, slot_low):
        source = 2 * (1 - half) + place
        return pltpu.make_async_remote_copy(
            src_ref=relay_on.at[array, place],
            dst_ref=outs[array].at[
                pl.ds(pl.multiple_of(slot_low, 2 * BLK), 2 * BLK), columns(source)
            ],
            send_sem=on_send.at[array, place],
            recv_sem=on_recv.at[array, place],
            device_id={"tm": neighbour},
            device_id_type=pl.DeviceIdType.MESH,
        )

    def relay_kept(array, place):
        source = 2 * (1 - half) + place
        return pltpu.make_async_copy(
            relay_own.at[array, place],
            outs[array].at[
                pl.ds(pl.multiple_of((1 - up) * 2 * BLK, 2 * BLK), 2 * BLK), columns(source)
            ],
            relay_local.at[array, place],
        )

    def send_pieces(array, chunk):
        far = chunk // 2 != half
        odd = lax.rem(chunk, 2) == 1

        @pl.when(jnp.logical_not(far))
        def _():
            send_some(array, chunk, (0, 1, 2))

        @pl.when(far & jnp.logical_not(odd))
        def _():
            send_some(array, chunk, (0,))
            middle_half(array, chunk, me).start()
            to_relay(array, 0, chunk, up).start()

        @pl.when(far & odd)
        def _():
            send_some(array, chunk, (2,))
            middle_half(array, chunk, me).start()
            to_relay(array, 1, chunk, up).start()

    def send_some(array, chunk, which):
        for piece in which:
            target = lax.rem(chunk + pieces[piece][0], shards)

            @pl.when(target == me)
            def _():
                own_outgoing(array, piece, chunk).start()

            @pl.when(target != me)
            def _():
                outgoing(array, piece, chunk, target, me).start()

    def kv_outgoing(array, source, target):
        return pltpu.make_async_remote_copy(
            src_ref=stage_kv.at[array, shard_rows(target), :],
            dst_ref=kv_outs[array].at[:, columns(source)],
            send_sem=kv_send.at[array, target],
            recv_sem=kv_recv.at[array, source],
            device_id={"tm": target},
            device_id_type=pl.DeviceIdType.MESH,
        )

    def kv_own(array):
        return pltpu.make_async_copy(
            stage_kv.at[array, shard_rows(me), :],
            kv_outs[array].at[:, columns(me)],
            kv_local.at[array],
        )

    barrier = pltpu.get_barrier_semaphore()
    for step in range(1, shards):
        pl.semaphore_signal(
            barrier,
            inc=1,
            device_id={"tm": lax.rem(me + step, shards)},
            device_id_type=pl.DeviceIdType.MESH,
        )
    for array in range(4):
        own_incoming(array).start()
    pl.semaphore_wait(barrier, shards - 1)
    for array in range(4):
        for step in range(1, shards):
            incoming(array, me, lax.rem(me + step, shards)).start()

    key_sum[...] = jnp.zeros_like(key_sum)
    value_sum[...] = jnp.zeros_like(value_sum)
    for array in range(4):
        own_incoming(array).wait()
    for array in range(2):
        for step in range(1, shards):
            source = lax.rem(me + step, shards)
            incoming(array, source, me).wait_recv()

    lane_block = lax.broadcasted_iota(jnp.int32, (1, rows), 1) // BLK

    def one_chunk(turn, carry):
        pair = turn // 2
        side = (turn - 2 * pair) * (1 - 2 * lax.rem(me, 2))
        chunk = lax.rem(me + side + shards // 2 + 2 * pair + shards, shards)

        @pl.when(chunk != me)
        def _():
            incoming(2, chunk, me).wait_recv()
            incoming(3, chunk, me).wait_recv()

        own = shard_rows(chunk)
        query = held[2, own, :]
        cotan = held[3, own, :]
        peak = jnp.full((1, rows), very_low, jnp.float32)
        for b in range(blocks):
            part = pl.ds(b * BLK, BLK)
            bias = jnp.full((1, rows), very_low, jnp.float32)
            for j in range(rows // BLK):
                a = chunk * (rows // BLK) + j
                seen = act_ref[b] * act_ref[a] * mask_ref[a, b]
                level = jnp.where(seen > 0, 0.0, very_low)
                bias = jnp.where(lane_block == j, level, bias)
            tile = lax.dot_general(
                held[0, part, :], query, (((1,), (1,)), ((), ())), preferred_element_type=jnp.float32
            )
            tile = tile * scaling + bias
            scores[part, :] = tile
            peak = jnp.maximum(peak, jnp.max(tile, axis=0, keepdims=True))
        peak = jnp.maximum(peak, -1e20)
        mass = jnp.zeros((1, rows), jnp.float32)
        for b in range(blocks):
            part = pl.ds(b * BLK, BLK)
            tile = jnp.exp(scores[part, :] - peak)
            scores[part, :] = tile
            weights[part, :] = tile.astype(jnp.bfloat16)
            mass = mass + jnp.sum(tile, axis=0, keepdims=True)
        inverse = 1.0 / jnp.where(mass > 0.0, mass, 1.0)
        att_t = lax.dot_general(
            held[1], weights[...], (((0,), (0,)), ((), ())), preferred_element_type=jnp.float32
        )
        att_t = (att_t * inverse).astype(jnp.bfloat16).astype(jnp.float32)
        delta = jnp.sum(jnp.transpose(cotan.astype(jnp.float32)) * att_t, axis=0, keepdims=True)
        last = rows // BLK - 1
        to_left = cnt_ref[0, chunk] > 0
        to_right = cnt_ref[1, chunk] > 0

        far = chunk // 2 != half
        raw_first = to_left | (far & (lax.rem(chunk, 2) == 1))
        raw_final = to_right | (far & (lax.rem(chunk, 2) == 0))

        def stage_slots(array, result):
            result = result.astype(jnp.bfloat16)
            first, final = result[:BLK], result[last * BLK :]
            zero = jnp.zeros_like(first)
            stage[array, chunk, pl.ds(0, BLK), :] = jnp.where(raw_first, first, zero)
            stage[array, chunk, pl.ds(BLK, BLK), :] = jnp.where(to_left, zero, first)
            stage[array, chunk, pl.ds(rows, BLK), :] = jnp.where(to_right, zero, final)
            stage[array, chunk, pl.ds(rows + BLK, BLK), :] = jnp.where(raw_final, final, zero)

        stage_slots(0, jnp.transpose(att_t))
        send_pieces(0, chunk)
        for b in range(blocks):
            part = pl.ds(b * BLK, BLK)
            tile = lax.dot_general(
                held[1, part, :], cotan, (((1,), (1,)), ((), ())), preferred_element_type=jnp.float32
            )
            probs = scores[part, :] * inverse
            grad = (probs * (tile - delta)).astype(jnp.bfloat16)
            grads[part, :] = grad
            key_sum[part, :] += jnp.dot(grad, query, preferred_element_type=jnp.float32)
            value_sum[part, :] += jnp.dot(
                probs.astype(jnp.bfloat16), cotan, preferred_element_type=jnp.float32
            )
        dq_t = lax.dot_general(
            held[0], grads[...], (((0,), (0,)), ((), ())), preferred_element_type=jnp.float32
        )
        stage_slots(1, jnp.transpose(dq_t * scaling))
        send_pieces(1, chunk)
        return carry

    lax.fori_loop(0, shards, one_chunk, 0)
    stage_kv[0] = (key_sum[...] * scaling).astype(jnp.bfloat16)
    stage_kv[1] = value_sum[...].astype(jnp.bfloat16)
    for array in range(2):
        for step in range(1, shards):
            kv_outgoing(array, me, lax.rem(me + step, shards)).start()
        kv_own(array).start()

    @pl.when(is_near)
    def _():
        lower = me - up
        right = cnt_ref[1, lower]
        left = cnt_ref[0, lower + 1]
        for array in range(2):
            for place in range(2):
                to_relay(array, 0, lower, place).wait_recv()
                to_relay(array, 1, lower + 1, place).wait_recv()
                for b, keep in ((0, right == up), (1, left == 1 - up)):
                    part = pl.ds(b * BLK, BLK)
                    block = relay_in[array, place, part, :]
                    zero = jnp.zeros_like(block)
                    relay_own[array, place, part, :] = jnp.where(keep, block, zero)
                    relay_on[array, place, part, :] = jnp.where(keep, zero, block)
                handed_on(array, place, up * 2 * BLK).start()
                relay_kept(array, place).start()
        for array in range(2):
            for place in range(2):
                handed_on(array, place, up * 2 * BLK).wait_send()
                relay_kept(array, place).wait()

    @pl.when(jnp.logical_not(is_near))
    def _():
        for array in range(2):
            for place in range(2):
                handed_on(array, place, (1 - up) * 2 * BLK).wait_recv()

    for step in range(1, shards):
        peer = lax.rem(me + step, shards)
        for array in range(4):
            incoming(array, me, peer).wait_send()
        for array in range(2):
            kv_outgoing(array, me, peer).wait_send()
            kv_outgoing(array, peer, me).wait_recv()

        @pl.when(peer // 2 == half)
        def _():
            for array in range(2):
                for piece in range(3):
                    outgoing(array, piece, 0, me, peer).wait_recv()
                outgoing(array, 1, peer, peer, me).wait_send()

        @pl.when(peer // 2 != half)
        def _():
            for array in range(2):
                middle_half(array, me, peer).wait_recv()
                middle_half(array, peer, me).wait_send()

            @pl.when(up == 0)
            def _():
                for array in range(2):
                    outgoing(array, 2, 0, me, peer).wait_recv()

            @pl.when(up == 1)
            def _():
                for array in range(2):
                    outgoing(array, 0, 0, me, peer).wait_recv()

    for step in range(shards):
        chunk = lax.rem(me + step, shards)
        for piece in (0, 2):
            if (step + pieces[piece][0]) % shards != 0:
                for array in range(2):
                    outgoing(array, piece, chunk, near, me).wait_send()
    for array in range(2):
        kv_own(array).wait()
        for piece in range(3):
            own_outgoing(array, piece, 0).wait()


def hand_out(*refs):
    count = len(refs) // 2
    done = refs[-1]
    copies = [
        pltpu.make_async_copy(refs[i], refs[count + i], done.at[i]) for i in range(count)
    ]
    for copy in copies:
        copy.start()
    for copy in copies:
        copy.wait()


def exchanged_heads(queries, key_rows, value_rows, cotangent, block_active, send_counts, block_mask):
    shards = lax.axis_size("tm")
    rows, width = queries.shape
    total = shards * rows
    slot_rows = rows + 2 * CAP * BLK
    anywhere = pl.BlockSpec(memory_space=pl.ANY)
    scalars = pl.BlockSpec(memory_space=pltpu.SMEM)
    results = pl.pallas_call(
        functools.partial(head_kernel, shards, rows),
        out_shape=(
            jax.ShapeDtypeStruct((slot_rows, width), jnp.bfloat16),
            jax.ShapeDtypeStruct((slot_rows, width), jnp.bfloat16),
            jax.ShapeDtypeStruct((rows, width), jnp.bfloat16),
            jax.ShapeDtypeStruct((rows, width), jnp.bfloat16),
        ),
        in_specs=[scalars] * 3 + [pl.BlockSpec(memory_space=pltpu.HBM)] * 4,
        out_specs=(anywhere,) * 4,
        scratch_shapes=[
            pltpu.VMEM((4, total, HD), jnp.bfloat16),
            pltpu.VMEM((total, rows), jnp.float32),
            pltpu.VMEM((total, rows), jnp.bfloat16),
            pltpu.VMEM((total, rows), jnp.bfloat16),
            pltpu.VMEM((total, HD), jnp.float32),
            pltpu.VMEM((total, HD), jnp.float32),
            pltpu.VMEM((2, shards, slot_rows, HD), jnp.bfloat16),
            pltpu.VMEM((2, total, HD), jnp.bfloat16),
            pltpu.SemaphoreType.DMA((4, shards)),
            pltpu.SemaphoreType.DMA((4, shards)),
            pltpu.SemaphoreType.DMA((2, 3, shards)),
            pltpu.SemaphoreType.DMA((2, 3, shards)),
            pltpu.SemaphoreType.DMA((2, shards)),
            pltpu.SemaphoreType.DMA((2, shards)),
            pltpu.SemaphoreType.DMA((4,)),
            pltpu.SemaphoreType.DMA((2, 3)),
            pltpu.SemaphoreType.DMA((2,)),
            pltpu.VMEM((2, 2, 2 * BLK, HD), jnp.bfloat16),
            pltpu.VMEM((2, 2, 2 * BLK, HD), jnp.bfloat16),
            pltpu.VMEM((2, 2, 2 * BLK, HD), jnp.bfloat16),
            pltpu.SemaphoreType.DMA((2, 2, 2)),
            pltpu.SemaphoreType.DMA((2, 2)),
            pltpu.SemaphoreType.DMA((2, 2)),
            pltpu.SemaphoreType.DMA((2, 2)),
        ],
        compiler_params=pltpu.CompilerParams(
            collective_id=0, has_side_effects=True, vmem_limit_bytes=63 * 1024 * 1024
        ),
    )(block_active, send_counts.T, block_mask, queries, key_rows, value_rows, cotangent)
    return pl.pallas_call(
        hand_out,
        out_shape=tuple(jax.ShapeDtypeStruct(r.shape, r.dtype) for r in results),
        in_specs=[anywhere] * 4,
        out_specs=(anywhere,) * 4,
        scratch_shapes=[pltpu.SemaphoreType.DMA((4,))],
    )(*results)


def routed(queries, key_rows, value_rows, cotangent, block_active, send_counts, block_mask):
    shards = lax.axis_size("tm")
    rows, width = queries.shape
    args = (queries, key_rows, value_rows, cotangent, block_active, send_counts, block_mask)
    if shards == 4 and width == shards * HD and rows == 2 * BLK:
        return exchanged_heads(*args)
    return body(*args)


def solution(mesh):
    in_specs = (
        P(("groups", "tm"), ("head", "mp")),
        P(("groups", "tm"), ("head", "mp")),
        P(("groups", "tm"), ("head", "mp")),
        P(("groups", "tm"), ("head", "mp")),
        P("groups"),
        P("groups", None),
        P("groups", None),
    )
    out_specs = (
        P(("groups", "tm"), ("head", "mp")),
        P(("groups", "tm"), ("head", "mp")),
        P(("groups", "tm"), ("head", "mp")),
        P(("groups", "tm"), ("head", "mp")),
    )
    return jax.shard_map(
        routed, mesh=mesh, in_specs=in_specs, out_specs=out_specs, check_vma=False)
```

```python
import functools
import math

import jax
import jax.numpy as jnp
from jax import lax
from jax.experimental import pallas as pl
from jax.experimental.pallas import tpu as pltpu
from jax.sharding import PartitionSpec as P

HD = 128
BLK = 128
CAP = 1


very_low = -1e30


def extended_2(shard, sides, width):
    for axis, dim in sides:
        peers, length = (lax.axis_size(axis), shard.shape[dim])
        up = [(i, (i + 1) % peers) for i in range(peers)]
        down = [(j, i) for i, j in up]
        last = lax.slice_in_dim(shard, length - width, length, axis=dim)
        first = lax.slice_in_dim(shard, 0, width, axis=dim)
        before = lax.ppermute(last, axis, up)
        after = lax.ppermute(first, axis, down)
        shard = jnp.concatenate([before, shard, after], axis=dim)
    return shard


def pick(table, positions, extent):
    matches = positions[:, None] == jnp.arange(extent, dtype=jnp.int32)[None, :]
    return jnp.sum(jnp.where(matches, table[None, :], 0), axis=1)


def slot_layout(block_active, send_counts, block_mask, shards, own_blocks, capacity):
    slot_count = own_blocks + 2 * capacity
    all_blocks = shards * own_blocks
    places = jnp.arange(shards * slot_count, dtype=jnp.int32)
    device = places // slot_count
    slot_index = places % slot_count
    before = (device + shards - 1) % shards
    following = (device + 1) % shards
    to_left = send_counts[:, 0]
    to_right = send_counts[:, 1]
    from_before = slot_index < capacity
    from_after = slot_index >= capacity + own_blocks
    owner_shard = jnp.where(from_before, before, jnp.where(from_after, following, device))
    local_block = jnp.where(
        from_before,
        own_blocks - capacity + slot_index,
        jnp.where(from_after, slot_index - capacity - own_blocks, slot_index - capacity),
    )
    middle_ok = (local_block >= pick(to_left, device, shards)) & (
        local_block < own_blocks - pick(to_right, device, shards)
    )
    holds_record = jnp.where(
        from_before,
        slot_index >= capacity - pick(to_right, before, shards),
        jnp.where(from_after, local_block < pick(to_left, following, shards), middle_ok),
    )
    anchor = owner_shard * own_blocks + local_block
    onehot = (anchor[:, None] == jnp.arange(all_blocks, dtype=jnp.int32)[None, :]).astype(
        jnp.float32
    )
    seeing = (block_mask * block_active[None, :]).astype(jnp.float32)
    block_rows = jnp.dot(onehot, seeing, precision=lax.Precision.HIGHEST)
    active = jnp.dot(onehot, block_active.astype(jnp.float32), precision=lax.Precision.HIGHEST)
    present = jnp.where(holds_record, active, 0.0)
    return (anchor, block_rows * present[:, None], present)


def block_hot(offset, length, extent):
    blocks = (offset + jnp.arange(length, dtype=jnp.int32)) // BLK
    return (blocks[:, None] == jnp.arange(extent, dtype=jnp.int32)[None, :]).astype(jnp.bfloat16)


def sweep(update, running, pieces, offset):
    row_count = pieces[0].shape[0]
    step_rows = math.gcd(row_count, 1024)
    if step_rows == row_count:
        return update(running, pieces, offset)

    def one_turn(turn_index, carried):
        part_pieces = tuple(
            (
                lax.dynamic_slice_in_dim(member, turn_index * step_rows, step_rows, 0)
                for member in pieces
            )
        )
        return update(carried, part_pieces, offset + turn_index * step_rows)

    return lax.fori_loop(0, row_count // step_rows, one_turn, running)


def body(queries, key_rows, value_rows, cotangent, block_active, send_counts, block_mask):
    shards = lax.axis_size("tm")
    shard_index = lax.axis_index("tm")
    model_width = queries.shape[1]
    head_count = model_width // HD
    own_rows = queries.shape[0]
    own_blocks = own_rows // BLK
    all_blocks = block_active.shape[0]
    slot_count = own_blocks + 2 * CAP
    slot_rows = slot_count * BLK
    scaling = 1.0 / math.sqrt(HD)
    anchor, table, present = slot_layout(
        block_active, send_counts, block_mask, shards, own_blocks, CAP
    )
    records = jnp.concatenate([queries, cotangent], axis=1)
    extended = extended_2(records, (("tm", 0),), CAP * BLK)
    query_slots = extended[:, :model_width].reshape(slot_rows, head_count, HD)
    cotan_slots = extended[:, model_width:].reshape(slot_rows, head_count, HD)
    my_table = lax.dynamic_slice_in_dim(table, shard_index * slot_count, slot_count, 0)
    query_table = jnp.repeat(my_table, BLK, axis=0).astype(jnp.bfloat16)
    live = (
        jnp.repeat(lax.dynamic_slice_in_dim(present, shard_index * slot_count, slot_count, 0), BLK)
        > 0.5
    )
    keys_all, values_all = (
        lax.all_gather(key_rows, "tm", axis=0, tiled=True),
        lax.all_gather(value_rows, "tm", axis=0, tiled=True),
    )

    def own_scores(key_piece, offset):
        allowed = (
            lax.dot_general(
                query_table,
                block_hot(offset, key_piece.shape[0], all_blocks),
                (((1,), (1,)), ((), ())),
                preferred_element_type=jnp.float32,
            )[:, None, :]
            > 0.5
        )
        scores = (
            jnp.einsum("qhd,khd->qhk", query_slots, key_piece, preferred_element_type=jnp.float32)
            * scaling
        )
        return (allowed, scores)

    def forward(running, pieces, offset):
        peak, masses, accum = running
        key_piece = pieces[0].reshape(-1, head_count, HD)
        value_piece = pieces[1].reshape(-1, head_count, HD)
        allowed, scores = own_scores(key_piece, offset)
        new_peak = jnp.maximum(peak, jnp.max(jnp.where(allowed, scores, very_low), axis=2))
        weights = jnp.where(
            allowed, jnp.exp(jnp.where(allowed, scores - new_peak[:, :, None], 0.0)), 0.0
        )
        shrink = jnp.exp(peak - new_peak)
        masses = masses * shrink + jnp.sum(weights, axis=2)
        accum = accum * shrink[:, :, None] + jnp.einsum(
            "qhk,khd->qhd",
            weights.astype(jnp.bfloat16),
            value_piece,
            preferred_element_type=jnp.float32,
        )
        return (new_peak, masses, accum)

    initial = (
        jnp.full((slot_rows, head_count), very_low, jnp.float32),
        jnp.zeros((slot_rows, head_count), jnp.float32),
        jnp.zeros((slot_rows, head_count, HD), jnp.float32),
    )
    peak, masses, accum = sweep(forward, initial, (keys_all, values_all), 0)
    denominator = jnp.where(live[:, None], masses, 1.0)
    attended = (accum / denominator[:, :, None]).astype(jnp.bfloat16)
    log_norm = peak + jnp.log(denominator)
    deltas = jnp.sum(cotan_slots.astype(jnp.float32) * attended.astype(jnp.float32), axis=2)

    def own_gradients(key_piece, value_piece, offset):
        allowed, scores = own_scores(key_piece, offset)
        probs = jnp.where(
            allowed, jnp.exp(jnp.where(allowed, scores - log_norm[:, :, None], 0.0)), 0.0
        )
        weight_grad = jnp.einsum(
            "qhd,khd->qhk", cotan_slots, value_piece, preferred_element_type=jnp.float32
        )
        return (probs, (probs * (weight_grad - deltas[:, :, None])).astype(jnp.bfloat16))

    zero_query = jnp.zeros((slot_rows, head_count, HD), jnp.float32)

    def query_pass(query_sum, pieces, offset):
        key_piece = pieces[0].reshape(-1, head_count, HD)
        value_piece = pieces[1].reshape(-1, head_count, HD)
        probs, score_grad = own_gradients(key_piece, value_piece, offset)
        return query_sum + jnp.einsum(
            "qhk,khd->qhd", score_grad, key_piece, preferred_element_type=jnp.float32
        )

    query_sum = sweep(query_pass, zero_query, (keys_all, values_all), 0)
    own_keys = key_rows.reshape(own_rows, head_count, HD)
    own_values = value_rows.reshape(own_rows, head_count, HD)
    own_hot = block_hot(shard_index * own_rows, own_rows, all_blocks)
    slot_table = table.astype(jnp.bfloat16)
    logsum_all, delta_all = (
        lax.all_gather(log_norm, "tm", axis=0, tiled=True),
        lax.all_gather(deltas, "tm", axis=0, tiled=True),
    )

    def owner_work(running, pieces, offset):
        key_sum, value_sum = running
        query_piece, cotan_piece = pieces
        row_count = query_piece.shape[0]
        logsum_piece = lax.dynamic_slice_in_dim(logsum_all, offset, row_count, 0)
        delta_piece = lax.dynamic_slice_in_dim(delta_all, offset, row_count, 0)
        piece_table = jnp.dot(
            block_hot(offset, row_count, shards * slot_count),
            slot_table,
            preferred_element_type=jnp.float32,
        ).astype(jnp.bfloat16)
        allowed = (
            lax.dot_general(
                piece_table, own_hot, (((1,), (1,)), ((), ())), preferred_element_type=jnp.float32
            )[:, None, :]
            > 0.5
        )
        query_three = query_piece.reshape(row_count, head_count, HD)
        cotan_three = cotan_piece.reshape(row_count, head_count, HD)
        scores = (
            jnp.einsum("qhd,khd->qhk", query_three, own_keys, preferred_element_type=jnp.float32)
            * scaling
        )
        probs = jnp.where(
            allowed, jnp.exp(jnp.where(allowed, scores - logsum_piece[:, :, None], 0.0)), 0.0
        )
        weight_grad = jnp.einsum(
            "qhd,khd->qhk", cotan_three, own_values, preferred_element_type=jnp.float32
        )
        score_grad = (probs * (weight_grad - delta_piece[:, :, None])).astype(jnp.bfloat16)
        key_sum = key_sum + jnp.einsum(
            "qhk,qhd->khd", score_grad, query_three, preferred_element_type=jnp.float32
        )
        value_sum = value_sum + jnp.einsum(
            "qhk,qhd->khd",
            probs.astype(jnp.bfloat16),
            cotan_three,
            preferred_element_type=jnp.float32,
        )
        return (key_sum, value_sum)

    key_zero = jnp.zeros((own_rows, head_count, HD), jnp.float32)
    key_sum, value_sum = sweep(
        owner_work,
        (key_zero, key_zero),
        (
            lax.all_gather(query_slots.reshape(slot_rows, model_width), "tm", axis=0, tiled=True),
            lax.all_gather(cotan_slots.reshape(slot_rows, model_width), "tm", axis=0, tiled=True),
        ),
        jnp.int32(0),
    )
    key_grad = (key_sum * scaling).astype(jnp.bfloat16).reshape(own_rows, model_width)
    value_grad = value_sum.astype(jnp.bfloat16).reshape(own_rows, model_width)
    query_grad = (query_sum * scaling).astype(jnp.bfloat16).reshape(slot_rows, model_width)
    return (attended.reshape(slot_rows, model_width), query_grad, key_grad, value_grad)


def head_kernel(
    shards,
    rows,
    act_ref,
    cnt_ref,
    mask_ref,
    q_hbm,
    k_hbm,
    v_hbm,
    g_hbm,
    att_hbm,
    dq_hbm,
    dk_hbm,
    dv_hbm,
    held,
    scores,
    weights,
    grads,
    key_sum,
    value_sum,
    stage,
    stage_kv,
    in_send,
    in_recv,
    out_send,
    out_recv,
    kv_send,
    kv_recv,
    in_local,
    out_local,
    kv_local,
    relay_in,
    relay_own,
    relay_on,
    relay_recv,
    on_send,
    on_recv,
    relay_local,
):
    me = lax.axis_index("tm")
    half = me // 2
    up = lax.rem(me, 2)
    near = 2 - half
    neighbour = me + 1 - 2 * up
    is_near = me == 1 + half
    total = shards * rows
    blocks = total // BLK
    scaling = 1.0 / math.sqrt(HD)
    sources = (k_hbm, v_hbm, q_hbm, g_hbm)
    outs = (att_hbm, dq_hbm)
    kv_outs = (dk_hbm, dv_hbm)

    def columns(index):
        return pl.ds(pl.multiple_of(index * HD, HD), HD)

    def shard_rows(index):
        return pl.ds(pl.multiple_of(index * rows, rows), rows)

    def incoming(array, source, target):
        return pltpu.make_async_remote_copy(
            src_ref=sources[array].at[:, columns(target)],
            dst_ref=held.at[array, shard_rows(source), :],
            send_sem=in_send.at[array, target],
            recv_sem=in_recv.at[array, source],
            device_id={"tm": target},
            device_id_type=pl.DeviceIdType.MESH,
        )

    def own_incoming(array):
        return pltpu.make_async_copy(
            sources[array].at[:, columns(me)],
            held.at[array, shard_rows(me), :],
            in_local.at[array],
        )

    pieces = (
        (shards - 1, 0, (rows // BLK + 1) * BLK, BLK),
        (0, BLK, BLK, rows),
        (1, BLK + rows, 0, BLK),
    )

    def outgoing(array, piece, chunk, target, source):
        _, low, slot_low, size = pieces[piece]
        return pltpu.make_async_remote_copy(
            src_ref=stage.at[array, chunk, pl.ds(low, size), :],
            dst_ref=outs[array].at[pl.ds(slot_low, size), columns(source)],
            send_sem=out_send.at[array, piece, chunk],
            recv_sem=out_recv.at[array, piece, source],
            device_id={"tm": target},
            device_id_type=pl.DeviceIdType.MESH,
        )

    def own_outgoing(array, piece, chunk):
        _, low, slot_low, size = pieces[piece]
        return pltpu.make_async_copy(
            stage.at[array, chunk, pl.ds(low, size), :],
            outs[array].at[pl.ds(slot_low, size), columns(me)],
            out_local.at[array, piece],
        )

    def middle_half(array, chunk, source):
        low = pl.multiple_of(BLK + lax.rem(chunk, 2) * BLK, BLK)
        return pltpu.make_async_remote_copy(
            src_ref=stage.at[array, chunk, pl.ds(low, BLK), :],
            dst_ref=outs[array].at[pl.ds(low, BLK), columns(source)],
            send_sem=out_send.at[array, 1, chunk],
            recv_sem=out_recv.at[array, 1, source],
            device_id={"tm": chunk},
            device_id_type=pl.DeviceIdType.MESH,
        )

    def to_relay(array, odd, chunk, source_place):
        low = 0 if odd else BLK + rows
        return pltpu.make_async_remote_copy(
            src_ref=stage.at[array, chunk, pl.ds(low, BLK), :],
            dst_ref=relay_in.at[array, source_place, pl.ds(odd * BLK, BLK), :],
            send_sem=out_send.at[array, 0 if odd else 2, chunk],
            recv_sem=relay_recv.at[array, odd, source_place],
            device_id={"tm": near},
            device_id_type=pl.DeviceIdType.MESH,
        )

    def handed_on(array, place, slot_low):
        source = 2 * (1 - half) + place
        return pltpu.make_async_remote_copy(
            src_ref=relay_on.at[array, place],
            dst_ref=outs[array].at[
                pl.ds(pl.multiple_of(slot_low, 2 * BLK), 2 * BLK), columns(source)
            ],
            send_sem=on_send.at[array, place],
            recv_sem=on_recv.at[array, place],
            device_id={"tm": neighbour},
            device_id_type=pl.DeviceIdType.MESH,
        )

    def relay_kept(array, place):
        source = 2 * (1 - half) + place
        return pltpu.make_async_copy(
            relay_own.at[array, place],
            outs[array].at[
                pl.ds(pl.multiple_of((1 - up) * 2 * BLK, 2 * BLK), 2 * BLK), columns(source)
            ],
            relay_local.at[array, place],
        )

    def send_pieces(array, chunk):
        far = chunk // 2 != half
        odd = lax.rem(chunk, 2) == 1

        @pl.when(jnp.logical_not(far))
        def _():
            send_some(array, chunk, (0, 1, 2))

        @pl.when(far & jnp.logical_not(odd))
        def _():
            send_some(array, chunk, (0,))
            middle_half(array, chunk, me).start()
            to_relay(array, 0, chunk, up).start()

        @pl.when(far & odd)
        def _():
            send_some(array, chunk, (2,))
            middle_half(array, chunk, me).start()
            to_relay(array, 1, chunk, up).start()

    def send_some(array, chunk, which):
        for piece in which:
            target = lax.rem(chunk + pieces[piece][0], shards)

            @pl.when(target == me)
            def _():
                own_outgoing(array, piece, chunk).start()

            @pl.when(target != me)
            def _():
                outgoing(array, piece, chunk, target, me).start()

    def kv_outgoing(array, source, target):
        return pltpu.make_async_remote_copy(
            src_ref=stage_kv.at[array, shard_rows(target), :],
            dst_ref=kv_outs[array].at[:, columns(source)],
            send_sem=kv_send.at[array, target],
            recv_sem=kv_recv.at[array, source],
            device_id={"tm": target},
            device_id_type=pl.DeviceIdType.MESH,
        )

    def kv_own(array):
        return pltpu.make_async_copy(
            stage_kv.at[array, shard_rows(me), :],
            kv_outs[array].at[:, columns(me)],
            kv_local.at[array],
        )

    barrier = pltpu.get_barrier_semaphore()
    for step in range(1, shards):
        pl.semaphore_signal(
            barrier,
            inc=1,
            device_id={"tm": lax.rem(me + step, shards)},
            device_id_type=pl.DeviceIdType.MESH,
        )
    for array in range(4):
        own_incoming(array).start()
    pl.semaphore_wait(barrier, shards - 1)
    for array in range(4):
        for step in range(1, shards):
            incoming(array, me, lax.rem(me + step, shards)).start()

    key_sum[...] = jnp.zeros_like(key_sum)
    value_sum[...] = jnp.zeros_like(value_sum)
    for array in range(4):
        own_incoming(array).wait()
    for array in range(2):
        for step in range(1, shards):
            source = lax.rem(me + step, shards)
            incoming(array, source, me).wait_recv()

    lane_block = lax.broadcasted_iota(jnp.int32, (1, rows), 1) // BLK

    def one_chunk(turn, carry):
        pair = turn // 2
        side = (turn - 2 * pair) * (1 - 2 * lax.rem(me, 2))
        chunk = lax.rem(me + side + shards // 2 + 2 * pair + shards, shards)

        @pl.when(chunk != me)
        def _():
            incoming(2, chunk, me).wait_recv()
            incoming(3, chunk, me).wait_recv()

        own = shard_rows(chunk)
        query = held[2, own, :]
        cotan = held[3, own, :]
        peak = jnp.full((1, rows), very_low, jnp.float32)
        for b in range(blocks):
            part = pl.ds(b * BLK, BLK)
            bias = jnp.full((1, rows), very_low, jnp.float32)
            for j in range(rows // BLK):
                a = chunk * (rows // BLK) + j
                seen = act_ref[b] * act_ref[a] * mask_ref[a, b]
                level = jnp.where(seen > 0, 0.0, very_low)
                bias = jnp.where(lane_block == j, level, bias)
            tile = lax.dot_general(
                held[0, part, :], query, (((1,), (1,)), ((), ())), preferred_element_type=jnp.float32
            )
            tile = tile * scaling + bias
            scores[part, :] = tile
            peak = jnp.maximum(peak, jnp.max(tile, axis=0, keepdims=True))
        peak = jnp.maximum(peak, -1e20)
        mass = jnp.zeros((1, rows), jnp.float32)
        for b in range(blocks):
            part = pl.ds(b * BLK, BLK)
            tile = jnp.exp(scores[part, :] - peak)
            scores[part, :] = tile
            weights[part, :] = tile.astype(jnp.bfloat16)
            mass = mass + jnp.sum(tile, axis=0, keepdims=True)
        inverse = 1.0 / jnp.where(mass > 0.0, mass, 1.0)
        att_t = lax.dot_general(
            held[1], weights[...], (((0,), (0,)), ((), ())), preferred_element_type=jnp.float32
        )
        att_t = (att_t * inverse).astype(jnp.bfloat16).astype(jnp.float32)
        delta = jnp.sum(jnp.transpose(cotan.astype(jnp.float32)) * att_t, axis=0, keepdims=True)
        last = rows // BLK - 1
        to_left = cnt_ref[0, chunk] > 0
        to_right = cnt_ref[1, chunk] > 0

        far = chunk // 2 != half
        raw_first = to_left | (far & (lax.rem(chunk, 2) == 1))
        raw_final = to_right | (far & (lax.rem(chunk, 2) == 0))

        def stage_slots(array, result):
            result = result.astype(jnp.bfloat16)
            first, final = result[:BLK], result[last * BLK :]
            zero = jnp.zeros_like(first)
            stage[array, chunk, pl.ds(0, BLK), :] = jnp.where(raw_first, first, zero)
            stage[array, chunk, pl.ds(BLK, BLK), :] = jnp.where(to_left, zero, first)
            stage[array, chunk, pl.ds(rows, BLK), :] = jnp.where(to_right, zero, final)
            stage[array, chunk, pl.ds(rows + BLK, BLK), :] = jnp.where(raw_final, final, zero)

        stage_slots(0, jnp.transpose(att_t))
        send_pieces(0, chunk)
        for b in range(blocks):
            part = pl.ds(b * BLK, BLK)
            tile = lax.dot_general(
                held[1, part, :], cotan, (((1,), (1,)), ((), ())), preferred_element_type=jnp.float32
            )
            probs = scores[part, :] * inverse
            grad = (probs * (tile - delta)).astype(jnp.bfloat16)
            grads[part, :] = grad
            key_sum[part, :] += jnp.dot(grad, query, preferred_element_type=jnp.float32)
            value_sum[part, :] += jnp.dot(
                probs.astype(jnp.bfloat16), cotan, preferred_element_type=jnp.float32
            )
        dq_t = lax.dot_general(
            held[0], grads[...], (((0,), (0,)), ((), ())), preferred_element_type=jnp.float32
        )
        stage_slots(1, jnp.transpose(dq_t * scaling))
        send_pieces(1, chunk)
        return carry

    lax.fori_loop(0, shards, one_chunk, 0)
    stage_kv[0] = (key_sum[...] * scaling).astype(jnp.bfloat16)
    stage_kv[1] = value_sum[...].astype(jnp.bfloat16)
    for array in range(2):
        for step in range(1, shards):
            kv_outgoing(array, me, lax.rem(me + step, shards)).start()
        kv_own(array).start()

    @pl.when(is_near)
    def _():
        lower = me - up
        right = cnt_ref[1, lower]
        left = cnt_ref[0, lower + 1]
        for array in range(2):
            for place in range(2):
                to_relay(array, 0, lower, place).wait_recv()
                to_relay(array, 1, lower + 1, place).wait_recv()
                for b, keep in ((0, right == up), (1, left == 1 - up)):
                    part = pl.ds(b * BLK, BLK)
                    block = relay_in[array, place, part, :]
                    zero = jnp.zeros_like(block)
                    relay_own[array, place, part, :] = jnp.where(keep, block, zero)
                    relay_on[array, place, part, :] = jnp.where(keep, zero, block)
                handed_on(array, place, up * 2 * BLK).start()
                relay_kept(array, place).start()
        for array in range(2):
            for place in range(2):
                handed_on(array, place, up * 2 * BLK).wait_send()
                relay_kept(array, place).wait()

    @pl.when(jnp.logical_not(is_near))
    def _():
        for array in range(2):
            for place in range(2):
                handed_on(array, place, (1 - up) * 2 * BLK).wait_recv()

    for step in range(1, shards):
        peer = lax.rem(me + step, shards)
        for array in range(4):
            incoming(array, me, peer).wait_send()
        for array in range(2):
            kv_outgoing(array, me, peer).wait_send()
            kv_outgoing(array, peer, me).wait_recv()

        @pl.when(peer // 2 == half)
        def _():
            for array in range(2):
                for piece in range(3):
                    outgoing(array, piece, 0, me, peer).wait_recv()
                outgoing(array, 1, peer, peer, me).wait_send()

        @pl.when(peer // 2 != half)
        def _():
            for array in range(2):
                middle_half(array, me, peer).wait_recv()
                middle_half(array, peer, me).wait_send()

            @pl.when(up == 0)
            def _():
                for array in range(2):
                    outgoing(array, 2, 0, me, peer).wait_recv()

            @pl.when(up == 1)
            def _():
                for array in range(2):
                    outgoing(array, 0, 0, me, peer).wait_recv()

    for step in range(shards):
        chunk = lax.rem(me + step, shards)
        for piece in (0, 2):
            if (step + pieces[piece][0]) % shards != 0:
                for array in range(2):
                    outgoing(array, piece, chunk, near, me).wait_send()
    for array in range(2):
        kv_own(array).wait()
        for piece in range(3):
            own_outgoing(array, piece, 0).wait()


def hand_out(*refs):
    count = 4
    sources, targets, held = refs[:count], refs[count : 2 * count], refs[2 * count : 3 * count]
    arrived, left = refs[3 * count :]
    inward = [pltpu.make_async_copy(sources[i], held[i], arrived.at[i]) for i in range(count)]
    outward = [pltpu.make_async_copy(held[i], targets[i], left.at[i]) for i in range(count)]
    for copy in inward:
        copy.start()
    for first, second in zip(inward, outward):
        first.wait()
        second.start()
    for copy in outward:
        copy.wait()


def exchanged_heads(queries, key_rows, value_rows, cotangent, block_active, send_counts, block_mask):
    shards = lax.axis_size("tm")
    rows, width = queries.shape
    total = shards * rows
    slot_rows = rows + 2 * CAP * BLK
    anywhere = pl.BlockSpec(memory_space=pl.ANY)
    scalars = pl.BlockSpec(memory_space=pltpu.SMEM)
    results = pl.pallas_call(
        functools.partial(head_kernel, shards, rows),
        out_shape=(
            jax.ShapeDtypeStruct((slot_rows, width), jnp.bfloat16),
            jax.ShapeDtypeStruct((slot_rows, width), jnp.bfloat16),
            jax.ShapeDtypeStruct((rows, width), jnp.bfloat16),
            jax.ShapeDtypeStruct((rows, width), jnp.bfloat16),
        ),
        in_specs=[scalars] * 3 + [pl.BlockSpec(memory_space=pltpu.HBM)] * 4,
        out_specs=(anywhere,) * 4,
        scratch_shapes=[
            pltpu.VMEM((4, total, HD), jnp.bfloat16),
            pltpu.VMEM((total, rows), jnp.float32),
            pltpu.VMEM((total, rows), jnp.bfloat16),
            pltpu.VMEM((total, rows), jnp.bfloat16),
            pltpu.VMEM((total, HD), jnp.float32),
            pltpu.VMEM((total, HD), jnp.float32),
            pltpu.VMEM((2, shards, slot_rows, HD), jnp.bfloat16),
            pltpu.VMEM((2, total, HD), jnp.bfloat16),
            pltpu.SemaphoreType.DMA((4, shards)),
            pltpu.SemaphoreType.DMA((4, shards)),
            pltpu.SemaphoreType.DMA((2, 3, shards)),
            pltpu.SemaphoreType.DMA((2, 3, shards)),
            pltpu.SemaphoreType.DMA((2, shards)),
            pltpu.SemaphoreType.DMA((2, shards)),
            pltpu.SemaphoreType.DMA((4,)),
            pltpu.SemaphoreType.DMA((2, 3)),
            pltpu.SemaphoreType.DMA((2,)),
            pltpu.VMEM((2, 2, 2 * BLK, HD), jnp.bfloat16),
            pltpu.VMEM((2, 2, 2 * BLK, HD), jnp.bfloat16),
            pltpu.VMEM((2, 2, 2 * BLK, HD), jnp.bfloat16),
            pltpu.SemaphoreType.DMA((2, 2, 2)),
            pltpu.SemaphoreType.DMA((2, 2)),
            pltpu.SemaphoreType.DMA((2, 2)),
            pltpu.SemaphoreType.DMA((2, 2)),
        ],
        compiler_params=pltpu.CompilerParams(
            collective_id=0, has_side_effects=True, vmem_limit_bytes=63 * 1024 * 1024
        ),
    )(block_active, send_counts.T, block_mask, queries, key_rows, value_rows, cotangent)
    return pl.pallas_call(
        hand_out,
        out_shape=tuple(jax.ShapeDtypeStruct(r.shape, r.dtype) for r in results),
        in_specs=[anywhere] * 4,
        out_specs=(anywhere,) * 4,
        scratch_shapes=[pltpu.VMEM(r.shape, r.dtype) for r in results]
        + [pltpu.SemaphoreType.DMA((4,)), pltpu.SemaphoreType.DMA((4,))],
    )(*results)


def routed(queries, key_rows, value_rows, cotangent, block_active, send_counts, block_mask):
    shards = lax.axis_size("tm")
    rows, width = queries.shape
    args = (queries, key_rows, value_rows, cotangent, block_active, send_counts, block_mask)
    if shards == 4 and width == shards * HD and rows == 2 * BLK:
        return exchanged_heads(*args)
    return body(*args)


def solution(mesh):
    in_specs = (
        P(("groups", "tm"), ("head", "mp")),
        P(("groups", "tm"), ("head", "mp")),
        P(("groups", "tm"), ("head", "mp")),
        P(("groups", "tm"), ("head", "mp")),
        P("groups"),
        P("groups", None),
        P("groups", None),
    )
    out_specs = (
        P(("groups", "tm"), ("head", "mp")),
        P(("groups", "tm"), ("head", "mp")),
        P(("groups", "tm"), ("head", "mp")),
        P(("groups", "tm"), ("head", "mp")),
    )
    return jax.shard_map(
        routed, mesh=mesh, in_specs=in_specs, out_specs=out_specs, check_vma=False)
```

```python
import functools
import math

import jax
import jax.numpy as jnp
from jax import lax
from jax.experimental import pallas as pl
from jax.experimental.pallas import tpu as pltpu
from jax.sharding import PartitionSpec as P

HD = 128
BLK = 128
CAP = 1


very_low = -1e30


def extended_2(shard, sides, width):
    for axis, dim in sides:
        peers, length = (lax.axis_size(axis), shard.shape[dim])
        up = [(i, (i + 1) % peers) for i in range(peers)]
        down = [(j, i) for i, j in up]
        last = lax.slice_in_dim(shard, length - width, length, axis=dim)
        first = lax.slice_in_dim(shard, 0, width, axis=dim)
        before = lax.ppermute(last, axis, up)
        after = lax.ppermute(first, axis, down)
        shard = jnp.concatenate([before, shard, after], axis=dim)
    return shard


def pick(table, positions, extent):
    matches = positions[:, None] == jnp.arange(extent, dtype=jnp.int32)[None, :]
    return jnp.sum(jnp.where(matches, table[None, :], 0), axis=1)


def slot_layout(block_active, send_counts, block_mask, shards, own_blocks, capacity):
    slot_count = own_blocks + 2 * capacity
    all_blocks = shards * own_blocks
    places = jnp.arange(shards * slot_count, dtype=jnp.int32)
    device = places // slot_count
    slot_index = places % slot_count
    before = (device + shards - 1) % shards
    following = (device + 1) % shards
    to_left = send_counts[:, 0]
    to_right = send_counts[:, 1]
    from_before = slot_index < capacity
    from_after = slot_index >= capacity + own_blocks
    owner_shard = jnp.where(from_before, before, jnp.where(from_after, following, device))
    local_block = jnp.where(
        from_before,
        own_blocks - capacity + slot_index,
        jnp.where(from_after, slot_index - capacity - own_blocks, slot_index - capacity),
    )
    middle_ok = (local_block >= pick(to_left, device, shards)) & (
        local_block < own_blocks - pick(to_right, device, shards)
    )
    holds_record = jnp.where(
        from_before,
        slot_index >= capacity - pick(to_right, before, shards),
        jnp.where(from_after, local_block < pick(to_left, following, shards), middle_ok),
    )
    anchor = owner_shard * own_blocks + local_block
    onehot = (anchor[:, None] == jnp.arange(all_blocks, dtype=jnp.int32)[None, :]).astype(
        jnp.float32
    )
    seeing = (block_mask * block_active[None, :]).astype(jnp.float32)
    block_rows = jnp.dot(onehot, seeing, precision=lax.Precision.HIGHEST)
    active = jnp.dot(onehot, block_active.astype(jnp.float32), precision=lax.Precision.HIGHEST)
    present = jnp.where(holds_record, active, 0.0)
    return (anchor, block_rows * present[:, None], present)


def block_hot(offset, length, extent):
    blocks = (offset + jnp.arange(length, dtype=jnp.int32)) // BLK
    return (blocks[:, None] == jnp.arange(extent, dtype=jnp.int32)[None, :]).astype(jnp.bfloat16)


def sweep(update, running, pieces, offset):
    row_count = pieces[0].shape[0]
    step_rows = math.gcd(row_count, 1024)
    if step_rows == row_count:
        return update(running, pieces, offset)

    def one_turn(turn_index, carried):
        part_pieces = tuple(
            (
                lax.dynamic_slice_in_dim(member, turn_index * step_rows, step_rows, 0)
                for member in pieces
            )
        )
        return update(carried, part_pieces, offset + turn_index * step_rows)

    return lax.fori_loop(0, row_count // step_rows, one_turn, running)


def body(queries, key_rows, value_rows, cotangent, block_active, send_counts, block_mask):
    shards = lax.axis_size("tm")
    shard_index = lax.axis_index("tm")
    model_width = queries.shape[1]
    head_count = model_width // HD
    own_rows = queries.shape[0]
    own_blocks = own_rows // BLK
    all_blocks = block_active.shape[0]
    slot_count = own_blocks + 2 * CAP
    slot_rows = slot_count * BLK
    scaling = 1.0 / math.sqrt(HD)
    anchor, table, present = slot_layout(
        block_active, send_counts, block_mask, shards, own_blocks, CAP
    )
    records = jnp.concatenate([queries, cotangent], axis=1)
    extended = extended_2(records, (("tm", 0),), CAP * BLK)
    query_slots = extended[:, :model_width].reshape(slot_rows, head_count, HD)
    cotan_slots = extended[:, model_width:].reshape(slot_rows, head_count, HD)
    my_table = lax.dynamic_slice_in_dim(table, shard_index * slot_count, slot_count, 0)
    query_table = jnp.repeat(my_table, BLK, axis=0).astype(jnp.bfloat16)
    live = (
        jnp.repeat(lax.dynamic_slice_in_dim(present, shard_index * slot_count, slot_count, 0), BLK)
        > 0.5
    )
    keys_all, values_all = (
        lax.all_gather(key_rows, "tm", axis=0, tiled=True),
        lax.all_gather(value_rows, "tm", axis=0, tiled=True),
    )

    def own_scores(key_piece, offset):
        allowed = (
            lax.dot_general(
                query_table,
                block_hot(offset, key_piece.shape[0], all_blocks),
                (((1,), (1,)), ((), ())),
                preferred_element_type=jnp.float32,
            )[:, None, :]
            > 0.5
        )
        scores = (
            jnp.einsum("qhd,khd->qhk", query_slots, key_piece, preferred_element_type=jnp.float32)
            * scaling
        )
        return (allowed, scores)

    def forward(running, pieces, offset):
        peak, masses, accum = running
        key_piece = pieces[0].reshape(-1, head_count, HD)
        value_piece = pieces[1].reshape(-1, head_count, HD)
        allowed, scores = own_scores(key_piece, offset)
        new_peak = jnp.maximum(peak, jnp.max(jnp.where(allowed, scores, very_low), axis=2))
        weights = jnp.where(
            allowed, jnp.exp(jnp.where(allowed, scores - new_peak[:, :, None], 0.0)), 0.0
        )
        shrink = jnp.exp(peak - new_peak)
        masses = masses * shrink + jnp.sum(weights, axis=2)
        accum = accum * shrink[:, :, None] + jnp.einsum(
            "qhk,khd->qhd",
            weights.astype(jnp.bfloat16),
            value_piece,
            preferred_element_type=jnp.float32,
        )
        return (new_peak, masses, accum)

    initial = (
        jnp.full((slot_rows, head_count), very_low, jnp.float32),
        jnp.zeros((slot_rows, head_count), jnp.float32),
        jnp.zeros((slot_rows, head_count, HD), jnp.float32),
    )
    peak, masses, accum = sweep(forward, initial, (keys_all, values_all), 0)
    denominator = jnp.where(live[:, None], masses, 1.0)
    attended = (accum / denominator[:, :, None]).astype(jnp.bfloat16)
    log_norm = peak + jnp.log(denominator)
    deltas = jnp.sum(cotan_slots.astype(jnp.float32) * attended.astype(jnp.float32), axis=2)

    def own_gradients(key_piece, value_piece, offset):
        allowed, scores = own_scores(key_piece, offset)
        probs = jnp.where(
            allowed, jnp.exp(jnp.where(allowed, scores - log_norm[:, :, None], 0.0)), 0.0
        )
        weight_grad = jnp.einsum(
            "qhd,khd->qhk", cotan_slots, value_piece, preferred_element_type=jnp.float32
        )
        return (probs, (probs * (weight_grad - deltas[:, :, None])).astype(jnp.bfloat16))

    zero_query = jnp.zeros((slot_rows, head_count, HD), jnp.float32)

    def query_pass(query_sum, pieces, offset):
        key_piece = pieces[0].reshape(-1, head_count, HD)
        value_piece = pieces[1].reshape(-1, head_count, HD)
        probs, score_grad = own_gradients(key_piece, value_piece, offset)
        return query_sum + jnp.einsum(
            "qhk,khd->qhd", score_grad, key_piece, preferred_element_type=jnp.float32
        )

    query_sum = sweep(query_pass, zero_query, (keys_all, values_all), 0)
    own_keys = key_rows.reshape(own_rows, head_count, HD)
    own_values = value_rows.reshape(own_rows, head_count, HD)
    own_hot = block_hot(shard_index * own_rows, own_rows, all_blocks)
    slot_table = table.astype(jnp.bfloat16)
    logsum_all, delta_all = (
        lax.all_gather(log_norm, "tm", axis=0, tiled=True),
        lax.all_gather(deltas, "tm", axis=0, tiled=True),
    )

    def owner_work(running, pieces, offset):
        key_sum, value_sum = running
        query_piece, cotan_piece = pieces
        row_count = query_piece.shape[0]
        logsum_piece = lax.dynamic_slice_in_dim(logsum_all, offset, row_count, 0)
        delta_piece = lax.dynamic_slice_in_dim(delta_all, offset, row_count, 0)
        piece_table = jnp.dot(
            block_hot(offset, row_count, shards * slot_count),
            slot_table,
            preferred_element_type=jnp.float32,
        ).astype(jnp.bfloat16)
        allowed = (
            lax.dot_general(
                piece_table, own_hot, (((1,), (1,)), ((), ())), preferred_element_type=jnp.float32
            )[:, None, :]
            > 0.5
        )
        query_three = query_piece.reshape(row_count, head_count, HD)
        cotan_three = cotan_piece.reshape(row_count, head_count, HD)
        scores = (
            jnp.einsum("qhd,khd->qhk", query_three, own_keys, preferred_element_type=jnp.float32)
            * scaling
        )
        probs = jnp.where(
            allowed, jnp.exp(jnp.where(allowed, scores - logsum_piece[:, :, None], 0.0)), 0.0
        )
        weight_grad = jnp.einsum(
            "qhd,khd->qhk", cotan_three, own_values, preferred_element_type=jnp.float32
        )
        score_grad = (probs * (weight_grad - delta_piece[:, :, None])).astype(jnp.bfloat16)
        key_sum = key_sum + jnp.einsum(
            "qhk,qhd->khd", score_grad, query_three, preferred_element_type=jnp.float32
        )
        value_sum = value_sum + jnp.einsum(
            "qhk,qhd->khd",
            probs.astype(jnp.bfloat16),
            cotan_three,
            preferred_element_type=jnp.float32,
        )
        return (key_sum, value_sum)

    key_zero = jnp.zeros((own_rows, head_count, HD), jnp.float32)
    key_sum, value_sum = sweep(
        owner_work,
        (key_zero, key_zero),
        (
            lax.all_gather(query_slots.reshape(slot_rows, model_width), "tm", axis=0, tiled=True),
            lax.all_gather(cotan_slots.reshape(slot_rows, model_width), "tm", axis=0, tiled=True),
        ),
        jnp.int32(0),
    )
    key_grad = (key_sum * scaling).astype(jnp.bfloat16).reshape(own_rows, model_width)
    value_grad = value_sum.astype(jnp.bfloat16).reshape(own_rows, model_width)
    query_grad = (query_sum * scaling).astype(jnp.bfloat16).reshape(slot_rows, model_width)
    return (attended.reshape(slot_rows, model_width), query_grad, key_grad, value_grad)


def head_kernel(
    shards,
    rows,
    act_ref,
    cnt_ref,
    mask_ref,
    q_hbm,
    k_hbm,
    v_hbm,
    g_hbm,
    att_hbm,
    dq_hbm,
    dk_hbm,
    dv_hbm,
    held,
    scores,
    weights,
    grads,
    key_sum,
    value_sum,
    stage,
    stage_kv,
    in_send,
    in_recv,
    out_send,
    out_recv,
    kv_send,
    kv_recv,
    in_local,
    out_local,
    kv_local,
    relay_in,
    relay_own,
    relay_on,
    relay_recv,
    on_send,
    on_recv,
    relay_local,
):
    me = lax.axis_index("tm")
    half = me // 2
    up = lax.rem(me, 2)
    near = 2 - half
    neighbour = me + 1 - 2 * up
    is_near = me == 1 + half
    total = shards * rows
    blocks = total // BLK
    scaling = 1.0 / math.sqrt(HD)
    sources = (k_hbm, v_hbm, q_hbm, g_hbm)
    outs = (att_hbm, dq_hbm)
    kv_outs = (dk_hbm, dv_hbm)

    def columns(index):
        return pl.ds(pl.multiple_of(index * HD, HD), HD)

    def shard_rows(index):
        return pl.ds(pl.multiple_of(index * rows, rows), rows)

    def incoming(array, source, target):
        return pltpu.make_async_remote_copy(
            src_ref=sources[array].at[:, columns(target)],
            dst_ref=held.at[array, shard_rows(source), :],
            send_sem=in_send.at[array, target],
            recv_sem=in_recv.at[array, source],
            device_id={"tm": target},
            device_id_type=pl.DeviceIdType.MESH,
        )

    def own_incoming(array):
        return pltpu.make_async_copy(
            sources[array].at[:, columns(me)],
            held.at[array, shard_rows(me), :],
            in_local.at[array],
        )

    pieces = (
        (shards - 1, 0, (rows // BLK + 1) * BLK, BLK),
        (0, BLK, BLK, rows),
        (1, BLK + rows, 0, BLK),
    )

    def outgoing(array, piece, chunk, target, source):
        _, low, slot_low, size = pieces[piece]
        return pltpu.make_async_remote_copy(
            src_ref=stage.at[array, chunk, pl.ds(low, size), :],
            dst_ref=outs[array].at[pl.ds(slot_low, size), columns(source)],
            send_sem=out_send.at[array, piece, chunk],
            recv_sem=out_recv.at[array, piece, source],
            device_id={"tm": target},
            device_id_type=pl.DeviceIdType.MESH,
        )

    def own_outgoing(array, piece, chunk):
        _, low, slot_low, size = pieces[piece]
        return pltpu.make_async_copy(
            stage.at[array, chunk, pl.ds(low, size), :],
            outs[array].at[pl.ds(slot_low, size), columns(me)],
            out_local.at[array, piece],
        )

    def middle_half(array, chunk, source):
        low = pl.multiple_of(BLK + lax.rem(chunk, 2) * BLK, BLK)
        return pltpu.make_async_remote_copy(
            src_ref=stage.at[array, chunk, pl.ds(low, BLK), :],
            dst_ref=outs[array].at[pl.ds(low, BLK), columns(source)],
            send_sem=out_send.at[array, 1, chunk],
            recv_sem=out_recv.at[array, 1, source],
            device_id={"tm": chunk},
            device_id_type=pl.DeviceIdType.MESH,
        )

    def to_relay(array, odd, chunk, source_place):
        low = 0 if odd else BLK + rows
        return pltpu.make_async_remote_copy(
            src_ref=stage.at[array, chunk, pl.ds(low, BLK), :],
            dst_ref=relay_in.at[array, source_place, pl.ds(odd * BLK, BLK), :],
            send_sem=out_send.at[array, 0 if odd else 2, chunk],
            recv_sem=relay_recv.at[array, odd, source_place],
            device_id={"tm": near},
            device_id_type=pl.DeviceIdType.MESH,
        )

    def handed_on(array, place, slot_low):
        source = 2 * (1 - half) + place
        return pltpu.make_async_remote_copy(
            src_ref=relay_on.at[array, place],
            dst_ref=outs[array].at[
                pl.ds(pl.multiple_of(slot_low, 2 * BLK), 2 * BLK), columns(source)
            ],
            send_sem=on_send.at[array, place],
            recv_sem=on_recv.at[array, place],
            device_id={"tm": neighbour},
            device_id_type=pl.DeviceIdType.MESH,
        )

    def relay_kept(array, place):
        source = 2 * (1 - half) + place
        return pltpu.make_async_copy(
            relay_own.at[array, place],
            outs[array].at[
                pl.ds(pl.multiple_of((1 - up) * 2 * BLK, 2 * BLK), 2 * BLK), columns(source)
            ],
            relay_local.at[array, place],
        )

    def send_pieces(array, chunk):
        far = chunk // 2 != half
        odd = lax.rem(chunk, 2) == 1

        @pl.when(jnp.logical_not(far))
        def _():
            send_some(array, chunk, (0, 1, 2))

        @pl.when(far & jnp.logical_not(odd))
        def _():
            send_some(array, chunk, (0,))
            middle_half(array, chunk, me).start()
            to_relay(array, 0, chunk, up).start()

        @pl.when(far & odd)
        def _():
            send_some(array, chunk, (2,))
            middle_half(array, chunk, me).start()
            to_relay(array, 1, chunk, up).start()

    def send_some(array, chunk, which):
        for piece in which:
            target = lax.rem(chunk + pieces[piece][0], shards)

            @pl.when(target == me)
            def _():
                own_outgoing(array, piece, chunk).start()

            @pl.when(target != me)
            def _():
                outgoing(array, piece, chunk, target, me).start()

    def kv_outgoing(array, source, target):
        return pltpu.make_async_remote_copy(
            src_ref=stage_kv.at[array, shard_rows(target), :],
            dst_ref=kv_outs[array].at[:, columns(source)],
            send_sem=kv_send.at[array, target],
            recv_sem=kv_recv.at[array, source],
            device_id={"tm": target},
            device_id_type=pl.DeviceIdType.MESH,
        )

    def kv_own(array):
        return pltpu.make_async_copy(
            stage_kv.at[array, shard_rows(me), :],
            kv_outs[array].at[:, columns(me)],
            kv_local.at[array],
        )

    barrier = pltpu.get_barrier_semaphore()
    for step in range(1, shards):
        pl.semaphore_signal(
            barrier,
            inc=1,
            device_id={"tm": lax.rem(me + step, shards)},
            device_id_type=pl.DeviceIdType.MESH,
        )
    for array in range(4):
        own_incoming(array).start()
    pl.semaphore_wait(barrier, shards - 1)
    for array in range(4):
        for step in range(1, shards):
            incoming(array, me, lax.rem(me + step, shards)).start()

    key_sum[...] = jnp.zeros_like(key_sum)
    value_sum[...] = jnp.zeros_like(value_sum)
    for array in range(4):
        own_incoming(array).wait()
    for array in range(2):
        for step in range(1, shards):
            source = lax.rem(me + step, shards)
            incoming(array, source, me).wait_recv()

    lane_block = lax.broadcasted_iota(jnp.int32, (1, rows), 1) // BLK

    def one_chunk(turn, carry):
        pair = turn // 2
        side = (turn - 2 * pair) * (1 - 2 * lax.rem(me, 2))
        chunk = lax.rem(me + side + shards // 2 + 2 * pair + shards, shards)

        @pl.when(chunk != me)
        def _():
            incoming(2, chunk, me).wait_recv()
            incoming(3, chunk, me).wait_recv()

        own = shard_rows(chunk)
        query = held[2, own, :]
        cotan = held[3, own, :]
        peak = jnp.full((1, rows), very_low, jnp.float32)
        for b in range(blocks):
            part = pl.ds(b * BLK, BLK)
            bias = jnp.full((1, rows), very_low, jnp.float32)
            for j in range(rows // BLK):
                a = chunk * (rows // BLK) + j
                seen = act_ref[b] * act_ref[a] * mask_ref[a, b]
                level = jnp.where(seen > 0, 0.0, very_low)
                bias = jnp.where(lane_block == j, level, bias)
            tile = lax.dot_general(
                held[0, part, :], query, (((1,), (1,)), ((), ())), preferred_element_type=jnp.float32
            )
            tile = tile * scaling + bias
            scores[part, :] = tile
            peak = jnp.maximum(peak, jnp.max(tile, axis=0, keepdims=True))
        peak = jnp.maximum(peak, -1e20)
        mass = jnp.zeros((1, rows), jnp.float32)
        for b in range(blocks):
            part = pl.ds(b * BLK, BLK)
            tile = jnp.exp(scores[part, :] - peak)
            scores[part, :] = tile
            weights[part, :] = tile.astype(jnp.bfloat16)
            mass = mass + jnp.sum(tile, axis=0, keepdims=True)
        inverse = 1.0 / jnp.where(mass > 0.0, mass, 1.0)
        att_t = lax.dot_general(
            held[1], weights[...], (((0,), (0,)), ((), ())), preferred_element_type=jnp.float32
        )
        att_t = (att_t * inverse).astype(jnp.bfloat16).astype(jnp.float32)
        delta = jnp.sum(jnp.transpose(cotan.astype(jnp.float32)) * att_t, axis=0, keepdims=True)
        last = rows // BLK - 1
        to_left = cnt_ref[0, chunk] > 0
        to_right = cnt_ref[1, chunk] > 0

        far = chunk // 2 != half
        raw_first = to_left | (far & (lax.rem(chunk, 2) == 1))
        raw_final = to_right | (far & (lax.rem(chunk, 2) == 0))

        def stage_slots(array, result):
            result = result.astype(jnp.bfloat16)
            first, final = result[:BLK], result[last * BLK :]
            zero = jnp.zeros_like(first)
            stage[array, chunk, pl.ds(0, BLK), :] = jnp.where(raw_first, first, zero)
            stage[array, chunk, pl.ds(BLK, BLK), :] = jnp.where(to_left, zero, first)
            stage[array, chunk, pl.ds(rows, BLK), :] = jnp.where(to_right, zero, final)
            stage[array, chunk, pl.ds(rows + BLK, BLK), :] = jnp.where(raw_final, final, zero)

        stage_slots(0, jnp.transpose(att_t))
        send_pieces(0, chunk)
        for b in range(blocks):
            part = pl.ds(b * BLK, BLK)
            tile = lax.dot_general(
                held[1, part, :], cotan, (((1,), (1,)), ((), ())), preferred_element_type=jnp.float32
            )
            probs = scores[part, :] * inverse
            grad = (probs * (tile - delta)).astype(jnp.bfloat16)
            grads[part, :] = grad
            key_sum[part, :] += jnp.dot(grad, query, preferred_element_type=jnp.float32)
            value_sum[part, :] += jnp.dot(
                probs.astype(jnp.bfloat16), cotan, preferred_element_type=jnp.float32
            )
        dq_t = lax.dot_general(
            held[0], grads[...], (((0,), (0,)), ((), ())), preferred_element_type=jnp.float32
        )
        stage_slots(1, jnp.transpose(dq_t * scaling))
        send_pieces(1, chunk)
        return carry

    lax.fori_loop(0, shards, one_chunk, 0)
    @pl.when(is_near)
    def _():
        lower = me - up
        right = cnt_ref[1, lower]
        left = cnt_ref[0, lower + 1]
        for array in range(2):
            for place in range(2):
                to_relay(array, 0, lower, place).wait_recv()
                to_relay(array, 1, lower + 1, place).wait_recv()
                for b, keep in ((0, right == up), (1, left == 1 - up)):
                    part = pl.ds(b * BLK, BLK)
                    block = relay_in[array, place, part, :]
                    zero = jnp.zeros_like(block)
                    relay_own[array, place, part, :] = jnp.where(keep, block, zero)
                    relay_on[array, place, part, :] = jnp.where(keep, zero, block)
                handed_on(array, place, up * 2 * BLK).start()
                relay_kept(array, place).start()

    stage_kv[0] = (key_sum[...] * scaling).astype(jnp.bfloat16)
    stage_kv[1] = value_sum[...].astype(jnp.bfloat16)
    for array in range(2):
        for step in range(1, shards):
            kv_outgoing(array, me, lax.rem(me + step, shards)).start()
        kv_own(array).start()

    @pl.when(is_near)
    def _():
        for array in range(2):
            for place in range(2):
                handed_on(array, place, up * 2 * BLK).wait_send()
                relay_kept(array, place).wait()

    @pl.when(jnp.logical_not(is_near))
    def _():
        for array in range(2):
            for place in range(2):
                handed_on(array, place, (1 - up) * 2 * BLK).wait_recv()

    for step in range(1, shards):
        peer = lax.rem(me + step, shards)
        for array in range(4):
            incoming(array, me, peer).wait_send()
        for array in range(2):
            kv_outgoing(array, me, peer).wait_send()
            kv_outgoing(array, peer, me).wait_recv()

        @pl.when(peer // 2 == half)
        def _():
            for array in range(2):
                for piece in range(3):
                    outgoing(array, piece, 0, me, peer).wait_recv()
                outgoing(array, 1, peer, peer, me).wait_send()

        @pl.when(peer // 2 != half)
        def _():
            for array in range(2):
                middle_half(array, me, peer).wait_recv()
                middle_half(array, peer, me).wait_send()

            @pl.when(up == 0)
            def _():
                for array in range(2):
                    outgoing(array, 2, 0, me, peer).wait_recv()

            @pl.when(up == 1)
            def _():
                for array in range(2):
                    outgoing(array, 0, 0, me, peer).wait_recv()

    for step in range(shards):
        chunk = lax.rem(me + step, shards)
        for piece in (0, 2):
            if (step + pieces[piece][0]) % shards != 0:
                for array in range(2):
                    outgoing(array, piece, chunk, near, me).wait_send()
    for array in range(2):
        kv_own(array).wait()
        for piece in range(3):
            own_outgoing(array, piece, 0).wait()


def hand_out(*refs):
    count = 4
    sources, targets, held = refs[:count], refs[count : 2 * count], refs[2 * count : 3 * count]
    arrived, left = refs[3 * count :]
    inward = [pltpu.make_async_copy(sources[i], held[i], arrived.at[i]) for i in range(count)]
    outward = [pltpu.make_async_copy(held[i], targets[i], left.at[i]) for i in range(count)]
    for copy in inward:
        copy.start()
    for first, second in zip(inward, outward):
        first.wait()
        second.start()
    for copy in outward:
        copy.wait()


def exchanged_heads(queries, key_rows, value_rows, cotangent, block_active, send_counts, block_mask):
    shards = lax.axis_size("tm")
    rows, width = queries.shape
    total = shards * rows
    slot_rows = rows + 2 * CAP * BLK
    anywhere = pl.BlockSpec(memory_space=pl.ANY)
    scalars = pl.BlockSpec(memory_space=pltpu.SMEM)
    results = pl.pallas_call(
        functools.partial(head_kernel, shards, rows),
        out_shape=(
            jax.ShapeDtypeStruct((slot_rows, width), jnp.bfloat16),
            jax.ShapeDtypeStruct((slot_rows, width), jnp.bfloat16),
            jax.ShapeDtypeStruct((rows, width), jnp.bfloat16),
            jax.ShapeDtypeStruct((rows, width), jnp.bfloat16),
        ),
        in_specs=[scalars] * 3 + [pl.BlockSpec(memory_space=pltpu.HBM)] * 4,
        out_specs=(anywhere,) * 4,
        scratch_shapes=[
            pltpu.VMEM((4, total, HD), jnp.bfloat16),
            pltpu.VMEM((total, rows), jnp.float32),
            pltpu.VMEM((total, rows), jnp.bfloat16),
            pltpu.VMEM((total, rows), jnp.bfloat16),
            pltpu.VMEM((total, HD), jnp.float32),
            pltpu.VMEM((total, HD), jnp.float32),
            pltpu.VMEM((2, shards, slot_rows, HD), jnp.bfloat16),
            pltpu.VMEM((2, total, HD), jnp.bfloat16),
            pltpu.SemaphoreType.DMA((4, shards)),
            pltpu.SemaphoreType.DMA((4, shards)),
            pltpu.SemaphoreType.DMA((2, 3, shards)),
            pltpu.SemaphoreType.DMA((2, 3, shards)),
            pltpu.SemaphoreType.DMA((2, shards)),
            pltpu.SemaphoreType.DMA((2, shards)),
            pltpu.SemaphoreType.DMA((4,)),
            pltpu.SemaphoreType.DMA((2, 3)),
            pltpu.SemaphoreType.DMA((2,)),
            pltpu.VMEM((2, 2, 2 * BLK, HD), jnp.bfloat16),
            pltpu.VMEM((2, 2, 2 * BLK, HD), jnp.bfloat16),
            pltpu.VMEM((2, 2, 2 * BLK, HD), jnp.bfloat16),
            pltpu.SemaphoreType.DMA((2, 2, 2)),
            pltpu.SemaphoreType.DMA((2, 2)),
            pltpu.SemaphoreType.DMA((2, 2)),
            pltpu.SemaphoreType.DMA((2, 2)),
        ],
        compiler_params=pltpu.CompilerParams(
            collective_id=0, has_side_effects=True, vmem_limit_bytes=63 * 1024 * 1024
        ),
    )(block_active, send_counts.T, block_mask, queries, key_rows, value_rows, cotangent)
    return pl.pallas_call(
        hand_out,
        out_shape=tuple(jax.ShapeDtypeStruct(r.shape, r.dtype) for r in results),
        in_specs=[anywhere] * 4,
        out_specs=(anywhere,) * 4,
        scratch_shapes=[pltpu.VMEM(r.shape, r.dtype) for r in results]
        + [pltpu.SemaphoreType.DMA((4,)), pltpu.SemaphoreType.DMA((4,))],
    )(*results)


def routed(queries, key_rows, value_rows, cotangent, block_active, send_counts, block_mask):
    shards = lax.axis_size("tm")
    rows, width = queries.shape
    args = (queries, key_rows, value_rows, cotangent, block_active, send_counts, block_mask)
    if shards == 4 and width == shards * HD and rows == 2 * BLK:
        return exchanged_heads(*args)
    return body(*args)


def solution(mesh):
    in_specs = (
        P(("groups", "tm"), ("head", "mp")),
        P(("groups", "tm"), ("head", "mp")),
        P(("groups", "tm"), ("head", "mp")),
        P(("groups", "tm"), ("head", "mp")),
        P("groups"),
        P("groups", None),
        P("groups", None),
    )
    out_specs = (
        P(("groups", "tm"), ("head", "mp")),
        P(("groups", "tm"), ("head", "mp")),
        P(("groups", "tm"), ("head", "mp")),
        P(("groups", "tm"), ("head", "mp")),
    )
    return jax.shard_map(
        routed, mesh=mesh, in_specs=in_specs, out_specs=out_specs, check_vma=False)
```

```python
import functools
import math

import jax
import jax.numpy as jnp
from jax import lax
from jax.experimental import pallas as pl
from jax.experimental.pallas import tpu as pltpu
from jax.sharding import PartitionSpec as P

HD = 128
BLK = 128
CAP = 1


very_low = -1e30


def extended_2(shard, sides, width):
    for axis, dim in sides:
        peers, length = (lax.axis_size(axis), shard.shape[dim])
        up = [(i, (i + 1) % peers) for i in range(peers)]
        down = [(j, i) for i, j in up]
        last = lax.slice_in_dim(shard, length - width, length, axis=dim)
        first = lax.slice_in_dim(shard, 0, width, axis=dim)
        before = lax.ppermute(last, axis, up)
        after = lax.ppermute(first, axis, down)
        shard = jnp.concatenate([before, shard, after], axis=dim)
    return shard


def pick(table, positions, extent):
    matches = positions[:, None] == jnp.arange(extent, dtype=jnp.int32)[None, :]
    return jnp.sum(jnp.where(matches, table[None, :], 0), axis=1)


def slot_layout(block_active, send_counts, block_mask, shards, own_blocks, capacity):
    slot_count = own_blocks + 2 * capacity
    all_blocks = shards * own_blocks
    places = jnp.arange(shards * slot_count, dtype=jnp.int32)
    device = places // slot_count
    slot_index = places % slot_count
    before = (device + shards - 1) % shards
    following = (device + 1) % shards
    to_left = send_counts[:, 0]
    to_right = send_counts[:, 1]
    from_before = slot_index < capacity
    from_after = slot_index >= capacity + own_blocks
    owner_shard = jnp.where(from_before, before, jnp.where(from_after, following, device))
    local_block = jnp.where(
        from_before,
        own_blocks - capacity + slot_index,
        jnp.where(from_after, slot_index - capacity - own_blocks, slot_index - capacity),
    )
    middle_ok = (local_block >= pick(to_left, device, shards)) & (
        local_block < own_blocks - pick(to_right, device, shards)
    )
    holds_record = jnp.where(
        from_before,
        slot_index >= capacity - pick(to_right, before, shards),
        jnp.where(from_after, local_block < pick(to_left, following, shards), middle_ok),
    )
    anchor = owner_shard * own_blocks + local_block
    onehot = (anchor[:, None] == jnp.arange(all_blocks, dtype=jnp.int32)[None, :]).astype(
        jnp.float32
    )
    seeing = (block_mask * block_active[None, :]).astype(jnp.float32)
    block_rows = jnp.dot(onehot, seeing, precision=lax.Precision.HIGHEST)
    active = jnp.dot(onehot, block_active.astype(jnp.float32), precision=lax.Precision.HIGHEST)
    present = jnp.where(holds_record, active, 0.0)
    return (anchor, block_rows * present[:, None], present)


def block_hot(offset, length, extent):
    blocks = (offset + jnp.arange(length, dtype=jnp.int32)) // BLK
    return (blocks[:, None] == jnp.arange(extent, dtype=jnp.int32)[None, :]).astype(jnp.bfloat16)


def sweep(update, running, pieces, offset):
    row_count = pieces[0].shape[0]
    step_rows = math.gcd(row_count, 1024)
    if step_rows == row_count:
        return update(running, pieces, offset)

    def one_turn(turn_index, carried):
        part_pieces = tuple(
            (
                lax.dynamic_slice_in_dim(member, turn_index * step_rows, step_rows, 0)
                for member in pieces
            )
        )
        return update(carried, part_pieces, offset + turn_index * step_rows)

    return lax.fori_loop(0, row_count // step_rows, one_turn, running)


def body(queries, key_rows, value_rows, cotangent, block_active, send_counts, block_mask):
    shards = lax.axis_size("tm")
    shard_index = lax.axis_index("tm")
    model_width = queries.shape[1]
    head_count = model_width // HD
    own_rows = queries.shape[0]
    own_blocks = own_rows // BLK
    all_blocks = block_active.shape[0]
    slot_count = own_blocks + 2 * CAP
    slot_rows = slot_count * BLK
    scaling = 1.0 / math.sqrt(HD)
    anchor, table, present = slot_layout(
        block_active, send_counts, block_mask, shards, own_blocks, CAP
    )
    records = jnp.concatenate([queries, cotangent], axis=1)
    extended = extended_2(records, (("tm", 0),), CAP * BLK)
    query_slots = extended[:, :model_width].reshape(slot_rows, head_count, HD)
    cotan_slots = extended[:, model_width:].reshape(slot_rows, head_count, HD)
    my_table = lax.dynamic_slice_in_dim(table, shard_index * slot_count, slot_count, 0)
    query_table = jnp.repeat(my_table, BLK, axis=0).astype(jnp.bfloat16)
    live = (
        jnp.repeat(lax.dynamic_slice_in_dim(present, shard_index * slot_count, slot_count, 0), BLK)
        > 0.5
    )
    keys_all, values_all = (
        lax.all_gather(key_rows, "tm", axis=0, tiled=True),
        lax.all_gather(value_rows, "tm", axis=0, tiled=True),
    )

    def own_scores(key_piece, offset):
        allowed = (
            lax.dot_general(
                query_table,
                block_hot(offset, key_piece.shape[0], all_blocks),
                (((1,), (1,)), ((), ())),
                preferred_element_type=jnp.float32,
            )[:, None, :]
            > 0.5
        )
        scores = (
            jnp.einsum("qhd,khd->qhk", query_slots, key_piece, preferred_element_type=jnp.float32)
            * scaling
        )
        return (allowed, scores)

    def forward(running, pieces, offset):
        peak, masses, accum = running
        key_piece = pieces[0].reshape(-1, head_count, HD)
        value_piece = pieces[1].reshape(-1, head_count, HD)
        allowed, scores = own_scores(key_piece, offset)
        new_peak = jnp.maximum(peak, jnp.max(jnp.where(allowed, scores, very_low), axis=2))
        weights = jnp.where(
            allowed, jnp.exp(jnp.where(allowed, scores - new_peak[:, :, None], 0.0)), 0.0
        )
        shrink = jnp.exp(peak - new_peak)
        masses = masses * shrink + jnp.sum(weights, axis=2)
        accum = accum * shrink[:, :, None] + jnp.einsum(
            "qhk,khd->qhd",
            weights.astype(jnp.bfloat16),
            value_piece,
            preferred_element_type=jnp.float32,
        )
        return (new_peak, masses, accum)

    initial = (
        jnp.full((slot_rows, head_count), very_low, jnp.float32),
        jnp.zeros((slot_rows, head_count), jnp.float32),
        jnp.zeros((slot_rows, head_count, HD), jnp.float32),
    )
    peak, masses, accum = sweep(forward, initial, (keys_all, values_all), 0)
    denominator = jnp.where(live[:, None], masses, 1.0)
    attended = (accum / denominator[:, :, None]).astype(jnp.bfloat16)
    log_norm = peak + jnp.log(denominator)
    deltas = jnp.sum(cotan_slots.astype(jnp.float32) * attended.astype(jnp.float32), axis=2)

    def own_gradients(key_piece, value_piece, offset):
        allowed, scores = own_scores(key_piece, offset)
        probs = jnp.where(
            allowed, jnp.exp(jnp.where(allowed, scores - log_norm[:, :, None], 0.0)), 0.0
        )
        weight_grad = jnp.einsum(
            "qhd,khd->qhk", cotan_slots, value_piece, preferred_element_type=jnp.float32
        )
        return (probs, (probs * (weight_grad - deltas[:, :, None])).astype(jnp.bfloat16))

    zero_query = jnp.zeros((slot_rows, head_count, HD), jnp.float32)

    def query_pass(query_sum, pieces, offset):
        key_piece = pieces[0].reshape(-1, head_count, HD)
        value_piece = pieces[1].reshape(-1, head_count, HD)
        probs, score_grad = own_gradients(key_piece, value_piece, offset)
        return query_sum + jnp.einsum(
            "qhk,khd->qhd", score_grad, key_piece, preferred_element_type=jnp.float32
        )

    query_sum = sweep(query_pass, zero_query, (keys_all, values_all), 0)
    own_keys = key_rows.reshape(own_rows, head_count, HD)
    own_values = value_rows.reshape(own_rows, head_count, HD)
    own_hot = block_hot(shard_index * own_rows, own_rows, all_blocks)
    slot_table = table.astype(jnp.bfloat16)
    logsum_all, delta_all = (
        lax.all_gather(log_norm, "tm", axis=0, tiled=True),
        lax.all_gather(deltas, "tm", axis=0, tiled=True),
    )

    def owner_work(running, pieces, offset):
        key_sum, value_sum = running
        query_piece, cotan_piece = pieces
        row_count = query_piece.shape[0]
        logsum_piece = lax.dynamic_slice_in_dim(logsum_all, offset, row_count, 0)
        delta_piece = lax.dynamic_slice_in_dim(delta_all, offset, row_count, 0)
        piece_table = jnp.dot(
            block_hot(offset, row_count, shards * slot_count),
            slot_table,
            preferred_element_type=jnp.float32,
        ).astype(jnp.bfloat16)
        allowed = (
            lax.dot_general(
                piece_table, own_hot, (((1,), (1,)), ((), ())), preferred_element_type=jnp.float32
            )[:, None, :]
            > 0.5
        )
        query_three = query_piece.reshape(row_count, head_count, HD)
        cotan_three = cotan_piece.reshape(row_count, head_count, HD)
        scores = (
            jnp.einsum("qhd,khd->qhk", query_three, own_keys, preferred_element_type=jnp.float32)
            * scaling
        )
        probs = jnp.where(
            allowed, jnp.exp(jnp.where(allowed, scores - logsum_piece[:, :, None], 0.0)), 0.0
        )
        weight_grad = jnp.einsum(
            "qhd,khd->qhk", cotan_three, own_values, preferred_element_type=jnp.float32
        )
        score_grad = (probs * (weight_grad - delta_piece[:, :, None])).astype(jnp.bfloat16)
        key_sum = key_sum + jnp.einsum(
            "qhk,qhd->khd", score_grad, query_three, preferred_element_type=jnp.float32
        )
        value_sum = value_sum + jnp.einsum(
            "qhk,qhd->khd",
            probs.astype(jnp.bfloat16),
            cotan_three,
            preferred_element_type=jnp.float32,
        )
        return (key_sum, value_sum)

    key_zero = jnp.zeros((own_rows, head_count, HD), jnp.float32)
    key_sum, value_sum = sweep(
        owner_work,
        (key_zero, key_zero),
        (
            lax.all_gather(query_slots.reshape(slot_rows, model_width), "tm", axis=0, tiled=True),
            lax.all_gather(cotan_slots.reshape(slot_rows, model_width), "tm", axis=0, tiled=True),
        ),
        jnp.int32(0),
    )
    key_grad = (key_sum * scaling).astype(jnp.bfloat16).reshape(own_rows, model_width)
    value_grad = value_sum.astype(jnp.bfloat16).reshape(own_rows, model_width)
    query_grad = (query_sum * scaling).astype(jnp.bfloat16).reshape(slot_rows, model_width)
    return (attended.reshape(slot_rows, model_width), query_grad, key_grad, value_grad)


def head_kernel(
    shards,
    rows,
    act_ref,
    cnt_ref,
    mask_ref,
    q_hbm,
    k_hbm,
    v_hbm,
    g_hbm,
    att_hbm,
    dq_hbm,
    dk_hbm,
    dv_hbm,
    held,
    scores,
    weights,
    grads,
    key_sum,
    value_sum,
    stage,
    stage_kv,
    in_send,
    in_recv,
    out_send,
    out_recv,
    kv_send,
    kv_recv,
    in_local,
    out_local,
    kv_local,
    relay_in,
    relay_own,
    relay_on,
    relay_recv,
    on_send,
    on_recv,
    relay_local,
):
    me = lax.axis_index("tm")
    half = me // 2
    up = lax.rem(me, 2)
    near = 2 - half
    neighbour = me + 1 - 2 * up
    is_near = me == 1 + half
    total = shards * rows
    blocks = total // BLK
    scaling = 1.0 / math.sqrt(HD)
    sources = (k_hbm, v_hbm, q_hbm, g_hbm)
    outs = (att_hbm, dq_hbm)
    kv_outs = (dk_hbm, dv_hbm)

    def columns(index):
        return pl.ds(pl.multiple_of(index * HD, HD), HD)

    def shard_rows(index):
        return pl.ds(pl.multiple_of(index * rows, rows), rows)

    def incoming(array, source, target):
        return pltpu.make_async_remote_copy(
            src_ref=sources[array].at[:, columns(target)],
            dst_ref=held.at[array, shard_rows(source), :],
            send_sem=in_send.at[array, target],
            recv_sem=in_recv.at[array, source],
            device_id={"tm": target},
            device_id_type=pl.DeviceIdType.MESH,
        )

    def own_incoming(array):
        return pltpu.make_async_copy(
            sources[array].at[:, columns(me)],
            held.at[array, shard_rows(me), :],
            in_local.at[array],
        )

    pieces = (
        (shards - 1, 0, (rows // BLK + 1) * BLK, BLK),
        (0, BLK, BLK, rows),
        (1, BLK + rows, 0, BLK),
    )

    def outgoing(array, piece, chunk, target, source):
        _, low, slot_low, size = pieces[piece]
        return pltpu.make_async_remote_copy(
            src_ref=stage.at[array, chunk, pl.ds(low, size), :],
            dst_ref=outs[array].at[pl.ds(slot_low, size), columns(source)],
            send_sem=out_send.at[array, piece, chunk],
            recv_sem=out_recv.at[array, piece, source],
            device_id={"tm": target},
            device_id_type=pl.DeviceIdType.MESH,
        )

    def own_outgoing(array, piece, chunk):
        _, low, slot_low, size = pieces[piece]
        return pltpu.make_async_copy(
            stage.at[array, chunk, pl.ds(low, size), :],
            outs[array].at[pl.ds(slot_low, size), columns(me)],
            out_local.at[array, piece],
        )

    def middle_half(array, chunk, source):
        low = pl.multiple_of(BLK + lax.rem(chunk, 2) * BLK, BLK)
        return pltpu.make_async_remote_copy(
            src_ref=stage.at[array, chunk, pl.ds(low, BLK), :],
            dst_ref=outs[array].at[pl.ds(low, BLK), columns(source)],
            send_sem=out_send.at[array, 1, chunk],
            recv_sem=out_recv.at[array, 1, source],
            device_id={"tm": chunk},
            device_id_type=pl.DeviceIdType.MESH,
        )

    def to_relay(array, odd, chunk, source_place):
        low = 0 if odd else BLK + rows
        return pltpu.make_async_remote_copy(
            src_ref=stage.at[array, chunk, pl.ds(low, BLK), :],
            dst_ref=relay_in.at[array, source_place, pl.ds(odd * BLK, BLK), :],
            send_sem=out_send.at[array, 0 if odd else 2, chunk],
            recv_sem=relay_recv.at[array, odd, source_place],
            device_id={"tm": near},
            device_id_type=pl.DeviceIdType.MESH,
        )

    def handed_on(array, place, slot_low):
        source = 2 * (1 - half) + place
        return pltpu.make_async_remote_copy(
            src_ref=relay_on.at[array, place],
            dst_ref=outs[array].at[
                pl.ds(pl.multiple_of(slot_low, 2 * BLK), 2 * BLK), columns(source)
            ],
            send_sem=on_send.at[array, place],
            recv_sem=on_recv.at[array, place],
            device_id={"tm": neighbour},
            device_id_type=pl.DeviceIdType.MESH,
        )

    def relay_kept(array, place):
        source = 2 * (1 - half) + place
        return pltpu.make_async_copy(
            relay_own.at[array, place],
            outs[array].at[
                pl.ds(pl.multiple_of((1 - up) * 2 * BLK, 2 * BLK), 2 * BLK), columns(source)
            ],
            relay_local.at[array, place],
        )

    def send_pieces(array, chunk):
        far = chunk // 2 != half
        odd = lax.rem(chunk, 2) == 1

        @pl.when(jnp.logical_not(far))
        def _():
            send_some(array, chunk, (0, 1, 2))

        @pl.when(far & jnp.logical_not(odd))
        def _():
            send_some(array, chunk, (0,))
            middle_half(array, chunk, me).start()
            to_relay(array, 0, chunk, up).start()

        @pl.when(far & odd)
        def _():
            send_some(array, chunk, (2,))
            middle_half(array, chunk, me).start()
            to_relay(array, 1, chunk, up).start()

    def send_some(array, chunk, which):
        for piece in which:
            target = lax.rem(chunk + pieces[piece][0], shards)

            @pl.when(target == me)
            def _():
                own_outgoing(array, piece, chunk).start()

            @pl.when(target != me)
            def _():
                outgoing(array, piece, chunk, target, me).start()

    def kv_outgoing(array, source, target):
        return pltpu.make_async_remote_copy(
            src_ref=stage_kv.at[array, shard_rows(target), :],
            dst_ref=kv_outs[array].at[:, columns(source)],
            send_sem=kv_send.at[array, target],
            recv_sem=kv_recv.at[array, source],
            device_id={"tm": target},
            device_id_type=pl.DeviceIdType.MESH,
        )

    def kv_own(array):
        return pltpu.make_async_copy(
            stage_kv.at[array, shard_rows(me), :],
            kv_outs[array].at[:, columns(me)],
            kv_local.at[array],
        )

    barrier = pltpu.get_barrier_semaphore()
    for step in range(1, shards):
        pl.semaphore_signal(
            barrier,
            inc=1,
            device_id={"tm": lax.rem(me + step, shards)},
            device_id_type=pl.DeviceIdType.MESH,
        )
    for array in range(4):
        own_incoming(array).start()
    pl.semaphore_wait(barrier, shards - 1)
    for array in range(4):
        for step in range(1, shards):
            incoming(array, me, lax.rem(me + step, shards)).start()

    key_sum[...] = jnp.zeros_like(key_sum)
    value_sum[...] = jnp.zeros_like(value_sum)
    for array in range(4):
        own_incoming(array).wait()
    for array in range(2):
        for step in range(1, shards):
            source = lax.rem(me + step, shards)
            incoming(array, source, me).wait_recv()

    lane_block = lax.broadcasted_iota(jnp.int32, (1, rows), 1) // BLK

    def one_chunk(turn, carry):
        pair = turn // 2
        side = (turn - 2 * pair) * (1 - 2 * lax.rem(me, 2))
        chunk = lax.rem(me + side + shards // 2 + 2 * pair + shards, shards)

        @pl.when(chunk != me)
        def _():
            incoming(2, chunk, me).wait_recv()
            incoming(3, chunk, me).wait_recv()

        own = shard_rows(chunk)
        query = held[2, own, :]
        cotan = held[3, own, :]
        peak = jnp.full((1, rows), very_low, jnp.float32)
        for b in range(blocks):
            part = pl.ds(b * BLK, BLK)
            bias = jnp.full((1, rows), very_low, jnp.float32)
            for j in range(rows // BLK):
                a = chunk * (rows // BLK) + j
                seen = act_ref[b] * act_ref[a] * mask_ref[a, b]
                level = jnp.where(seen > 0, 0.0, very_low)
                bias = jnp.where(lane_block == j, level, bias)
            tile = lax.dot_general(
                held[0, part, :], query, (((1,), (1,)), ((), ())), preferred_element_type=jnp.float32
            )
            tile = tile * scaling + bias
            scores[part, :] = tile
            peak = jnp.maximum(peak, jnp.max(tile, axis=0, keepdims=True))
        peak = jnp.maximum(peak, -1e20)
        mass = jnp.zeros((1, rows), jnp.float32)
        for b in range(blocks):
            part = pl.ds(b * BLK, BLK)
            tile = jnp.exp(scores[part, :] - peak)
            scores[part, :] = tile
            weights[part, :] = tile.astype(jnp.bfloat16)
            mass = mass + jnp.sum(tile, axis=0, keepdims=True)
        inverse = 1.0 / jnp.where(mass > 0.0, mass, 1.0)
        att_t = lax.dot_general(
            held[1], weights[...], (((0,), (0,)), ((), ())), preferred_element_type=jnp.float32
        )
        att_t = (att_t * inverse).astype(jnp.bfloat16).astype(jnp.float32)
        delta = jnp.sum(jnp.transpose(cotan.astype(jnp.float32)) * att_t, axis=0, keepdims=True)
        last = rows // BLK - 1
        to_left = cnt_ref[0, chunk] > 0
        to_right = cnt_ref[1, chunk] > 0

        far = chunk // 2 != half
        raw_first = to_left | (far & (lax.rem(chunk, 2) == 1))
        raw_final = to_right | (far & (lax.rem(chunk, 2) == 0))

        def stage_slots(array, result):
            result = result.astype(jnp.bfloat16)
            first, final = result[:BLK], result[last * BLK :]
            zero = jnp.zeros_like(first)
            stage[array, chunk, pl.ds(0, BLK), :] = jnp.where(raw_first, first, zero)
            stage[array, chunk, pl.ds(BLK, BLK), :] = jnp.where(to_left, zero, first)
            stage[array, chunk, pl.ds(rows, BLK), :] = jnp.where(to_right, zero, final)
            stage[array, chunk, pl.ds(rows + BLK, BLK), :] = jnp.where(raw_final, final, zero)

        stage_slots(0, jnp.transpose(att_t))
        send_pieces(0, chunk)
        for b in range(blocks):
            part = pl.ds(b * BLK, BLK)
            tile = lax.dot_general(
                held[1, part, :], cotan, (((1,), (1,)), ((), ())), preferred_element_type=jnp.float32
            )
            probs = scores[part, :] * inverse
            grad = (probs * (tile - delta)).astype(jnp.bfloat16)
            grads[part, :] = grad
            key_sum[part, :] += jnp.dot(grad, query, preferred_element_type=jnp.float32)
            value_sum[part, :] += jnp.dot(
                probs.astype(jnp.bfloat16), cotan, preferred_element_type=jnp.float32
            )
        dq_t = lax.dot_general(
            held[0], grads[...], (((0,), (0,)), ((), ())), preferred_element_type=jnp.float32
        )
        stage_slots(1, jnp.transpose(dq_t * scaling))
        send_pieces(1, chunk)
        return carry

    lax.fori_loop(0, shards, one_chunk, 0)
    @pl.when(is_near)
    def _():
        lower = me - up
        right = cnt_ref[1, lower]
        left = cnt_ref[0, lower + 1]
        for array in range(2):
            for place in range(2):
                to_relay(array, 0, lower, place).wait_recv()
                to_relay(array, 1, lower + 1, place).wait_recv()
                for b, keep in ((0, right == up), (1, left == 1 - up)):
                    part = pl.ds(b * BLK, BLK)
                    block = relay_in[array, place, part, :]
                    zero = jnp.zeros_like(block)
                    relay_own[array, place, part, :] = jnp.where(keep, block, zero)
                    relay_on[array, place, part, :] = jnp.where(keep, zero, block)
                handed_on(array, place, up * 2 * BLK).start()
                relay_kept(array, place).start()

    for array, total_sum, factor in ((0, key_sum, scaling), (1, value_sum, 1.0)):
        stage_kv[array] = (total_sum[...] * factor).astype(jnp.bfloat16)
        for step in (2, 1, 3):
            kv_outgoing(array, me, lax.rem(me + step, shards)).start()
        kv_own(array).start()

    @pl.when(is_near)
    def _():
        for array in range(2):
            for place in range(2):
                handed_on(array, place, up * 2 * BLK).wait_send()
                relay_kept(array, place).wait()

    @pl.when(jnp.logical_not(is_near))
    def _():
        for array in range(2):
            for place in range(2):
                handed_on(array, place, (1 - up) * 2 * BLK).wait_recv()

    for step in range(1, shards):
        peer = lax.rem(me + step, shards)
        for array in range(4):
            incoming(array, me, peer).wait_send()
        for array in range(2):
            kv_outgoing(array, me, peer).wait_send()
            kv_outgoing(array, peer, me).wait_recv()

        @pl.when(peer // 2 == half)
        def _():
            for array in range(2):
                for piece in range(3):
                    outgoing(array, piece, 0, me, peer).wait_recv()
                outgoing(array, 1, peer, peer, me).wait_send()

        @pl.when(peer // 2 != half)
        def _():
            for array in range(2):
                middle_half(array, me, peer).wait_recv()
                middle_half(array, peer, me).wait_send()

            @pl.when(up == 0)
            def _():
                for array in range(2):
                    outgoing(array, 2, 0, me, peer).wait_recv()

            @pl.when(up == 1)
            def _():
                for array in range(2):
                    outgoing(array, 0, 0, me, peer).wait_recv()

    for step in range(shards):
        chunk = lax.rem(me + step, shards)
        for piece in (0, 2):
            if (step + pieces[piece][0]) % shards != 0:
                for array in range(2):
                    outgoing(array, piece, chunk, near, me).wait_send()
    for array in range(2):
        kv_own(array).wait()
        for piece in range(3):
            own_outgoing(array, piece, 0).wait()


def hand_out(*refs):
    count = 4
    sources, targets, held = refs[:count], refs[count : 2 * count], refs[2 * count : 3 * count]
    arrived, left = refs[3 * count :]
    inward = [pltpu.make_async_copy(sources[i], held[i], arrived.at[i]) for i in range(count)]
    outward = [pltpu.make_async_copy(held[i], targets[i], left.at[i]) for i in range(count)]
    for copy in inward:
        copy.start()
    for first, second in zip(inward, outward):
        first.wait()
        second.start()
    for copy in outward:
        copy.wait()


def exchanged_heads(queries, key_rows, value_rows, cotangent, block_active, send_counts, block_mask):
    shards = lax.axis_size("tm")
    rows, width = queries.shape
    total = shards * rows
    slot_rows = rows + 2 * CAP * BLK
    anywhere = pl.BlockSpec(memory_space=pl.ANY)
    scalars = pl.BlockSpec(memory_space=pltpu.SMEM)
    results = pl.pallas_call(
        functools.partial(head_kernel, shards, rows),
        out_shape=(
            jax.ShapeDtypeStruct((slot_rows, width), jnp.bfloat16),
            jax.ShapeDtypeStruct((slot_rows, width), jnp.bfloat16),
            jax.ShapeDtypeStruct((rows, width), jnp.bfloat16),
            jax.ShapeDtypeStruct((rows, width), jnp.bfloat16),
        ),
        in_specs=[scalars] * 3 + [pl.BlockSpec(memory_space=pltpu.HBM)] * 4,
        out_specs=(anywhere,) * 4,
        scratch_shapes=[
            pltpu.VMEM((4, total, HD), jnp.bfloat16),
            pltpu.VMEM((total, rows), jnp.float32),
            pltpu.VMEM((total, rows), jnp.bfloat16),
            pltpu.VMEM((total, rows), jnp.bfloat16),
            pltpu.VMEM((total, HD), jnp.float32),
            pltpu.VMEM((total, HD), jnp.float32),
            pltpu.VMEM((2, shards, slot_rows, HD), jnp.bfloat16),
            pltpu.VMEM((2, total, HD), jnp.bfloat16),
            pltpu.SemaphoreType.DMA((4, shards)),
            pltpu.SemaphoreType.DMA((4, shards)),
            pltpu.SemaphoreType.DMA((2, 3, shards)),
            pltpu.SemaphoreType.DMA((2, 3, shards)),
            pltpu.SemaphoreType.DMA((2, shards)),
            pltpu.SemaphoreType.DMA((2, shards)),
            pltpu.SemaphoreType.DMA((4,)),
            pltpu.SemaphoreType.DMA((2, 3)),
            pltpu.SemaphoreType.DMA((2,)),
            pltpu.VMEM((2, 2, 2 * BLK, HD), jnp.bfloat16),
            pltpu.VMEM((2, 2, 2 * BLK, HD), jnp.bfloat16),
            pltpu.VMEM((2, 2, 2 * BLK, HD), jnp.bfloat16),
            pltpu.SemaphoreType.DMA((2, 2, 2)),
            pltpu.SemaphoreType.DMA((2, 2)),
            pltpu.SemaphoreType.DMA((2, 2)),
            pltpu.SemaphoreType.DMA((2, 2)),
        ],
        compiler_params=pltpu.CompilerParams(
            collective_id=0, has_side_effects=True, vmem_limit_bytes=63 * 1024 * 1024
        ),
    )(block_active, send_counts.T, block_mask, queries, key_rows, value_rows, cotangent)
    return pl.pallas_call(
        hand_out,
        out_shape=tuple(jax.ShapeDtypeStruct(r.shape, r.dtype) for r in results),
        in_specs=[anywhere] * 4,
        out_specs=(anywhere,) * 4,
        scratch_shapes=[pltpu.VMEM(r.shape, r.dtype) for r in results]
        + [pltpu.SemaphoreType.DMA((4,)), pltpu.SemaphoreType.DMA((4,))],
    )(*results)


def routed(queries, key_rows, value_rows, cotangent, block_active, send_counts, block_mask):
    shards = lax.axis_size("tm")
    rows, width = queries.shape
    args = (queries, key_rows, value_rows, cotangent, block_active, send_counts, block_mask)
    if shards == 4 and width == shards * HD and rows == 2 * BLK:
        return exchanged_heads(*args)
    return body(*args)


def solution(mesh):
    in_specs = (
        P(("groups", "tm"), ("head", "mp")),
        P(("groups", "tm"), ("head", "mp")),
        P(("groups", "tm"), ("head", "mp")),
        P(("groups", "tm"), ("head", "mp")),
        P("groups"),
        P("groups", None),
        P("groups", None),
    )
    out_specs = (
        P(("groups", "tm"), ("head", "mp")),
        P(("groups", "tm"), ("head", "mp")),
        P(("groups", "tm"), ("head", "mp")),
        P(("groups", "tm"), ("head", "mp")),
    )
    return jax.shard_map(
        routed, mesh=mesh, in_specs=in_specs, out_specs=out_specs, check_vma=False)
```
